512 devices in a mesh: freq: 8 (over y), tile: 64 (over z, x, core).
Axes of the slice: x: 4, y: 8, z: 8, core: 2. Of those that a mesh axis runs over, the one named last changes fastest.
Arguments:
- source: float32 [6, 256, 16, 128], P(None, 'tile'), may hold values from -6 to 6
- conductivity: float32 [256, 16, 128], P('tile'), may hold values from 0.3 to 3.3
- freq_factor: float32 [8], P('freq'), may hold values from 0.5 to 8
- observed: float32 [8, 6, 32768], P('freq', None, 'tile'), may hold values from -6 to 6
- slot_cells: int32 [32768], P('tile'), may hold values from 0 to 8191
- block_counts: int32 [4096], P('tile'), may hold values from 0 to 8, as said below
Outputs:
- field: float32 [8, 6, 256, 16, 128], P('freq', None, 'tile')
- gradient: float32 [256, 16, 128], P('tile')
The draws below stay inside these ranges and needn't reach their ends.
Inputs may be any that keep to these rules, and one draw needn't show every extreme that they name: block_counts[s * 64 + d] is the number of live slots in the block that tile s holds for tile d; in every draw some tile receives 8 live records from every tile.
All inputs are finite; a program needn't handle non-finite values.
Results may differ from the reference program's by a relative error of at most 0.0001.
Values sent between devices are 32-bit elements; how exact they have to be, the bound alone decides.
No kernel may reach another device: no remote copies, remote signals or barrier semaphores. Data moves between devices by JAX's collectives and lax.ppermute only.
A program may use at most 64 MiB of HBM per device.

```python
import math
import jax
import jax.numpy as jnp

CX = 4
NY = 16
NZ = 128
CAP = 8
SWEEPS = 4
NX = 256
FREQS = 8
RECS = 32768
N_TILE = 64


def draw_block_counts(key, part):
    key = jax.random.fold_in(key, 5)
    key_heavy, key_raw, key_full = jax.random.split(key, 3)
    heavy = jax.random.randint(key_heavy, (N_TILE,), 0, 4)
    limit = CAP * (heavy + 1) // 4
    raw = jax.random.randint(key_raw, (N_TILE, N_TILE), 0, 1 << 20) % (limit[None, :] + 1)
    full = jax.random.randint(key_full, (), 0, N_TILE)
    column = jnp.arange(N_TILE, dtype=jnp.int32)[None, :]
    counts = jnp.where(column == full, CAP, raw)
    return counts.reshape(-1).astype(jnp.int32)


def plant(drawn, rng, low, largest):
    spot = [jax.random.randint(jax.random.fold_in(rng, axis), (), 0, length) for axis, length in enumerate(drawn.shape)]
    longest = drawn.shape.index(max(drawn.shape))
    beside = spot[:longest] + [(spot[longest] + 1) % drawn.shape[longest]] + spot[longest + 1:]
    return drawn.at[tuple(spot)].set(low).at[tuple(beside)].set(largest)


def steps_of(own_key, dims, cuts, low, high):
    def one(position, shards_of):
        steps = jax.random.uniform(jax.random.fold_in(jax.random.fold_in(own_key, 6), position), (shards_of,), jnp.float32, low / len(cuts), high / len(cuts))
        return jnp.repeat(jnp.exp(steps), dims[position] // shards_of).reshape((-1,) + (1,) * (len(dims) - position - 1))

    level = one(*cuts[0])
    for cut in cuts[1:]:
        level = level * one(*cut)
    return level


def gaussian(rng, extent, spread, reach, pieces=(), kind=jnp.bfloat16):
    loudness = steps_of(rng, extent, pieces, -0.22, 0.18) if pieces else 1.0
    array = jax.random.normal(rng, extent, jnp.float32) * spread * loudness
    return jnp.minimum(jnp.maximum(array, -reach), reach).astype(kind)


def setup_inputs(seed: int = 0) -> dict:
    arg_keys = jax.random.split(jax.random.key(seed), 7)
    return {
        "source": gaussian(arg_keys[0], (6, NX, NY, NZ), 1.0, 6.0, ((1, 64),), jnp.float32),
        "conductivity": jnp.clip(jnp.exp(math.log(3.3) - 2.39789522 * jax.random.uniform(arg_keys[1], (NX, NY, NZ), jnp.float32) ** steps_of(arg_keys[1], (NX, NY, NZ), ((0, 64),), -0.2, 0.2)), 0.3, 3.3),
        "freq_factor": jnp.clip(jnp.exp(math.log(8.0) - 2.7725887 * jax.random.uniform(arg_keys[2], (FREQS,), jnp.float32) ** steps_of(arg_keys[2], (FREQS,), ((0, 8),), -0.2, 0.2)), 0.5, 8.0),
        "observed": gaussian(arg_keys[3], (FREQS, 6, RECS), 1.0, 6.0, ((0, 8), (2, 64)), jnp.float32),
        "slot_cells": plant(jax.random.randint(arg_keys[4], (RECS,), 0, CX * NY * NZ), jax.random.fold_in(arg_keys[4], 1), 0, (CX * NY * NZ) - 1).astype(jnp.int32),
        "block_counts": draw_block_counts(jax.random.fold_in(arg_keys[6], 71), 0),
    }


DAMPING = 0.8


def relax(field, conductance, source, factor):
    middle = field[:, 1:-1]
    beside = field[:, 2:] + field[:, :-2]
    padded_y = jnp.pad(middle, ((0, 0), (0, 0), (1, 1), (0, 0)))
    beside = beside + padded_y[:, :, 2:] + padded_y[:, :, :-2]
    padded_z = jnp.pad(middle, ((0, 0), (0, 0), (0, 0), (1, 1)))
    beside = beside + padded_z[:, :, :, 2:] + padded_z[:, :, :, :-2]
    laplace_term = 6.0 * middle - beside
    absorb = factor * conductance
    applied_re = laplace_term[:3] - absorb * middle[3:]
    applied_im = laplace_term[3:] + absorb * middle[:3]
    resid_re = source[:3] - applied_re
    resid_im = source[3:] - applied_im
    divisor = 36.0 + absorb * absorb
    delta_re = DAMPING * (6.0 * resid_re + absorb * resid_im) / divisor
    delta_im = DAMPING * (6.0 * resid_im - absorb * resid_re) / divisor
    return middle + jnp.concatenate([delta_re, delta_im], 0)


def solve(source, conductivity, factor):
    field = jnp.zeros_like(source)
    for sweep_index in range(SWEEPS):
        padded = jnp.pad(field, ((0, 0), (1, 1), (0, 0), (0, 0)))
        field = relax(padded, conductivity, source, factor)
    return field


def reference(source, conductivity, freq_factor, observed, slot_cells, block_counts):
    tile_cells = CX * NY * NZ
    slot = jnp.arange(RECS, dtype=jnp.int32)
    block = slot // CAP
    target = block % N_TILE
    within = slot % CAP
    live = (within < block_counts[block]).astype(jnp.float32)
    global_cell = (target * tile_cells + slot_cells).astype(jnp.int32)
    fields = []
    gradient = jnp.zeros((NX, NY, NZ), jnp.float32)
    for index in range(FREQS):
        factor = freq_factor[index]
        field = solve(source, conductivity, factor)
        fields.append(field)
        flat = field.reshape(6, -1)
        misfit = (flat[:, global_cell] - observed[index]) * live[None, :]
        adjoint_source = jnp.zeros((6, NX * NY * NZ), jnp.float32).at[:, global_cell].add(misfit)
        adjoint = solve(adjoint_source.reshape(6, NX, NY, NZ), conductivity, factor)
        term = jnp.sum(adjoint[:3] * field[3:] + adjoint[3:] * field[:3], axis=0)
        gradient = gradient + factor * term
    return jnp.stack(fields), gradient
```

```python
import jax
import jax.numpy as jnp
from jax import lax
from jax.experimental import pallas as pl
from jax.experimental.pallas import tpu as pltpu
from jax.sharding import PartitionSpec as P

SWEEPS = 4
DAMPING = 0.8
HALO = SWEEPS - 1
ROWS = 8
LANES = 128

VMEM = pl.BlockSpec(memory_space=pltpu.VMEM)
SMEM = pl.BlockSpec(memory_space=pltpu.SMEM)


def pack_kernel(source, cond, observed, cells, counts, to_right, to_left, payload, values, columns):
    depth = cond.shape[0]
    for out, first in ((to_right, depth - HALO), (to_left, 0)):
        out[:6] = source[:, first:first + HALO]
        out[6] = cond[first:first + HALO]
    tiles = counts.shape[1]
    slots = cells.shape[1]
    cap = slots // tiles
    values[0:6] = observed[0]
    values[6:7] = cells[...].astype(jnp.float32)
    owner = lax.broadcasted_iota(jnp.int32, (tiles, slots), 1) // cap
    spread = (owner == lax.broadcasted_iota(jnp.int32, (tiles, slots), 0)).astype(jnp.bfloat16)
    count = jnp.broadcast_to(counts[...].astype(jnp.float32), (8, tiles)).astype(jnp.bfloat16)
    repeated = lax.dot_general(count, spread, (((1,), (0,)), ((), ())), preferred_element_type=jnp.float32)
    within = lax.broadcasted_iota(jnp.int32, (8, slots), 1) % cap
    live = (within.astype(jnp.float32) < repeated).astype(jnp.float32)
    values[7:8] = live[7:8]
    columns[...] = jnp.zeros_like(columns)
    for part in range(slots // LANES):
        turned = values[:, part * LANES:(part + 1) * LANES].T
        columns[cap + part * LANES:cap + (part + 1) * LANES, 0:ROWS] = turned
    planes = [jnp.zeros((tiles, LANES), jnp.float32), jnp.zeros((tiles, LANES), jnp.float32)]
    for group in range(3):
        for slot in range(cap):
            piece = columns[pl.ds(group * cap + slot, tiles, stride=cap), :]
            shift = (group % 2) * 64 + slot * ROWS
            planes[group // 2] += pltpu.roll(piece, shift, 1) if shift else piece
    for plane in range(2):
        payload[:, plane, :] = planes[plane]


def spread_kernel(received, out, left, right):
    tiles = received.shape[0]
    turned = []
    for plane in range(2):
        here = received[:, plane, :]
        turned.append(jnp.concatenate([here, pltpu.roll(here, LANES - ROWS, 1)], axis=0).T)
    layer = out.shape[2]
    depth = out.shape[1] - 2 * HALO
    plan = (
        ((depth - HALO) * layer, HALO * layer, 0),
        (0, depth * layer, HALO),
        (0, HALO * layer, HALO + depth),
    )
    for group, (first, rows, where) in enumerate(plan):
        base = (group % 2) * 64
        record = jnp.concatenate(
            [turned[group // 2][base + 16 * j:base + 16 * j + ROWS] for j in range(4)], axis=1
        )
        slots = record.shape[1]
        alive = record[7:8]
        cell = record[6:7].astype(jnp.int32)
        value = jnp.where(alive > 0.0, record, 0.0)
        high = value.astype(jnp.bfloat16).astype(jnp.float32)
        rest = value - high
        middle = rest.astype(jnp.bfloat16).astype(jnp.float32)
        low = rest - middle
        row = lax.broadcasted_iota(jnp.int32, (rows, slots), 0) + first
        hit = row == (cell >> 7)
        place = 0
        for terms, names in ((high, (0, 1, 2, 3, 4, 5, 7)), (middle, range(6)), (low, range(6))):
            for name in names:
                left[place:place + rows] = jnp.where(hit, terms[name:name + 1], 0.0).astype(jnp.bfloat16)
                place += rows
        lane = lax.broadcasted_iota(jnp.int32, (LANES, slots), 0) == (cell & (LANES - 1))
        right[...] = lane.astype(jnp.float32).astype(jnp.bfloat16)
        sums = lax.dot_general(
            left[:place], right[...], (((1,), (1,)), ((), ())), preferred_element_type=jnp.float32
        )
        for name in range(6):
            total = sums[name * rows:(name + 1) * rows]
            total = total + sums[(7 + name) * rows:(8 + name) * rows]
            total = total + sums[(13 + name) * rows:(14 + name) * rows]
            out[name, where:where + rows // layer] = total.reshape(rows // layer, layer, LANES)
        out[6, where:where + rows // layer] = sums[6 * rows:7 * rows].reshape(rows // layer, layer, LANES)


PITCH = 24


def clear(buffer, layers):
    for part in range(6):
        for layer in range(layers + 1):
            buffer[part, layer * PITCH:layer * PITCH + 8] = jnp.zeros((8, LANES), jnp.float32)


def coefficients(factor, cond, hl, hr, pq, depth):
    tile = lax.axis_index("tile")
    last = lax.axis_size("tile") - 1
    layers = depth + 2 * HALO
    for layer in range(layers):
        if layer < HALO:
            sigma, scale = hl[6, layer], jnp.where(tile > 0, DAMPING, 0.0)
        elif layer < HALO + depth:
            sigma, scale = cond[layer - HALO], DAMPING
        else:
            sigma, scale = hr[6, layer - HALO - depth], jnp.where(tile < last, DAMPING, 0.0)
        absorb = factor * sigma
        weight = scale / (36.0 + absorb * absorb)
        pq[0, layer] = 6.0 * weight
        pq[1, layer] = absorb * weight


def first_sweep(src, pq, dst, layers):
    def step(layer, carry):
        at = pl.ds(pl.multiple_of(layer * PITCH + 8, 8), 16)
        p, q = pq[0, layer], pq[1, layer]
        for part in range(3):
            re, im = src[part, layer], src[part + 3, layer]
            dst[part, at] = p * re + q * im
            dst[part + 3, at] = p * im - q * re
        return carry

    lax.fori_loop(0, layers, step, 0, unroll=2)


def sweep(src, pq, old, new, lo, hi, unroll, emit=None):
    lane = lax.broadcasted_iota(jnp.int32, (16, LANES), 1)
    not_first, not_last = lane > 0, lane < LANES - 1

    def neighbours(part, base):
        middle = old[part, pl.ds(base, 16)]
        beside = old[part, pl.ds(base - PITCH, 16)] + old[part, pl.ds(base + PITCH, 16)]
        beside = beside + (old[part, pl.ds(base - 1, 16)] + old[part, pl.ds(base + 1, 16)])
        beside = beside + jnp.where(not_first, pltpu.roll(middle, 1, 1), 0.0)
        beside = beside + jnp.where(not_last, pltpu.roll(middle, LANES - 1, 1), 0.0)
        return middle, beside

    def step(layer, carry):
        base = layer * PITCH + 8
        p, q = pq[0, layer], pq[1, layer]
        results = []
        for part in range(3):
            mid_re, sum_re = neighbours(part, base)
            mid_im, sum_im = neighbours(part + 3, base)
            sum_re = sum_re + src[part, layer]
            sum_im = sum_im + src[part + 3, layer]
            new_re = (1.0 - DAMPING) * mid_re + (p * sum_re + q * sum_im)
            new_im = (1.0 - DAMPING) * mid_im + (p * sum_im - q * sum_re)
            if emit is None:
                at = pl.ds(pl.multiple_of(base, 8), 16)
                new[part, at] = new_re
                new[part + 3, at] = new_im
            results.append((new_re, new_im))
        if emit is not None:
            emit(layer, results)
        return carry

    lax.fori_loop(lo, hi, step, 0, unroll=unroll)


def relax(src, pq, one, two, depth, emit):
    layers = depth + 2 * HALO
    clear(one, layers)
    clear(two, layers)
    first_sweep(src, pq, one, layers)
    old, new = one, two
    for index in range(1, SWEEPS):
        final = index == SWEEPS - 1
        sweep(src, pq, old, new, index, layers - index, 2, emit if final else None)
        old, new = new, old


def forward_kernel(factor, source, cond, hl, hr, field, to_right, to_left, src, pq, one, two):
    depth = cond.shape[0]
    coefficients(factor[0], cond, hl, hr, pq, depth)
    src[:, 0:HALO] = hl[:6]
    src[:, HALO:HALO + depth] = source[...]
    src[:, HALO + depth:] = hr[:6]

    def emit(layer, results):
        for part, (re, im) in enumerate(results):
            field[0, part, layer - HALO] = re
            field[0, part + 3, layer - HALO] = im

    relax(src, pq, one, two, depth, emit)
    to_right[...] = field[0, :, depth - HALO:]
    to_left[...] = field[0, :, 0:HALO]


def adjoint_kernel(factor, sums, cond, hl, hr, field, fl, fr, terms, src, pq, one, two):
    depth = cond.shape[0]
    coefficients(factor[0], cond, hl, hr, pq, depth)
    for part in range(6):
        src[part, 0:HALO] = sums[6, 0:HALO] * fl[part] - sums[part, 0:HALO]
        own = slice(HALO, HALO + depth)
        src[part, own] = sums[6, own] * field[0, part] - sums[part, own]
        src[part, HALO + depth:] = sums[6, HALO + depth:] * fr[part] - sums[part, HALO + depth:]

    def emit(layer, results):
        at = layer - HALO
        total = 0.0
        for part, (re, im) in enumerate(results):
            total = total + (re * field[0, part + 3, at] + im * field[0, part, at])
        total = factor[0] * total
        rows = pl.ds(pl.multiple_of(at * 16, 16), 16)
        for copy in range(terms.shape[0]):
            terms[copy, rows] = total

    relax(src, pq, one, two, depth, emit)


def working(depth):
    layers = depth + 2 * HALO
    buffer = pltpu.VMEM((6, layers * PITCH + 8, LANES), jnp.float32)
    return [
        pltpu.VMEM((6, layers, 16, LANES), jnp.float32),
        pltpu.VMEM((2, layers, 16, LANES), jnp.float32),
        buffer,
        buffer,
    ]


def shape(*dims):
    return jax.ShapeDtypeStruct(dims, jnp.float32)


def cost(flops, size):
    return pl.CostEstimate(flops=flops, bytes_accessed=size, transcendentals=0)


def body(source, conductivity, freq_factor, observed, slot_cells, block_counts):
    tiles, freqs = lax.axis_size("tile"), lax.axis_size("freq")
    depth, ny, nz = conductivity.shape
    slots = slot_cells.shape[0]
    to_right, to_left, payload = pl.pallas_call(
        pack_kernel,
        out_shape=(shape(7, HALO, ny, nz), shape(7, HALO, ny, nz), shape(tiles, 2, LANES)),
        in_specs=[VMEM] * 5,
        out_specs=(VMEM, VMEM, VMEM),
        scratch_shapes=[
            pltpu.VMEM((ROWS, slots), jnp.float32),
            pltpu.VMEM((slots + 2 * (slots // tiles), LANES), jnp.float32),
        ],
        cost_estimate=cost(10**6, 10**6),
        name="pack",
    )(source, conductivity, observed, slot_cells.reshape(1, -1), block_counts.reshape(1, -1))
    rightward = [(i, i + 1) for i in range(tiles - 1)]
    leftward = [(i + 1, i) for i in range(tiles - 1)]
    hl = lax.ppermute(to_right, "tile", rightward)
    hr = lax.ppermute(to_left, "tile", leftward)
    received = lax.all_to_all(payload, "tile", split_axis=0, concat_axis=0, tiled=True)
    field, to_right, to_left = pl.pallas_call(
        forward_kernel,
        out_shape=(shape(1, 6, depth, ny, nz), shape(6, HALO, ny, nz), shape(6, HALO, ny, nz)),
        in_specs=[SMEM] + [VMEM] * 4,
        out_specs=(VMEM, VMEM, VMEM),
        scratch_shapes=working(depth),
        cost_estimate=cost(10**7, 10**6),
        name="forward",
    )(freq_factor, source, conductivity, hl, hr)
    fl = lax.ppermute(to_right, "tile", rightward)
    fr = lax.ppermute(to_left, "tile", leftward)
    layers = depth + 2 * HALO
    sums = pl.pallas_call(
        spread_kernel,
        out_shape=shape(7, layers, ny, nz),
        in_specs=[VMEM],
        out_specs=VMEM,
        scratch_shapes=[
            pltpu.VMEM((19 * depth * ny, slots), jnp.bfloat16),
            pltpu.VMEM((LANES, slots), jnp.bfloat16),
        ],
        cost_estimate=cost(10**7, 10**6),
        name="spread",
    )(received)
    terms = pl.pallas_call(
        adjoint_kernel,
        out_shape=shape(freqs, depth * ny, nz),
        in_specs=[SMEM] + [VMEM] * 7,
        out_specs=VMEM,
        scratch_shapes=working(depth),
        cost_estimate=cost(10**7, 10**6),
        name="adjoint",
    )(freq_factor, sums, conductivity, hl, hr, field, fl, fr)
    terms = lax.all_to_all(terms, "freq", split_axis=0, concat_axis=0, tiled=True)
    gradient = jnp.sum(terms, axis=0).reshape(depth, ny, nz)
    return (field, gradient)


def solution(mesh):
    in_specs = (
        P(None, "tile", None, None),
        P("tile", None, None),
        P("freq"),
        P("freq", None, "tile"),
        P("tile"),
        P("tile"),
    )
    out_specs = (P("freq", None, "tile", None, None), P("tile", None, None))
    return jax.shard_map(body, mesh=mesh, in_specs=in_specs, out_specs=out_specs, check_vma=False)
```

```python
import jax
import jax.numpy as jnp
from jax import lax
from jax.experimental import pallas as pl
from jax.experimental.pallas import tpu as pltpu
from jax.sharding import PartitionSpec as P

SWEEPS = 4
DAMPING = 0.8
HALO = SWEEPS - 1
ROWS = 8
LANES = 128

VMEM = pl.BlockSpec(memory_space=pltpu.VMEM)
SMEM = pl.BlockSpec(memory_space=pltpu.SMEM)


def pack_kernel(source, cond, observed, cells, counts, to_right, to_left, payload, values, columns):
    depth = cond.shape[0]
    for out, first in ((to_right, depth - HALO), (to_left, 0)):
        out[:6] = source[:, first:first + HALO]
        out[6] = cond[first:first + HALO]
    tiles = counts.shape[1]
    slots = cells.shape[1]
    cap = slots // tiles
    for part in range(6):
        values[part:part + 1] = observed[part]
    values[6:7] = cells[...].astype(jnp.float32)
    owner = lax.broadcasted_iota(jnp.int32, (tiles, slots), 1) // cap
    spread = (owner == lax.broadcasted_iota(jnp.int32, (tiles, slots), 0)).astype(jnp.bfloat16)
    count = jnp.broadcast_to(counts[...].astype(jnp.float32), (8, tiles)).astype(jnp.bfloat16)
    repeated = lax.dot_general(count, spread, (((1,), (0,)), ((), ())), preferred_element_type=jnp.float32)
    within = lax.broadcasted_iota(jnp.int32, (8, slots), 1) % cap
    live = (within.astype(jnp.float32) < repeated).astype(jnp.float32)
    values[7:8] = live[7:8]
    columns[...] = jnp.zeros_like(columns)
    for part in range(slots // LANES):
        turned = values[:, part * LANES:(part + 1) * LANES].T
        columns[cap + part * LANES:cap + (part + 1) * LANES, 0:ROWS] = turned
    planes = [jnp.zeros((tiles, LANES), jnp.float32), jnp.zeros((tiles, LANES), jnp.float32)]
    for group in range(3):
        for slot in range(cap):
            piece = columns[pl.ds(group * cap + slot, tiles, stride=cap), :]
            shift = (group % 2) * 64 + slot * ROWS
            planes[group // 2] += pltpu.roll(piece, shift, 1) if shift else piece
    for plane in range(2):
        payload[:, plane, :] = planes[plane]


def spread_kernel(received, out, left, right):
    tiles = received.shape[0]
    turned = []
    for plane in range(2):
        here = received[:, plane, :]
        turned.append(jnp.concatenate([here, pltpu.roll(here, LANES - ROWS, 1)], axis=0).T)
    layer = out.shape[2]
    depth = out.shape[1] - 2 * HALO
    plan = (
        ((depth - HALO) * layer, HALO * layer, 0),
        (0, depth * layer, HALO),
        (0, HALO * layer, HALO + depth),
    )
    for group, (first, rows, where) in enumerate(plan):
        base = (group % 2) * 64
        record = jnp.concatenate(
            [turned[group // 2][base + 16 * j:base + 16 * j + ROWS] for j in range(4)], axis=1
        )
        slots = record.shape[1]
        alive = record[7:8]
        cell = record[6:7].astype(jnp.int32)
        value = jnp.where(alive > 0.0, record, 0.0)
        high = value.astype(jnp.bfloat16).astype(jnp.float32)
        rest = value - high
        middle = rest.astype(jnp.bfloat16).astype(jnp.float32)
        low = rest - middle
        row = lax.broadcasted_iota(jnp.int32, (rows, slots), 0) + first
        hit = row == (cell >> 7)
        place = 0
        for terms, names in ((high, (0, 1, 2, 3, 4, 5, 7)), (middle, range(6)), (low, range(6))):
            for name in names:
                left[place:place + rows] = jnp.where(hit, terms[name:name + 1], 0.0).astype(jnp.bfloat16)
                place += rows
        lane = lax.broadcasted_iota(jnp.int32, (LANES, slots), 0) == (cell & (LANES - 1))
        right[...] = lane.astype(jnp.float32).astype(jnp.bfloat16)
        sums = lax.dot_general(
            left[:place], right[...], (((1,), (1,)), ((), ())), preferred_element_type=jnp.float32
        )
        for name in range(6):
            total = sums[name * rows:(name + 1) * rows]
            total = total + sums[(7 + name) * rows:(8 + name) * rows]
            total = total + sums[(13 + name) * rows:(14 + name) * rows]
            out[name, where:where + rows // layer] = total.reshape(rows // layer, layer, LANES)
        out[6, where:where + rows // layer] = sums[6 * rows:7 * rows].reshape(rows // layer, layer, LANES)


PITCH = 24


def clear(buffer, layers):
    for part in range(6):
        for layer in range(layers + 1):
            buffer[part, layer * PITCH:layer * PITCH + 8] = jnp.zeros((8, LANES), jnp.float32)


def coefficients(factor, cond, hl, hr, pq, depth):
    tile = lax.axis_index("tile")
    last = lax.axis_size("tile") - 1
    layers = depth + 2 * HALO
    for layer in range(layers):
        if layer < HALO:
            sigma, scale = hl[6, layer], jnp.where(tile > 0, DAMPING, 0.0)
        elif layer < HALO + depth:
            sigma, scale = cond[layer - HALO], DAMPING
        else:
            sigma, scale = hr[6, layer - HALO - depth], jnp.where(tile < last, DAMPING, 0.0)
        absorb = factor * sigma
        weight = scale / (36.0 + absorb * absorb)
        pq[0, layer] = 6.0 * weight
        pq[1, layer] = absorb * weight


def first_sweep(src, pq, dst, layers):
    def step(layer, carry):
        at = pl.ds(pl.multiple_of(layer * PITCH + 8, 8), 16)
        p, q = pq[0, layer], pq[1, layer]
        for part in range(3):
            re, im = src[part, layer], src[part + 3, layer]
            dst[part, at] = p * re + q * im
            dst[part + 3, at] = p * im - q * re
        return carry

    lax.fori_loop(0, layers, step, 0, unroll=2)


def sweep(src, pq, old, new, lo, hi, unroll, emit=None):
    lane = lax.broadcasted_iota(jnp.int32, (16, LANES), 1)
    not_first, not_last = lane > 0, lane < LANES - 1

    def neighbours(part, base):
        middle = old[part, pl.ds(base, 16)]
        beside = old[part, pl.ds(base - PITCH, 16)] + old[part, pl.ds(base + PITCH, 16)]
        beside = beside + (old[part, pl.ds(base - 1, 16)] + old[part, pl.ds(base + 1, 16)])
        beside = beside + jnp.where(not_first, pltpu.roll(middle, 1, 1), 0.0)
        beside = beside + jnp.where(not_last, pltpu.roll(middle, LANES - 1, 1), 0.0)
        return middle, beside

    def step(layer, carry):
        base = layer * PITCH + 8
        p, q = pq[0, layer], pq[1, layer]
        results = []
        for part in range(3):
            mid_re, sum_re = neighbours(part, base)
            mid_im, sum_im = neighbours(part + 3, base)
            sum_re = sum_re + src[part, layer]
            sum_im = sum_im + src[part + 3, layer]
            new_re = (1.0 - DAMPING) * mid_re + (p * sum_re + q * sum_im)
            new_im = (1.0 - DAMPING) * mid_im + (p * sum_im - q * sum_re)
            if emit is None:
                at = pl.ds(pl.multiple_of(base, 8), 16)
                new[part, at] = new_re
                new[part + 3, at] = new_im
            results.append((new_re, new_im))
        if emit is not None:
            emit(layer, results)
        return carry

    lax.fori_loop(lo, hi, step, 0, unroll=unroll)


def relax(src, pq, one, two, depth, emit):
    layers = depth + 2 * HALO
    clear(one, layers)
    clear(two, layers)
    first_sweep(src, pq, one, layers)
    old, new = one, two
    for index in range(1, SWEEPS):
        final = index == SWEEPS - 1
        sweep(src, pq, old, new, index, layers - index, 2, emit if final else None)
        old, new = new, old


def forward_kernel(factor, source, cond, hl, hr, field, to_right, to_left, src, pq, one, two):
    depth = cond.shape[0]
    coefficients(factor[0], cond, hl, hr, pq, depth)
    src[:, 0:HALO] = hl[:6]
    src[:, HALO:HALO + depth] = source[...]
    src[:, HALO + depth:] = hr[:6]

    def emit(layer, results):
        for part, (re, im) in enumerate(results):
            field[0, part, layer - HALO] = re
            field[0, part + 3, layer - HALO] = im

    relax(src, pq, one, two, depth, emit)
    to_right[...] = field[0, :, depth - HALO:]
    to_left[...] = field[0, :, 0:HALO]


def adjoint_kernel(factor, sums, cond, hl, hr, field, fl, fr, terms, src, pq, one, two):
    depth = cond.shape[0]
    coefficients(factor[0], cond, hl, hr, pq, depth)
    for part in range(6):
        src[part, 0:HALO] = sums[6, 0:HALO] * fl[part] - sums[part, 0:HALO]
        own = slice(HALO, HALO + depth)
        src[part, own] = sums[6, own] * field[0, part] - sums[part, own]
        src[part, HALO + depth:] = sums[6, HALO + depth:] * fr[part] - sums[part, HALO + depth:]

    def emit(layer, results):
        at = layer - HALO
        total = 0.0
        for part, (re, im) in enumerate(results):
            total = total + (re * field[0, part + 3, at] + im * field[0, part, at])
        total = factor[0] * total
        rows = pl.ds(pl.multiple_of(at * 16, 16), 16)
        for copy in range(terms.shape[0]):
            terms[copy, rows] = total

    relax(src, pq, one, two, depth, emit)


def working(depth):
    layers = depth + 2 * HALO
    buffer = pltpu.VMEM((6, layers * PITCH + 8, LANES), jnp.float32)
    return [
        pltpu.VMEM((6, layers, 16, LANES), jnp.float32),
        pltpu.VMEM((2, layers, 16, LANES), jnp.float32),
        buffer,
        buffer,
    ]


def shape(*dims):
    return jax.ShapeDtypeStruct(dims, jnp.float32)


LIMIT = pltpu.CompilerParams(vmem_limit_bytes=16 * 2**20)


def cost(flops, size):
    return pl.CostEstimate(flops=flops, bytes_accessed=size, transcendentals=0)


def body(source, conductivity, freq_factor, observed, slot_cells, block_counts):
    tiles, freqs = lax.axis_size("tile"), lax.axis_size("freq")
    depth, ny, nz = conductivity.shape
    slots = slot_cells.shape[0]
    to_right, to_left, payload = pl.pallas_call(
        pack_kernel,
        out_shape=(shape(7, HALO, ny, nz), shape(7, HALO, ny, nz), shape(tiles, 2, LANES)),
        in_specs=[VMEM] * 5,
        out_specs=(VMEM, VMEM, VMEM),
        scratch_shapes=[
            pltpu.VMEM((ROWS, slots), jnp.float32),
            pltpu.VMEM((slots + 2 * (slots // tiles), LANES), jnp.float32),
        ],
        cost_estimate=cost(10**6, 10**6),
        name="pack",
    )(source, conductivity, observed.transpose(1, 0, 2), slot_cells.reshape(1, -1), block_counts.reshape(1, -1))
    rightward = [(i, i + 1) for i in range(tiles - 1)]
    leftward = [(i + 1, i) for i in range(tiles - 1)]
    hl = lax.ppermute(to_right, "tile", rightward)
    hr = lax.ppermute(to_left, "tile", leftward)
    received = lax.all_to_all(payload, "tile", split_axis=0, concat_axis=0, tiled=True)
    field, to_right, to_left = pl.pallas_call(
        forward_kernel,
        out_shape=(shape(1, 6, depth, ny, nz), shape(6, HALO, ny, nz), shape(6, HALO, ny, nz)),
        in_specs=[SMEM] + [VMEM] * 4,
        out_specs=(VMEM, VMEM, VMEM),
        scratch_shapes=working(depth),
        cost_estimate=cost(10**10, 10**9),
        compiler_params=LIMIT,
        name="forward",
    )(freq_factor, source, conductivity, hl, hr)
    fl = lax.ppermute(to_right, "tile", rightward)
    fr = lax.ppermute(to_left, "tile", leftward)
    layers = depth + 2 * HALO
    sums = pl.pallas_call(
        spread_kernel,
        out_shape=shape(7, layers, ny, nz),
        in_specs=[VMEM],
        out_specs=VMEM,
        scratch_shapes=[
            pltpu.VMEM((19 * depth * ny, slots), jnp.bfloat16),
            pltpu.VMEM((LANES, slots), jnp.bfloat16),
        ],
        cost_estimate=cost(10**10, 10**9),
        compiler_params=LIMIT,
        name="spread",
    )(received)
    terms = pl.pallas_call(
        adjoint_kernel,
        out_shape=shape(freqs, depth * ny, nz),
        in_specs=[SMEM] + [VMEM] * 7,
        out_specs=VMEM,
        scratch_shapes=working(depth),
        cost_estimate=cost(10**7, 10**6),
        compiler_params=LIMIT,
        name="adjoint",
    )(freq_factor, sums, conductivity, hl, hr, field, fl, fr)
    terms = lax.all_to_all(terms, "freq", split_axis=0, concat_axis=0, tiled=True)
    gradient = jnp.sum(terms, axis=0).reshape(depth, ny, nz)
    return (field, gradient)


def solution(mesh):
    in_specs = (
        P(None, "tile", None, None),
        P("tile", None, None),
        P("freq"),
        P("freq", None, "tile"),
        P("tile"),
        P("tile"),
    )
    out_specs = (P("freq", None, "tile", None, None), P("tile", None, None))
    return jax.shard_map(body, mesh=mesh, in_specs=in_specs, out_specs=out_specs, check_vma=False)
```

```python
import jax
import jax.numpy as jnp
from jax import lax
from jax.experimental import pallas as pl
from jax.experimental.pallas import tpu as pltpu
from jax.sharding import PartitionSpec as P

SWEEPS = 4
DAMPING = 0.8
HALO = SWEEPS - 1
ROWS = 8
LANES = 128

VMEM = pl.BlockSpec(memory_space=pltpu.VMEM)
SMEM = pl.BlockSpec(memory_space=pltpu.SMEM)
HBM = pl.BlockSpec(memory_space=pltpu.HBM)


def pack_kernel(
    source, cond, observed, cells, counts, own, near_edge, payload,
    observed_in, cells_in, counts_in, values, columns, arrived,
):
    core = lax.axis_index("tile") % 2
    edge = pl.ds(2 * core, 2)
    copies = [
        pltpu.make_async_copy(start, end, arrived.at[i])
        for i, (start, end) in enumerate(
            (
                (observed, observed_in),
                (cells, cells_in),
                (counts, counts_in),
                (cond, own.at[6]),
                (cond.at[edge], near_edge.at[6]),
                (source, own.at[pl.ds(0, 6)]),
                (source.at[:, edge], near_edge.at[pl.ds(0, 6)]),
            )
        )
    ]
    for copy in copies:
        copy.start()
    for copy in copies[:3]:
        copy.wait()
    tiles = counts.shape[1]
    slots = cells.shape[1]
    cap = slots // tiles
    for part in range(6):
        values[part:part + 1] = observed_in[part]
    values[6:7] = cells_in[...].astype(jnp.float32)
    owner = lax.broadcasted_iota(jnp.int32, (tiles, slots), 1) // cap
    spread = (owner == lax.broadcasted_iota(jnp.int32, (tiles, slots), 0)).astype(jnp.bfloat16)
    count = jnp.broadcast_to(counts_in[...].astype(jnp.float32), (8, tiles)).astype(jnp.bfloat16)
    repeated = lax.dot_general(count, spread, (((1,), (0,)), ((), ())), preferred_element_type=jnp.float32)
    within = lax.broadcasted_iota(jnp.int32, (8, slots), 1) % cap
    live = (within.astype(jnp.float32) < repeated).astype(jnp.float32)
    values[7:8] = live[7:8]
    columns[...] = jnp.zeros_like(columns)
    for part in range(slots // LANES):
        turned = values[:, part * LANES:(part + 1) * LANES].T
        columns[cap + part * LANES:cap + (part + 1) * LANES, 0:ROWS] = turned
    planes = [jnp.zeros((tiles, LANES), jnp.float32), jnp.zeros((tiles, LANES), jnp.float32)]
    for group in range(3):
        for slot in range(cap):
            piece = columns[pl.ds(group * cap + slot, tiles, stride=cap), :]
            shift = (group % 2) * 64 + slot * ROWS
            planes[group // 2] += pltpu.roll(piece, shift, 1) if shift else piece
    for plane in range(2):
        payload[:, plane, :] = planes[plane]
    for copy in copies[3:]:
        copy.wait()


def spread_kernel(received, out, left, right):
    tiles = received.shape[0]
    turned = []
    for plane in range(2):
        here = received[:, plane, :]
        turned.append(jnp.concatenate([here, pltpu.roll(here, LANES - ROWS, 1)], axis=0).T)
    layer = out.shape[2]
    depth = out.shape[1] - 2 * HALO
    plan = (
        ((depth - HALO) * layer, HALO * layer, 0),
        (0, depth * layer, HALO),
        (0, HALO * layer, HALO + depth),
    )
    for group, (first, rows, where) in enumerate(plan):
        base = (group % 2) * 64
        record = jnp.concatenate(
            [turned[group // 2][base + 16 * j:base + 16 * j + ROWS] for j in range(4)], axis=1
        )
        slots = record.shape[1]
        alive = record[7:8]
        cell = record[6:7].astype(jnp.int32)
        value = jnp.where(alive > 0.0, record, 0.0)
        high = value.astype(jnp.bfloat16).astype(jnp.float32)
        rest = value - high
        middle = rest.astype(jnp.bfloat16).astype(jnp.float32)
        low = rest - middle
        row = lax.broadcasted_iota(jnp.int32, (rows, slots), 0) + first
        hit = row == (cell >> 7)
        place = 0
        for terms, names in ((high, (0, 1, 2, 3, 4, 5, 7)), (middle, range(6)), (low, range(6))):
            for name in names:
                left[place:place + rows] = jnp.where(hit, terms[name:name + 1], 0.0).astype(jnp.bfloat16)
                place += rows
        lane = lax.broadcasted_iota(jnp.int32, (LANES, slots), 0) == (cell & (LANES - 1))
        right[...] = lane.astype(jnp.float32).astype(jnp.bfloat16)
        sums = lax.dot_general(
            left[:place], right[...], (((1,), (1,)), ((), ())), preferred_element_type=jnp.float32
        )
        for name in range(6):
            total = sums[name * rows:(name + 1) * rows]
            total = total + sums[(7 + name) * rows:(8 + name) * rows]
            total = total + sums[(13 + name) * rows:(14 + name) * rows]
            out[name, where:where + rows // layer] = total.reshape(rows // layer, layer, LANES)
        out[6, where:where + rows // layer] = sums[6 * rows:7 * rows].reshape(rows // layer, layer, LANES)


PITCH = 24


def clear(buffer, layers):
    for part in range(6):
        for layer in range(layers + 1):
            buffer[part, layer * PITCH:layer * PITCH + 8] = jnp.zeros((8, LANES), jnp.float32)


def coefficients(absorbs, pq, tile, tiles):
    depth = len(absorbs) - 4 * HALO
    for layer, absorb in enumerate(absorbs):
        place = tile * depth + layer - 2 * HALO
        scale = jnp.where((place >= 0) & (place < tiles * depth), DAMPING, 0.0)
        weight = scale / (36.0 + absorb * absorb)
        pq[0, layer] = 6.0 * weight
        pq[1, layer] = absorb * weight


def first_sweep(src, pq, dst, layers):
    def step(layer, carry):
        at = pl.ds(pl.multiple_of(layer * PITCH + 8, 8), 16)
        p, q = pq[0, layer], pq[1, layer]
        for part in range(3):
            re, im = src[part, layer], src[part + 3, layer]
            dst[part, at] = p * re + q * im
            dst[part + 3, at] = p * im - q * re
        return carry

    lax.fori_loop(0, layers, step, 0, unroll=2)


def sweep(src, pq, old, new, lo, hi, unroll, emit=None):
    lane = lax.broadcasted_iota(jnp.int32, (16, LANES), 1)
    not_first, not_last = lane > 0, lane < LANES - 1

    def neighbours(part, base):
        middle = old[part, pl.ds(base, 16)]
        beside = old[part, pl.ds(base - PITCH, 16)] + old[part, pl.ds(base + PITCH, 16)]
        beside = beside + (old[part, pl.ds(base - 1, 16)] + old[part, pl.ds(base + 1, 16)])
        beside = beside + jnp.where(not_first, pltpu.roll(middle, 1, 1), 0.0)
        beside = beside + jnp.where(not_last, pltpu.roll(middle, LANES - 1, 1), 0.0)
        return middle, beside

    def step(layer, carry):
        base = layer * PITCH + 8
        p, q = pq[0, layer], pq[1, layer]
        results = []
        for part in range(3):
            mid_re, sum_re = neighbours(part, base)
            mid_im, sum_im = neighbours(part + 3, base)
            sum_re = sum_re + src[part, layer]
            sum_im = sum_im + src[part + 3, layer]
            new_re = (1.0 - DAMPING) * mid_re + (p * sum_re + q * sum_im)
            new_im = (1.0 - DAMPING) * mid_im + (p * sum_im - q * sum_re)
            if emit is None:
                at = pl.ds(pl.multiple_of(base, 8), 16)
                new[part, at] = new_re
                new[part + 3, at] = new_im
            results.append((new_re, new_im))
        if emit is not None:
            emit(layer, results)
        return carry

    lax.fori_loop(lo, hi, step, 0, unroll=unroll)


def relax(src, pq, one, two, emit):
    layers = src.shape[1]
    clear(one, layers)
    clear(two, layers)
    first_sweep(src, pq, one, layers)
    old, new = one, two
    for index in range(1, SWEEPS):
        final = index == SWEEPS - 1
        sweep(src, pq, old, new, index, layers - index, 2, emit if final else None)
        old, new = new, old


def choose_kernel(own, other, out):
    core = lax.axis_index("tile") % 2
    depth = own.shape[1]
    out[:, 0:depth] = other[...]
    out[:, depth:] = own[:, pl.ds(2 * (1 - core), 2)]


def forward_kernel(factor, own, other, far, edge, near, near_pq, src, pq, one, two):
    depth = own.shape[1]
    tile, tiles = lax.axis_index("tile"), lax.axis_size("tile")
    even = tile % 2 == 0
    views = [(far, depth + i, edge, i) for i in range(2)]
    views += [(far, i, other, i) for i in range(depth)]
    views += [(own, i, own, i) for i in range(depth)]
    views += [(other, i, far, i) for i in range(depth)]
    views += [(edge, i, far, depth + i) for i in range(2)]
    absorbs = []
    for layer, (first, at, second, there) in enumerate(views):
        if first is second:
            src[:, layer] = first[:6, at]
            absorbs.append(factor[0] * first[6, at])
        else:
            src[:, layer] = jnp.where(even, first[:6, at], second[:6, there])
            absorbs.append(factor[0] * jnp.where(even, first[6, at], second[6, there]))
    coefficients(absorbs, pq, tile, tiles)
    near_pq[...] = pq[:, HALO:-HALO]

    def emit(layer, results):
        for part, (re, im) in enumerate(results):
            near[part, layer - HALO] = re
            near[part + 3, layer - HALO] = im

    relax(src, pq, one, two, emit)


def adjoint_kernel(factor, sums, near, pq, terms, field, src, one, two, left):
    depth = near.shape[1] - 2 * HALO
    copy = pltpu.make_async_copy(near.at[:, pl.ds(HALO, depth)], field.at[0], left)
    copy.start()
    for part in range(6):
        src[part] = sums[6] * near[part] - sums[part]

    def emit(layer, results):
        total = 0.0
        for part, (re, im) in enumerate(results):
            total = total + (re * near[part + 3, layer] + im * near[part, layer])
        total = factor[0] * total
        rows = pl.ds(pl.multiple_of((layer - HALO) * 16, 16), 16)
        for index in range(terms.shape[0]):
            terms[index, rows] = total

    relax(src, pq, one, two, emit)
    copy.wait()


def working(layers):
    buffer = pltpu.VMEM((6, layers * PITCH + 8, LANES), jnp.float32)
    return [pltpu.VMEM((6, layers, 16, LANES), jnp.float32), buffer, buffer]


def shape(*dims):
    return jax.ShapeDtypeStruct(dims, jnp.float32)


LIMIT = pltpu.CompilerParams(vmem_limit_bytes=16 * 2**20)


def cost(flops, size):
    return pl.CostEstimate(flops=flops, bytes_accessed=size, transcendentals=0)


def body(source, conductivity, freq_factor, observed, slot_cells, block_counts):
    tiles, freqs = lax.axis_size("tile"), lax.axis_size("freq")
    depth, ny, nz = conductivity.shape
    slots = slot_cells.shape[0]
    own, near_edge, payload = pl.pallas_call(
        pack_kernel,
        out_shape=(shape(7, depth, ny, nz), shape(7, 2, ny, nz), shape(tiles, 2, LANES)),
        in_specs=[HBM] * 5,
        out_specs=(VMEM, VMEM, VMEM),
        scratch_shapes=[
            pltpu.VMEM((6, 1, slots), jnp.float32),
            pltpu.VMEM((1, slots), jnp.int32),
            pltpu.VMEM((1, tiles), jnp.int32),
            pltpu.VMEM((ROWS, slots), jnp.float32),
            pltpu.VMEM((slots + 2 * (slots // tiles), LANES), jnp.float32),
            pltpu.SemaphoreType.DMA((7,)),
        ],
        compiler_params=LIMIT,
        cost_estimate=cost(10**6, 10**6),
        name="pack",
    )(
        *(
            pltpu.with_memory_space_constraint(x, pltpu.HBM)
            for x in (
                source,
                conductivity,
                observed.transpose(1, 0, 2),
                slot_cells.reshape(1, -1),
                block_counts.reshape(1, -1),
            )
        )
    )
    chips = tiles // 2
    other = lax.ppermute(own, "tile", [(i, i ^ 1) for i in range(tiles)])
    received = lax.all_to_all(payload, "tile", split_axis=0, concat_axis=0, tiled=True)
    six = pl.pallas_call(
        choose_kernel,
        out_shape=shape(7, depth + 2, ny, nz),
        in_specs=[VMEM] * 2,
        out_specs=VMEM,
        compiler_params=LIMIT,
        cost_estimate=cost(10**10, 10**9),
        name="choose",
    )(own, other)
    up = [(2 * k, 2 * k + 2) for k in range(chips - 1)]
    down = [(2 * k + 2, 2 * k) for k in range(chips - 1)]
    far = lax.ppermute(six, "tile", up + [(i + 1, j + 1) for i, j in down])
    edge = lax.ppermute(near_edge, "tile", down + [(i + 1, j + 1) for i, j in up])
    wide, layers = depth + 4 * HALO, depth + 2 * HALO
    near, near_pq = pl.pallas_call(
        forward_kernel,
        out_shape=(shape(6, layers, ny, nz), shape(2, layers, ny, nz)),
        in_specs=[SMEM] + [VMEM] * 4,
        out_specs=(VMEM, VMEM),
        scratch_shapes=[working(wide)[0], pltpu.VMEM((2, wide, ny, nz), jnp.float32)] + working(wide)[1:],
        compiler_params=LIMIT,
        cost_estimate=cost(10**6, 10**6),
        name="forward",
    )(freq_factor, own, other, far, edge)
    sums = pl.pallas_call(
        spread_kernel,
        out_shape=shape(7, layers, ny, nz),
        in_specs=[VMEM],
        out_specs=VMEM,
        scratch_shapes=[
            pltpu.VMEM((19 * depth * ny, slots), jnp.bfloat16),
            pltpu.VMEM((LANES, slots), jnp.bfloat16),
        ],
        compiler_params=LIMIT,
        cost_estimate=cost(10**10, 10**9),
        name="spread",
    )(received)
    terms, field = pl.pallas_call(
        adjoint_kernel,
        out_shape=(shape(freqs, depth * ny, nz), shape(1, 6, depth, ny, nz)),
        in_specs=[SMEM] + [VMEM] * 3,
        out_specs=(VMEM, HBM),
        scratch_shapes=working(layers) + [pltpu.SemaphoreType.DMA],
        compiler_params=LIMIT,
        cost_estimate=cost(10**7, 10**6),
        name="adjoint",
    )(freq_factor, sums, near, near_pq)
    terms = lax.all_to_all(terms, "freq", split_axis=0, concat_axis=0, tiled=True)
    gradient = jnp.sum(terms, axis=0).reshape(depth, ny, nz)
    return (field, gradient)


def solution(mesh):
    in_specs = (
        P(None, "tile", None, None),
        P("tile", None, None),
        P("freq"),
        P("freq", None, "tile"),
        P("tile"),
        P("tile"),
    )
    out_specs = (P("freq", None, "tile", None, None), P("tile", None, None))
    return jax.shard_map(body, mesh=mesh, in_specs=in_specs, out_specs=out_specs, check_vma=False)
```

```python
import jax
import jax.numpy as jnp
from jax import lax
from jax.experimental import pallas as pl
from jax.experimental.pallas import tpu as pltpu
from jax.sharding import PartitionSpec as P

SWEEPS = 4
DAMPING = 0.8
HALO = SWEEPS - 1
ROWS = 8
LANES = 128

VMEM = pl.BlockSpec(memory_space=pltpu.VMEM)
SMEM = pl.BlockSpec(memory_space=pltpu.SMEM)
HBM = pl.BlockSpec(memory_space=pltpu.HBM)


def pack_kernel(
    source, cond, observed, cells, counts, own, near_edge, payload,
    observed_in, cells_in, counts_in, values, columns, arrived,
):
    core = lax.axis_index("tile") % 2
    edge = pl.ds(2 * (1 - core), 2)
    copies = [
        pltpu.make_async_copy(start, end, arrived.at[i])
        for i, (start, end) in enumerate(
            (
                (observed, observed_in),
                (cells, cells_in),
                (counts, counts_in),
                (cond, own.at[6]),
                (cond.at[edge], near_edge.at[6]),
                (source, own.at[pl.ds(0, 6)]),
                (source.at[:, edge], near_edge.at[pl.ds(0, 6)]),
            )
        )
    ]
    for copy in copies:
        copy.start()
    for copy in copies[:3]:
        copy.wait()
    tiles = counts.shape[1]
    slots = cells.shape[1]
    cap = slots // tiles
    for part in range(6):
        values[part:part + 1] = observed_in[part]
    values[6:7] = cells_in[...].astype(jnp.float32)
    owner = lax.broadcasted_iota(jnp.int32, (tiles, slots), 1) // cap
    spread = (owner == lax.broadcasted_iota(jnp.int32, (tiles, slots), 0)).astype(jnp.bfloat16)
    count = jnp.broadcast_to(counts_in[...].astype(jnp.float32), (8, tiles)).astype(jnp.bfloat16)
    repeated = lax.dot_general(count, spread, (((1,), (0,)), ((), ())), preferred_element_type=jnp.float32)
    within = lax.broadcasted_iota(jnp.int32, (8, slots), 1) % cap
    live = (within.astype(jnp.float32) < repeated).astype(jnp.float32)
    values[7:8] = live[7:8]
    columns[...] = jnp.zeros_like(columns)
    for part in range(slots // LANES):
        turned = values[:, part * LANES:(part + 1) * LANES].T
        columns[cap + part * LANES:cap + (part + 1) * LANES, 0:ROWS] = turned
    planes = [jnp.zeros((tiles, LANES), jnp.float32), jnp.zeros((tiles, LANES), jnp.float32)]
    for group in range(3):
        for slot in range(cap):
            piece = columns[pl.ds(group * cap + slot, tiles, stride=cap), :]
            shift = (group % 2) * 64 + slot * ROWS
            planes[group // 2] += pltpu.roll(piece, shift, 1) if shift else piece
    for plane in range(2):
        payload[:, plane, :] = planes[plane]
    for copy in copies[3:]:
        copy.wait()


def spread_kernel(received, out, left, right):
    tiles = received.shape[0]
    turned = []
    for plane in range(2):
        here = received[:, plane, :]
        turned.append(jnp.concatenate([here, pltpu.roll(here, LANES - ROWS, 1)], axis=0).T)
    layer = out.shape[2]
    depth = out.shape[1] - 2 * HALO
    plan = (
        ((depth - HALO) * layer, HALO * layer, 0),
        (0, depth * layer, HALO),
        (0, HALO * layer, HALO + depth),
    )
    for group, (first, rows, where) in enumerate(plan):
        base = (group % 2) * 64
        record = jnp.concatenate(
            [turned[group // 2][base + 16 * j:base + 16 * j + ROWS] for j in range(4)], axis=1
        )
        slots = record.shape[1]
        alive = record[7:8]
        cell = record[6:7].astype(jnp.int32)
        value = jnp.where(alive > 0.0, record, 0.0)
        high = value.astype(jnp.bfloat16).astype(jnp.float32)
        rest = value - high
        middle = rest.astype(jnp.bfloat16).astype(jnp.float32)
        low = rest - middle
        row = lax.broadcasted_iota(jnp.int32, (rows, slots), 0) + first
        hit = row == (cell >> 7)
        place = 0
        for terms, names in ((high, (0, 1, 2, 3, 4, 5, 7)), (middle, range(6)), (low, range(6))):
            for name in names:
                left[place:place + rows] = jnp.where(hit, terms[name:name + 1], 0.0).astype(jnp.bfloat16)
                place += rows
        lane = lax.broadcasted_iota(jnp.int32, (LANES, slots), 0) == (cell & (LANES - 1))
        right[...] = lane.astype(jnp.float32).astype(jnp.bfloat16)
        sums = lax.dot_general(
            left[:place], right[...], (((1,), (1,)), ((), ())), preferred_element_type=jnp.float32
        )
        for name in range(6):
            total = sums[name * rows:(name + 1) * rows]
            total = total + sums[(7 + name) * rows:(8 + name) * rows]
            total = total + sums[(13 + name) * rows:(14 + name) * rows]
            out[name, where:where + rows // layer] = total.reshape(rows // layer, layer, LANES)
        out[6, where:where + rows // layer] = sums[6 * rows:7 * rows].reshape(rows // layer, layer, LANES)


PITCH = 24


def clear(buffer, layers):
    for part in range(6):
        for layer in range(layers + 1):
            buffer[part, layer * PITCH:layer * PITCH + 8] = jnp.zeros((8, LANES), jnp.float32)


def coefficients(absorbs, pq, tile, tiles):
    depth = len(absorbs) - 4 * HALO
    for layer, absorb in enumerate(absorbs):
        place = tile * depth + layer - 2 * HALO
        scale = jnp.where((place >= 0) & (place < tiles * depth), DAMPING, 0.0)
        weight = scale / (36.0 + absorb * absorb)
        pq[0, layer] = 6.0 * weight
        pq[1, layer] = absorb * weight


def first_sweep(src, pq, dst, layers):
    def step(layer, carry):
        at = pl.ds(pl.multiple_of(layer * PITCH + 8, 8), 16)
        p, q = pq[0, layer], pq[1, layer]
        for part in range(3):
            re, im = src[part, layer], src[part + 3, layer]
            dst[part, at] = p * re + q * im
            dst[part + 3, at] = p * im - q * re
        return carry

    lax.fori_loop(0, layers, step, 0, unroll=2)


def sweep(src, pq, old, new, lo, hi, unroll, emit=None):
    lane = lax.broadcasted_iota(jnp.int32, (16, LANES), 1)
    not_first, not_last = lane > 0, lane < LANES - 1

    def neighbours(part, base):
        middle = old[part, pl.ds(base, 16)]
        beside = old[part, pl.ds(base - PITCH, 16)] + old[part, pl.ds(base + PITCH, 16)]
        beside = beside + (old[part, pl.ds(base - 1, 16)] + old[part, pl.ds(base + 1, 16)])
        beside = beside + jnp.where(not_first, pltpu.roll(middle, 1, 1), 0.0)
        beside = beside + jnp.where(not_last, pltpu.roll(middle, LANES - 1, 1), 0.0)
        return middle, beside

    def step(layer, carry):
        base = layer * PITCH + 8
        p, q = pq[0, layer], pq[1, layer]
        results = []
        for part in range(3):
            mid_re, sum_re = neighbours(part, base)
            mid_im, sum_im = neighbours(part + 3, base)
            sum_re = sum_re + src[part, layer]
            sum_im = sum_im + src[part + 3, layer]
            new_re = (1.0 - DAMPING) * mid_re + (p * sum_re + q * sum_im)
            new_im = (1.0 - DAMPING) * mid_im + (p * sum_im - q * sum_re)
            if emit is None:
                at = pl.ds(pl.multiple_of(base, 8), 16)
                new[part, at] = new_re
                new[part + 3, at] = new_im
            results.append((new_re, new_im))
        if emit is not None:
            emit(layer, results)
        return carry

    lax.fori_loop(lo, hi, step, 0, unroll=unroll)


def relax(src, pq, one, two, emit):
    layers = src.shape[1]
    clear(one, layers)
    clear(two, layers)
    first_sweep(src, pq, one, layers)
    old, new = one, two
    for index in range(1, SWEEPS):
        final = index == SWEEPS - 1
        sweep(src, pq, old, new, index, layers - index, 2, emit if final else None)
        old, new = new, old


def choose_kernel(own, across, out):
    out[0] = own[...]
    out[1] = across[...]


def forward_kernel(factor, own, across, edge, other, near, near_pq, src, pq, one, two):
    depth = own.shape[1]
    tile, tiles = lax.axis_index("tile"), lax.axis_size("tile")
    even = tile % 2 == 0
    mine, theirs = other.at[0], other.at[1]
    views = [(edge, i, across, depth - 2 + i) for i in range(2)]
    views += [(theirs, i, mine, i) for i in range(depth)]
    views += [(own, i, own, i) for i in range(depth)]
    views += [(mine, i, theirs, i) for i in range(depth)]
    views += [(across, i, edge, i) for i in range(2)]
    absorbs = []
    for layer, (first, at, second, there) in enumerate(views):
        if first is second:
            src[:, layer] = first[:6, at]
            absorbs.append(factor[0] * first[6, at])
        else:
            src[:, layer] = jnp.where(even, first[:6, at], second[:6, there])
            absorbs.append(factor[0] * jnp.where(even, first[6, at], second[6, there]))
    coefficients(absorbs, pq, tile, tiles)
    near_pq[...] = pq[:, HALO:-HALO]

    def emit(layer, results):
        for part, (re, im) in enumerate(results):
            near[part, layer - HALO] = re
            near[part + 3, layer - HALO] = im

    relax(src, pq, one, two, emit)


def adjoint_kernel(factor, sums, near, pq, terms, field, src, one, two, left):
    depth = near.shape[1] - 2 * HALO
    copy = pltpu.make_async_copy(near.at[:, pl.ds(HALO, depth)], field.at[0], left)
    copy.start()
    for part in range(6):
        src[part] = sums[6] * near[part] - sums[part]

    def emit(layer, results):
        total = 0.0
        for part, (re, im) in enumerate(results):
            total = total + (re * near[part + 3, layer] + im * near[part, layer])
        total = factor[0] * total
        rows = pl.ds(pl.multiple_of((layer - HALO) * 16, 16), 16)
        for index in range(terms.shape[0]):
            terms[index, rows] = total

    relax(src, pq, one, two, emit)
    copy.wait()


def working(layers):
    buffer = pltpu.VMEM((6, layers * PITCH + 8, LANES), jnp.float32)
    return [pltpu.VMEM((6, layers, 16, LANES), jnp.float32), buffer, buffer]


def shape(*dims):
    return jax.ShapeDtypeStruct(dims, jnp.float32)


LIMIT = pltpu.CompilerParams(vmem_limit_bytes=16 * 2**20)


def cost(flops, size):
    return pl.CostEstimate(flops=flops, bytes_accessed=size, transcendentals=0)


def body(source, conductivity, freq_factor, observed, slot_cells, block_counts):
    tiles, freqs = lax.axis_size("tile"), lax.axis_size("freq")
    depth, ny, nz = conductivity.shape
    slots = slot_cells.shape[0]
    own, near_edge, payload = pl.pallas_call(
        pack_kernel,
        out_shape=(shape(7, depth, ny, nz), shape(7, 2, ny, nz), shape(tiles, 2, LANES)),
        in_specs=[HBM] * 5,
        out_specs=(VMEM, VMEM, VMEM),
        scratch_shapes=[
            pltpu.VMEM((6, 1, slots), jnp.float32),
            pltpu.VMEM((1, slots), jnp.int32),
            pltpu.VMEM((1, tiles), jnp.int32),
            pltpu.VMEM((ROWS, slots), jnp.float32),
            pltpu.VMEM((slots + 2 * (slots // tiles), LANES), jnp.float32),
            pltpu.SemaphoreType.DMA((7,)),
        ],
        compiler_params=LIMIT,
        cost_estimate=cost(10**6, 10**6),
        name="pack",
    )(
        *(
            pltpu.with_memory_space_constraint(x, pltpu.HBM)
            for x in (
                source,
                conductivity,
                observed.transpose(1, 0, 2),
                slot_cells.reshape(1, -1),
                block_counts.reshape(1, -1),
            )
        )
    )
    chips = tiles // 2
    up = [(2 * k, 2 * k + 2) for k in range(chips - 1)]
    down = [(2 * k + 2, 2 * k) for k in range(chips - 1)]
    across = lax.ppermute(own, "tile", down + [(i + 1, j + 1) for i, j in up])
    edge = lax.ppermute(near_edge, "tile", up + [(i + 1, j + 1) for i, j in down])
    received = lax.all_to_all(payload, "tile", split_axis=0, concat_axis=0, tiled=True)
    chosen = pl.pallas_call(
        choose_kernel,
        out_shape=shape(2, 7, depth, ny, nz),
        in_specs=[VMEM] * 2,
        out_specs=VMEM,
        compiler_params=LIMIT,
        cost_estimate=cost(10**10, 10**9),
        name="choose",
    )(own, across)
    other = lax.ppermute(chosen, "tile", [(i, i ^ 1) for i in range(tiles)])
    wide, layers = depth + 4 * HALO, depth + 2 * HALO
    near, near_pq = pl.pallas_call(
        forward_kernel,
        out_shape=(shape(6, layers, ny, nz), shape(2, layers, ny, nz)),
        in_specs=[SMEM] + [VMEM] * 4,
        out_specs=(VMEM, VMEM),
        scratch_shapes=[working(wide)[0], pltpu.VMEM((2, wide, ny, nz), jnp.float32)] + working(wide)[1:],
        compiler_params=LIMIT,
        cost_estimate=cost(10**6, 10**6),
        name="forward",
    )(freq_factor, own, across, edge, other)
    sums = pl.pallas_call(
        spread_kernel,
        out_shape=shape(7, layers, ny, nz),
        in_specs=[VMEM],
        out_specs=VMEM,
        scratch_shapes=[
            pltpu.VMEM((19 * depth * ny, slots), jnp.bfloat16),
            pltpu.VMEM((LANES, slots), jnp.bfloat16),
        ],
        compiler_params=LIMIT,
        cost_estimate=cost(10**10, 10**9),
        name="spread",
    )(received)
    terms, field = pl.pallas_call(
        adjoint_kernel,
        out_shape=(shape(freqs, depth * ny, nz), shape(1, 6, depth, ny, nz)),
        in_specs=[SMEM] + [VMEM] * 3,
        out_specs=(VMEM, HBM),
        scratch_shapes=working(layers) + [pltpu.SemaphoreType.DMA],
        compiler_params=LIMIT,
        cost_estimate=cost(10**7, 10**6),
        name="adjoint",
    )(freq_factor, sums, near, near_pq)
    terms = lax.all_to_all(terms, "freq", split_axis=0, concat_axis=0, tiled=True)
    gradient = jnp.sum(terms, axis=0).reshape(depth, ny, nz)
    return (field, gradient)


def solution(mesh):
    in_specs = (
        P(None, "tile", None, None),
        P("tile", None, None),
        P("freq"),
        P("freq", None, "tile"),
        P("tile"),
        P("tile"),
    )
    out_specs = (P("freq", None, "tile", None, None), P("tile", None, None))
    return jax.shard_map(body, mesh=mesh, in_specs=in_specs, out_specs=out_specs, check_vma=False)
```

```python
import jax
import jax.numpy as jnp
from jax import lax
from jax.experimental import pallas as pl
from jax.experimental.pallas import tpu as pltpu
from jax.sharding import PartitionSpec as P

SWEEPS = 4
DAMPING = 0.8
HALO = SWEEPS - 1
ROWS = 8
LANES = 128

VMEM = pl.BlockSpec(memory_space=pltpu.VMEM)
SMEM = pl.BlockSpec(memory_space=pltpu.SMEM)
HBM = pl.BlockSpec(memory_space=pltpu.HBM)


def pack_kernel(
    source, cond, observed, cells, counts, own, near_edge, payload,
    observed_in, cells_in, counts_in, values, columns, arrived,
):
    core = lax.axis_index("tile") % 2
    edge = pl.ds(2 * (1 - core), 2)
    copies = [
        pltpu.make_async_copy(start, end, arrived.at[i])
        for i, (start, end) in enumerate(
            (
                (observed, observed_in),
                (cells, cells_in),
                (counts, counts_in),
                (cond, own.at[6]),
                (cond.at[edge], near_edge.at[6]),
                (source, own.at[pl.ds(0, 6)]),
                (source.at[:, edge], near_edge.at[pl.ds(0, 6)]),
            )
        )
    ]
    for copy in copies:
        copy.start()
    for copy in copies[:3]:
        copy.wait()
    tiles = counts.shape[1]
    slots = cells.shape[1]
    cap = slots // tiles
    for part in range(6):
        values[part:part + 1] = observed_in[part]
    values[6:7] = cells_in[...].astype(jnp.float32)
    owner = lax.broadcasted_iota(jnp.int32, (tiles, slots), 1) // cap
    spread = (owner == lax.broadcasted_iota(jnp.int32, (tiles, slots), 0)).astype(jnp.bfloat16)
    count = jnp.broadcast_to(counts_in[...].astype(jnp.float32), (8, tiles)).astype(jnp.bfloat16)
    repeated = lax.dot_general(count, spread, (((1,), (0,)), ((), ())), preferred_element_type=jnp.float32)
    within = lax.broadcasted_iota(jnp.int32, (8, slots), 1) % cap
    live = (within.astype(jnp.float32) < repeated).astype(jnp.float32)
    values[7:8] = live[7:8]
    columns[...] = jnp.zeros_like(columns)
    for part in range(slots // LANES):
        turned = values[:, part * LANES:(part + 1) * LANES].T
        columns[cap + part * LANES:cap + (part + 1) * LANES, 0:ROWS] = turned
    planes = [jnp.zeros((tiles, LANES), jnp.float32), jnp.zeros((tiles, LANES), jnp.float32)]
    for group in range(3):
        for slot in range(cap):
            piece = columns[pl.ds(group * cap + slot, tiles, stride=cap), :]
            shift = (group % 2) * 64 + slot * ROWS
            planes[group // 2] += pltpu.roll(piece, shift, 1) if shift else piece
    for plane in range(2):
        payload[:, plane, :] = planes[plane]
    for copy in copies[3:]:
        copy.wait()


def spread_kernel(received, out, left, right):
    tiles = received.shape[0]
    turned = []
    for plane in range(2):
        here = received[:, plane, :]
        turned.append(jnp.concatenate([here, pltpu.roll(here, LANES - ROWS, 1)], axis=0).T)
    layer = out.shape[2]
    depth = out.shape[1] - 2 * HALO
    half = depth * layer // 2
    plan = ((depth - HALO, HALO, 0), (0, depth, HALO), (0, HALO, HALO + depth))
    for group, (first, layers, where) in enumerate(plan):
        base = (group % 2) * 64
        record = jnp.concatenate(
            [turned[group // 2][base + 16 * j:base + 16 * j + ROWS] for j in range(4)], axis=1
        )
        slots = record.shape[1]
        alive = record[7:8]
        cell = record[6:7].astype(jnp.int32)
        value = jnp.where(alive > 0.0, record, 0.0)
        high = value.astype(jnp.bfloat16).astype(jnp.float32)
        rest = value - high
        middle = rest.astype(jnp.bfloat16).astype(jnp.float32)
        low = rest - middle
        row = cell // LANES
        hit = lax.broadcasted_iota(jnp.int32, (half, slots), 0) == row % half
        place = 0
        for terms, names in ((high, (0, 1, 2, 3, 4, 5, 7)), (middle, range(6)), (low, range(6))):
            for name in names:
                left[group, place:place + half] = jnp.where(hit, terms[name:name + 1], 0.0).astype(jnp.bfloat16)
                place += half
        column = cell % LANES + LANES * (row // half)
        lane = lax.broadcasted_iota(jnp.int32, (2 * LANES, slots), 0) == column
        right[group] = lane.astype(jnp.float32).astype(jnp.bfloat16)
        sums = lax.dot_general(
            left[group], right[group], (((1,), (1,)), ((), ())), preferred_element_type=jnp.float32
        )
        for name in range(7):
            total = sums[name * half:(name + 1) * half]
            if name < 6:
                total = total + sums[(7 + name) * half:(8 + name) * half]
                total = total + sums[(13 + name) * half:(14 + name) * half]
            for index in range(layers):
                side, at = divmod((first + index) * layer, half)
                out[name, where + index] = total[at:at + layer, side * LANES:(side + 1) * LANES]


PITCH = 24


def clear(buffer, layers):
    for part in range(6):
        for layer in range(layers + 1):
            buffer[part, layer * PITCH:layer * PITCH + 8] = jnp.zeros((8, LANES), jnp.float32)


def coefficients(absorbs, pq, tile, tiles):
    depth = len(absorbs) - 4 * HALO
    for layer, absorb in enumerate(absorbs):
        place = tile * depth + layer - 2 * HALO
        scale = jnp.where((place >= 0) & (place < tiles * depth), DAMPING, 0.0)
        weight = scale / (36.0 + absorb * absorb)
        pq[0, layer] = 6.0 * weight
        pq[1, layer] = absorb * weight


def first_sweep(src, pq, dst, layers):
    def step(layer, carry):
        at = pl.ds(pl.multiple_of(layer * PITCH + 8, 8), 16)
        p, q = pq[0, layer], pq[1, layer]
        for part in range(3):
            re, im = src[part, layer], src[part + 3, layer]
            dst[part, at] = p * re + q * im
            dst[part + 3, at] = p * im - q * re
        return carry

    lax.fori_loop(0, layers, step, 0, unroll=2)


def sweep(src, pq, old, new, lo, hi, emit=None):
    lane = lax.broadcasted_iota(jnp.int32, (16, LANES), 1)
    not_first, not_last = lane > 0, lane < LANES - 1

    def neighbours(part, base):
        middle = old[part, pl.ds(base, 16)]
        beside = old[part, pl.ds(base - PITCH, 16)] + old[part, pl.ds(base + PITCH, 16)]
        beside = beside + (old[part, pl.ds(base - 1, 16)] + old[part, pl.ds(base + 1, 16)])
        beside = beside + jnp.where(not_first, pltpu.roll(middle, 1, 1), 0.0)
        beside = beside + jnp.where(not_last, pltpu.roll(middle, LANES - 1, 1), 0.0)
        return middle, beside

    def step(layer, carry):
        base = layer * PITCH + 8
        p, q = pq[0, layer], pq[1, layer]
        results = []
        for part in range(3):
            mid_re, sum_re = neighbours(part, base)
            mid_im, sum_im = neighbours(part + 3, base)
            sum_re = sum_re + src[part, layer]
            sum_im = sum_im + src[part + 3, layer]
            new_re = (1.0 - DAMPING) * mid_re + (p * sum_re + q * sum_im)
            new_im = (1.0 - DAMPING) * mid_im + (p * sum_im - q * sum_re)
            if emit is None:
                at = pl.ds(pl.multiple_of(base, 8), 16)
                new[part, at] = new_re
                new[part + 3, at] = new_im
            results.append((new_re, new_im))
        if emit is not None:
            emit(layer, results)
        return carry

    lax.fori_loop(lo, hi, step, 0, unroll=hi - lo)


def relax(src, pq, one, two, emit):
    layers = src.shape[1]
    clear(one, layers)
    clear(two, layers)
    first_sweep(src, pq, one, layers)
    old, new = one, two
    for index in range(1, SWEEPS):
        final = index == SWEEPS - 1
        sweep(src, pq, old, new, index, layers - index, emit if final else None)
        old, new = new, old


def choose_kernel(own, across, out):
    out[0] = own[...]
    out[1] = across[...]


def forward_kernel(factor, own, across, edge, other, near, near_pq, src, pq, one, two):
    depth = own.shape[1]
    tile, tiles = lax.axis_index("tile"), lax.axis_size("tile")
    even = tile % 2 == 0
    mine, theirs = other.at[0], other.at[1]
    views = [(edge, i, across, depth - 2 + i) for i in range(2)]
    views += [(theirs, i, mine, i) for i in range(depth)]
    views += [(own, i, own, i) for i in range(depth)]
    views += [(mine, i, theirs, i) for i in range(depth)]
    views += [(across, i, edge, i) for i in range(2)]
    absorbs = []
    for layer, (first, at, second, there) in enumerate(views):
        if first is second:
            src[:, layer] = first[:6, at]
            absorbs.append(factor[0] * first[6, at])
        else:
            src[:, layer] = jnp.where(even, first[:6, at], second[:6, there])
            absorbs.append(factor[0] * jnp.where(even, first[6, at], second[6, there]))
    coefficients(absorbs, pq, tile, tiles)
    near_pq[...] = pq[:, HALO:-HALO]

    def emit(layer, results):
        for part, (re, im) in enumerate(results):
            near[part, layer - HALO] = re
            near[part + 3, layer - HALO] = im

    relax(src, pq, one, two, emit)


def adjoint_kernel(factor, sums, near, pq, terms, field, src, one, two, left):
    depth = near.shape[1] - 2 * HALO
    copy = pltpu.make_async_copy(near.at[:, pl.ds(HALO, depth)], field.at[0], left)
    copy.start()
    for part in range(6):
        src[part] = sums[6] * near[part] - sums[part]

    def emit(layer, results):
        total = 0.0
        for part, (re, im) in enumerate(results):
            total = total + (re * near[part + 3, layer] + im * near[part, layer])
        total = factor[0] * total
        rows = pl.ds(pl.multiple_of((layer - HALO) * 16, 16), 16)
        for index in range(terms.shape[0]):
            terms[index, rows] = total

    relax(src, pq, one, two, emit)
    copy.wait()


def working(layers):
    buffer = pltpu.VMEM((6, layers * PITCH + 8, LANES), jnp.float32)
    return [pltpu.VMEM((6, layers, 16, LANES), jnp.float32), buffer, buffer]


def shape(*dims):
    return jax.ShapeDtypeStruct(dims, jnp.float32)


LIMIT = pltpu.CompilerParams(vmem_limit_bytes=16 * 2**20)


def cost(flops, size):
    return pl.CostEstimate(flops=flops, bytes_accessed=size, transcendentals=0)


def pack(source, conductivity, observed, slot_cells, block_counts):
    depth, ny, nz = conductivity.shape
    slots, tiles = slot_cells.shape[0], block_counts.shape[0]
    return pl.pallas_call(
        pack_kernel,
        out_shape=(shape(7, depth, ny, nz), shape(7, 2, ny, nz), shape(tiles, 2, LANES)),
        in_specs=[HBM] * 5,
        out_specs=(VMEM, VMEM, VMEM),
        scratch_shapes=[
            pltpu.VMEM((6, 1, slots), jnp.float32),
            pltpu.VMEM((1, slots), jnp.int32),
            pltpu.VMEM((1, tiles), jnp.int32),
            pltpu.VMEM((ROWS, slots), jnp.float32),
            pltpu.VMEM((slots + 2 * (slots // tiles), LANES), jnp.float32),
            pltpu.SemaphoreType.DMA((7,)),
        ],
        compiler_params=LIMIT,
        cost_estimate=cost(10**6, 10**6),
        name="pack",
    )(
        *(
            pltpu.with_memory_space_constraint(x, pltpu.HBM)
            for x in (
                source,
                conductivity,
                observed.transpose(1, 0, 2),
                slot_cells.reshape(1, -1),
                block_counts.reshape(1, -1),
            )
        )
    )


def choose(own, across):
    return pl.pallas_call(
        choose_kernel,
        out_shape=shape(2, *own.shape),
        in_specs=[VMEM] * 2,
        out_specs=VMEM,
        compiler_params=LIMIT,
        cost_estimate=cost(10**10, 10**9),
        name="choose",
    )(own, across)


def forward(factor, own, across, edge, other):
    depth, ny, nz = own.shape[1:]
    wide, layers = depth + 4 * HALO, depth + 2 * HALO
    return pl.pallas_call(
        forward_kernel,
        out_shape=(shape(6, layers, ny, nz), shape(2, layers, ny, nz)),
        in_specs=[SMEM] + [VMEM] * 4,
        out_specs=(VMEM, VMEM),
        scratch_shapes=[working(wide)[0], pltpu.VMEM((2, wide, ny, nz), jnp.float32)] + working(wide)[1:],
        compiler_params=LIMIT,
        cost_estimate=cost(10**6, 10**6),
        name="forward",
    )(factor, own, across, edge, other)


def spread(received, depth, ny, nz):
    slots = received.shape[0] * received.shape[2] // (2 * ROWS)
    return pl.pallas_call(
        spread_kernel,
        out_shape=shape(7, depth + 2 * HALO, ny, nz),
        in_specs=[VMEM],
        out_specs=VMEM,
        scratch_shapes=[
            pltpu.VMEM((3, 19 * depth * ny // 2, slots), jnp.bfloat16),
            pltpu.VMEM((3, 2 * LANES, slots), jnp.bfloat16),
        ],
        compiler_params=LIMIT,
        cost_estimate=cost(10**10, 10**9),
        name="spread",
    )(received)


def adjoint(factor, sums, near, near_pq, freqs):
    layers, ny, nz = near.shape[1:]
    depth = layers - 2 * HALO
    return pl.pallas_call(
        adjoint_kernel,
        out_shape=(shape(freqs, depth * ny, nz), shape(1, 6, depth, ny, nz)),
        in_specs=[SMEM] + [VMEM] * 3,
        out_specs=(VMEM, HBM),
        scratch_shapes=working(layers) + [pltpu.SemaphoreType.DMA],
        compiler_params=LIMIT,
        cost_estimate=cost(10**7, 10**6),
        name="adjoint",
    )(factor, sums, near, near_pq)


def body(source, conductivity, freq_factor, observed, slot_cells, block_counts):
    tiles, freqs = lax.axis_size("tile"), lax.axis_size("freq")
    depth, ny, nz = conductivity.shape
    own, near_edge, payload = pack(source, conductivity, observed, slot_cells, block_counts)
    chips = tiles // 2
    up = [(2 * k, 2 * k + 2) for k in range(chips - 1)]
    down = [(2 * k + 2, 2 * k) for k in range(chips - 1)]
    across = lax.ppermute(own, "tile", down + [(i + 1, j + 1) for i, j in up])
    edge = lax.ppermute(near_edge, "tile", up + [(i + 1, j + 1) for i, j in down])
    received = lax.all_to_all(payload, "tile", split_axis=0, concat_axis=0, tiled=True)
    chosen = choose(own, across)
    other = lax.ppermute(chosen, "tile", [(i, i ^ 1) for i in range(tiles)])
    near, near_pq = forward(freq_factor, own, across, edge, other)
    sums = spread(received, depth, ny, nz)
    terms, field = adjoint(freq_factor, sums, near, near_pq, freqs)
    terms = lax.all_to_all(terms, "freq", split_axis=0, concat_axis=0, tiled=True)
    gradient = jnp.sum(terms, axis=0).reshape(depth, ny, nz)
    return (field, gradient)


def solution(mesh):
    in_specs = (
        P(None, "tile", None, None),
        P("tile", None, None),
        P("freq"),
        P("freq", None, "tile"),
        P("tile"),
        P("tile"),
    )
    out_specs = (P("freq", None, "tile", None, None), P("tile", None, None))
    return jax.shard_map(body, mesh=mesh, in_specs=in_specs, out_specs=out_specs, check_vma=False)
```

```python
import jax
import jax.numpy as jnp
from jax import lax
from jax.experimental import pallas as pl
from jax.experimental.pallas import tpu as pltpu
from jax.sharding import PartitionSpec as P

SWEEPS = 4
DAMPING = 0.8
HALO = SWEEPS - 1
ROWS = 8
LANES = 128

VMEM = pl.BlockSpec(memory_space=pltpu.VMEM)
SMEM = pl.BlockSpec(memory_space=pltpu.SMEM)
HBM = pl.BlockSpec(memory_space=pltpu.HBM)


def pack_kernel(
    source, cond, observed, cells, counts, own, near_edge, payload,
    observed_in, cells_in, counts_in, values, columns, arrived,
):
    core = lax.axis_index("tile") % 2
    edge = pl.ds(2 * (1 - core), 2)
    copies = [
        pltpu.make_async_copy(start, end, arrived.at[i])
        for i, (start, end) in enumerate(
            (
                (observed, observed_in),
                (cells, cells_in),
                (counts, counts_in),
                (cond, own.at[6]),
                (cond.at[edge], near_edge.at[6]),
                (source, own.at[pl.ds(0, 6)]),
                (source.at[:, edge], near_edge.at[pl.ds(0, 6)]),
            )
        )
    ]
    for copy in copies:
        copy.start()
    for copy in copies[:3]:
        copy.wait()
    tiles = counts.shape[1]
    slots = cells.shape[1]
    cap = slots // tiles
    for part in range(6):
        values[part:part + 1] = observed_in[part]
    values[6:7] = cells_in[...].astype(jnp.float32)
    owner = lax.broadcasted_iota(jnp.int32, (tiles, slots), 1) // cap
    spread = (owner == lax.broadcasted_iota(jnp.int32, (tiles, slots), 0)).astype(jnp.bfloat16)
    count = jnp.broadcast_to(counts_in[...].astype(jnp.float32), (8, tiles)).astype(jnp.bfloat16)
    repeated = lax.dot_general(count, spread, (((1,), (0,)), ((), ())), preferred_element_type=jnp.float32)
    within = lax.broadcasted_iota(jnp.int32, (8, slots), 1) % cap
    live = (within.astype(jnp.float32) < repeated).astype(jnp.float32)
    values[7:8] = live[7:8]
    columns[...] = jnp.zeros_like(columns)
    for part in range(slots // LANES):
        turned = values[:, part * LANES:(part + 1) * LANES].T
        columns[cap + part * LANES:cap + (part + 1) * LANES, 0:ROWS] = turned
    planes = [jnp.zeros((tiles, LANES), jnp.float32), jnp.zeros((tiles, LANES), jnp.float32)]
    for group in range(3):
        for slot in range(cap):
            piece = columns[pl.ds(group * cap + slot, tiles, stride=cap), :]
            shift = (group % 2) * 64 + slot * ROWS
            planes[group // 2] += pltpu.roll(piece, shift, 1) if shift else piece
    for plane in range(2):
        payload[:, plane, :] = planes[plane]
    for copy in copies[3:]:
        copy.wait()


def spread_kernel(received, out, left, right):
    tiles = received.shape[0]
    turned = []
    for plane in range(2):
        here = received[:, plane, :]
        turned.append(jnp.concatenate([here, pltpu.roll(here, LANES - ROWS, 1)], axis=0).T)
    layer = out.shape[2]
    depth = out.shape[1] - 2 * HALO
    half = depth * layer // 2
    plan = ((depth - HALO, HALO, 0), (0, depth, HALO), (0, HALO, HALO + depth))
    for group, (first, layers, where) in enumerate(plan):
        base = (group % 2) * 64
        record = jnp.concatenate(
            [turned[group // 2][base + 16 * j:base + 16 * j + ROWS] for j in range(4)], axis=1
        )
        slots = record.shape[1]
        alive = record[7:8]
        cell = record[6:7].astype(jnp.int32)
        value = jnp.where(alive > 0.0, record, 0.0)
        high = value.astype(jnp.bfloat16).astype(jnp.float32)
        rest = value - high
        middle = rest.astype(jnp.bfloat16).astype(jnp.float32)
        low = rest - middle
        row = cell // LANES
        hit = lax.broadcasted_iota(jnp.int32, (half, slots), 0) == row % half
        place = 0
        for terms, names in ((high, (0, 1, 2, 3, 4, 5, 7)), (middle, range(6)), (low, range(6))):
            for name in names:
                left[group, place:place + half] = jnp.where(hit, terms[name:name + 1], 0.0).astype(jnp.bfloat16)
                place += half
        column = cell % LANES + LANES * (row // half)
        lane = lax.broadcasted_iota(jnp.int32, (2 * LANES, slots), 0) == column
        right[group] = lane.astype(jnp.float32).astype(jnp.bfloat16)
        sums = lax.dot_general(
            left[group], right[group], (((1,), (1,)), ((), ())), preferred_element_type=jnp.float32
        )
        for name in range(7):
            total = sums[name * half:(name + 1) * half]
            if name < 6:
                total = total + sums[(7 + name) * half:(8 + name) * half]
                total = total + sums[(13 + name) * half:(14 + name) * half]
            for index in range(layers):
                side, at = divmod((first + index) * layer, half)
                out[name, where + index] = total[at:at + layer, side * LANES:(side + 1) * LANES]


PITCH = 24


def clear(buffer, layers):
    for part in range(6):
        for layer in range(layers + 1):
            buffer[part, layer * PITCH:layer * PITCH + 8] = jnp.zeros((8, LANES), jnp.float32)


def coefficients(absorbs, pq, tile, tiles):
    depth = len(absorbs) - 4 * HALO
    for layer, absorb in enumerate(absorbs):
        place = tile * depth + layer - 2 * HALO
        scale = jnp.where((place >= 0) & (place < tiles * depth), DAMPING, 0.0)
        weight = scale / (36.0 + absorb * absorb)
        pq[0, layer] = 6.0 * weight
        pq[1, layer] = absorb * weight


def first_sweep(src, pq, dst, layers):
    def step(layer, carry):
        at = pl.ds(pl.multiple_of(layer * PITCH + 8, 8), 16)
        p, q = pq[0, layer], pq[1, layer]
        for part in range(3):
            re, im = src[part, layer], src[part + 3, layer]
            dst[part, at] = p * re + q * im
            dst[part + 3, at] = p * im - q * re
        return carry

    lax.fori_loop(0, layers, step, 0, unroll=2)


def sweep(src, pq, old, new, lo, hi, emit=None):
    lane = lax.broadcasted_iota(jnp.int32, (16, LANES), 1)
    not_first, not_last = lane > 0, lane < LANES - 1

    def neighbours(part, base):
        middle = old[part, pl.ds(base, 16)]
        beside = old[part, pl.ds(base - PITCH, 16)] + old[part, pl.ds(base + PITCH, 16)]
        beside = beside + (old[part, pl.ds(base - 1, 16)] + old[part, pl.ds(base + 1, 16)])
        beside = beside + jnp.where(not_first, pltpu.roll(middle, 1, 1), 0.0)
        beside = beside + jnp.where(not_last, pltpu.roll(middle, LANES - 1, 1), 0.0)
        return middle, beside

    def step(layer, carry):
        base = layer * PITCH + 8
        p, q = pq[0, layer], pq[1, layer]
        results = []
        for part in range(3):
            mid_re, sum_re = neighbours(part, base)
            mid_im, sum_im = neighbours(part + 3, base)
            sum_re = sum_re + src[part, layer]
            sum_im = sum_im + src[part + 3, layer]
            new_re = (1.0 - DAMPING) * mid_re + (p * sum_re + q * sum_im)
            new_im = (1.0 - DAMPING) * mid_im + (p * sum_im - q * sum_re)
            if emit is None:
                at = pl.ds(pl.multiple_of(base, 8), 16)
                new[part, at] = new_re
                new[part + 3, at] = new_im
            results.append((new_re, new_im))
        if emit is not None:
            emit(layer, results)
        return carry

    lax.fori_loop(lo, hi, step, 0, unroll=hi - lo)


def relax(src, pq, one, two, emit):
    layers = src.shape[1]
    clear(one, layers)
    clear(two, layers)
    first_sweep(src, pq, one, layers)
    old, new = one, two
    for index in range(1, SWEEPS):
        final = index == SWEEPS - 1
        sweep(src, pq, old, new, index, layers - index, emit if final else None)
        old, new = new, old


def choose_kernel(own, across, edge, out):
    del edge
    out[0] = own[...]
    out[1] = across[...]


def solve_kernel(
    factor, sums, own, across, edge, other, terms, field, near, far_src, far_pq, far_one, far_two,
    src, pq, one, two, written,
):
    depth = own.shape[1]
    tile, tiles = lax.axis_index("tile"), lax.axis_size("tile")
    even = tile % 2 == 0
    mine, theirs = other.at[0], other.at[1]
    views = [(edge, i, across, depth - 2 + i) for i in range(2)]
    views += [(theirs, i, mine, i) for i in range(depth)]
    views += [(own, i, own, i) for i in range(depth)]
    views += [(mine, i, theirs, i) for i in range(depth)]
    views += [(across, i, edge, i) for i in range(2)]
    absorbs = []
    for layer, (first, at, second, there) in enumerate(views):
        if first is second:
            far_src[:, layer] = first[:6, at]
            absorbs.append(factor[0] * first[6, at])
        else:
            far_src[:, layer] = jnp.where(even, first[:6, at], second[:6, there])
            absorbs.append(factor[0] * jnp.where(even, first[6, at], second[6, there]))
    coefficients(absorbs, far_pq, tile, tiles)
    pq[...] = far_pq[:, HALO:-HALO]

    def keep(layer, results):
        for part, (re, im) in enumerate(results):
            near[part, layer - HALO] = re
            near[part + 3, layer - HALO] = im

    relax(far_src, far_pq, far_one, far_two, keep)
    copy = pltpu.make_async_copy(near.at[:, pl.ds(HALO, depth)], field.at[0], written)
    copy.start()
    for part in range(6):
        src[part] = sums[6] * near[part] - sums[part]

    def emit(layer, results):
        total = 0.0
        for part, (re, im) in enumerate(results):
            total = total + (re * near[part + 3, layer] + im * near[part, layer])
        total = factor[0] * total
        rows = pl.ds(pl.multiple_of((layer - HALO) * 16, 16), 16)
        for index in range(terms.shape[0]):
            terms[index, rows] = total

    relax(src, pq, one, two, emit)
    copy.wait()


def working(layers):
    buffer = pltpu.VMEM((6, layers * PITCH + 8, LANES), jnp.float32)
    return [
        pltpu.VMEM((6, layers, 16, LANES), jnp.float32),
        pltpu.VMEM((2, layers, 16, LANES), jnp.float32),
        buffer,
        buffer,
    ]


def shape(*dims):
    return jax.ShapeDtypeStruct(dims, jnp.float32)


LIMIT = pltpu.CompilerParams(vmem_limit_bytes=16 * 2**20)


def cost(flops, size):
    return pl.CostEstimate(flops=flops, bytes_accessed=size, transcendentals=0)


def pack(source, conductivity, observed, slot_cells, block_counts):
    depth, ny, nz = conductivity.shape
    slots, tiles = slot_cells.shape[0], block_counts.shape[0]
    return pl.pallas_call(
        pack_kernel,
        out_shape=(shape(7, depth, ny, nz), shape(7, 2, ny, nz), shape(tiles, 2, LANES)),
        in_specs=[HBM] * 5,
        out_specs=(VMEM, VMEM, VMEM),
        scratch_shapes=[
            pltpu.VMEM((6, 1, slots), jnp.float32),
            pltpu.VMEM((1, slots), jnp.int32),
            pltpu.VMEM((1, tiles), jnp.int32),
            pltpu.VMEM((ROWS, slots), jnp.float32),
            pltpu.VMEM((slots + 2 * (slots // tiles), LANES), jnp.float32),
            pltpu.SemaphoreType.DMA((7,)),
        ],
        compiler_params=LIMIT,
        cost_estimate=cost(10**6, 10**6),
        name="pack",
    )(
        *(
            pltpu.with_memory_space_constraint(x, pltpu.HBM)
            for x in (
                source,
                conductivity,
                observed.transpose(1, 0, 2),
                slot_cells.reshape(1, -1),
                block_counts.reshape(1, -1),
            )
        )
    )


def choose(own, across, edge):
    return pl.pallas_call(
        choose_kernel,
        out_shape=shape(2, *own.shape),
        in_specs=[VMEM] * 3,
        out_specs=VMEM,
        compiler_params=LIMIT,
        cost_estimate=cost(10**10, 10**9),
        name="choose",
    )(own, across, edge)


def spread(received, depth, ny, nz):
    slots = received.shape[0] * received.shape[2] // (2 * ROWS)
    return pl.pallas_call(
        spread_kernel,
        out_shape=shape(7, depth + 2 * HALO, ny, nz),
        in_specs=[VMEM],
        out_specs=VMEM,
        scratch_shapes=[
            pltpu.VMEM((3, 19 * depth * ny // 2, slots), jnp.bfloat16),
            pltpu.VMEM((3, 2 * LANES, slots), jnp.bfloat16),
        ],
        compiler_params=LIMIT,
        cost_estimate=cost(10**10, 10**9),
        name="spread",
    )(received)


def solve(factor, sums, own, across, edge, other, freqs):
    depth, ny, nz = own.shape[1:]
    wide, layers = depth + 4 * HALO, depth + 2 * HALO
    return pl.pallas_call(
        solve_kernel,
        out_shape=(shape(freqs, depth * ny, nz), shape(1, 6, depth, ny, nz)),
        in_specs=[SMEM] + [VMEM] * 5,
        out_specs=(VMEM, HBM),
        scratch_shapes=[
            pltpu.VMEM((6, layers, ny, nz), jnp.float32),
            *working(wide),
            *working(layers),
            pltpu.SemaphoreType.DMA,
        ],
        compiler_params=LIMIT,
        cost_estimate=cost(10**7, 10**6),
        name="solve",
    )(factor, sums, own, across, edge, other)


def body(source, conductivity, freq_factor, observed, slot_cells, block_counts):
    tiles, freqs = lax.axis_size("tile"), lax.axis_size("freq")
    depth, ny, nz = conductivity.shape
    own, near_edge, payload = pack(source, conductivity, observed, slot_cells, block_counts)
    chips = tiles // 2
    up = [(2 * k, 2 * k + 2) for k in range(chips - 1)]
    down = [(2 * k + 2, 2 * k) for k in range(chips - 1)]
    across = lax.ppermute(own, "tile", down + [(i + 1, j + 1) for i, j in up])
    edge = lax.ppermute(near_edge, "tile", up + [(i + 1, j + 1) for i, j in down])
    received = lax.all_to_all(payload, "tile", split_axis=0, concat_axis=0, tiled=True)
    chosen = choose(own, across, edge)
    other = lax.ppermute(chosen, "tile", [(i, i ^ 1) for i in range(tiles)])
    sums = spread(received, depth, ny, nz)
    terms, field = solve(freq_factor, sums, own, across, edge, other, freqs)
    terms = lax.all_to_all(terms, "freq", split_axis=0, concat_axis=0, tiled=True)
    gradient = jnp.sum(terms, axis=0).reshape(depth, ny, nz)
    return (field, gradient)


def solution(mesh):
    in_specs = (
        P(None, "tile", None, None),
        P("tile", None, None),
        P("freq"),
        P("freq", None, "tile"),
        P("tile"),
        P("tile"),
    )
    out_specs = (P("freq", None, "tile", None, None), P("tile", None, None))
    return jax.shard_map(body, mesh=mesh, in_specs=in_specs, out_specs=out_specs, check_vma=False)
```

```python
import jax
import jax.numpy as jnp
from jax import lax
from jax.experimental import pallas as pl
from jax.experimental.pallas import tpu as pltpu
from jax.sharding import PartitionSpec as P

SWEEPS = 4
DAMPING = 0.8
HALO = SWEEPS - 1
ROWS = 8
LANES = 128

VMEM = pl.BlockSpec(memory_space=pltpu.VMEM)
SMEM = pl.BlockSpec(memory_space=pltpu.SMEM)
HBM = pl.BlockSpec(memory_space=pltpu.HBM)


def pack_kernel(
    source, cond, observed, cells, counts, own, payload,
    observed_in, cells_in, counts_in, values, columns, arrived,
):
    copies = [
        pltpu.make_async_copy(start, end, arrived.at[i])
        for i, (start, end) in enumerate(
            (
                (observed, observed_in),
                (cells, cells_in),
                (counts, counts_in),
                (cond, own.at[6]),
                (source, own.at[pl.ds(0, 6)]),
            )
        )
    ]
    for copy in copies:
        copy.start()
    for copy in copies[:3]:
        copy.wait()
    tiles = counts.shape[1]
    slots = cells.shape[1]
    cap = slots // tiles
    for part in range(6):
        values[part:part + 1] = observed_in[part]
    values[6:7] = cells_in[...].astype(jnp.float32)
    owner = lax.broadcasted_iota(jnp.int32, (tiles, slots), 1) // cap
    spread = (owner == lax.broadcasted_iota(jnp.int32, (tiles, slots), 0)).astype(jnp.bfloat16)
    count = jnp.broadcast_to(counts_in[...].astype(jnp.float32), (8, tiles)).astype(jnp.bfloat16)
    repeated = lax.dot_general(count, spread, (((1,), (0,)), ((), ())), preferred_element_type=jnp.float32)
    within = lax.broadcasted_iota(jnp.int32, (8, slots), 1) % cap
    live = (within.astype(jnp.float32) < repeated).astype(jnp.float32)
    values[7:8] = live[7:8]
    columns[...] = jnp.zeros_like(columns)
    for part in range(slots // LANES):
        turned = values[:, part * LANES:(part + 1) * LANES].T
        columns[cap + part * LANES:cap + (part + 1) * LANES, 0:ROWS] = turned
    planes = [jnp.zeros((tiles, LANES), jnp.float32), jnp.zeros((tiles, LANES), jnp.float32)]
    for group in range(3):
        for slot in range(cap):
            piece = columns[pl.ds(group * cap + slot, tiles, stride=cap), :]
            shift = (group % 2) * 64 + slot * ROWS
            planes[group // 2] += pltpu.roll(piece, shift, 1) if shift else piece
    for plane in range(2):
        payload[:, plane, :] = planes[plane]
    for copy in copies[3:]:
        copy.wait()


def spread_kernel(received, out, left, right):
    tiles = received.shape[0]
    turned = []
    for plane in range(2):
        here = received[:, plane, :]
        turned.append(jnp.concatenate([here, pltpu.roll(here, LANES - ROWS, 1)], axis=0).T)
    layer = out.shape[2]
    depth = out.shape[1] - 2 * HALO
    half = depth * layer // 2
    plan = ((depth - HALO, HALO, 0), (0, depth, HALO), (0, HALO, HALO + depth))
    for group, (first, layers, where) in enumerate(plan):
        base = (group % 2) * 64
        record = jnp.concatenate(
            [turned[group // 2][base + 16 * j:base + 16 * j + ROWS] for j in range(4)], axis=1
        )
        slots = record.shape[1]
        alive = record[7:8]
        cell = record[6:7].astype(jnp.int32)
        value = jnp.where(alive > 0.0, record, 0.0)
        high = value.astype(jnp.bfloat16).astype(jnp.float32)
        rest = value - high
        middle = rest.astype(jnp.bfloat16).astype(jnp.float32)
        low = rest - middle
        row = cell // LANES
        hit = lax.broadcasted_iota(jnp.int32, (half, slots), 0) == row % half
        place = 0
        for terms, names in ((high, (0, 1, 2, 3, 4, 5, 7)), (middle, range(6)), (low, range(6))):
            for name in names:
                left[group, place:place + half] = jnp.where(hit, terms[name:name + 1], 0.0).astype(jnp.bfloat16)
                place += half
        column = cell % LANES + LANES * (row // half)
        lane = lax.broadcasted_iota(jnp.int32, (2 * LANES, slots), 0) == column
        right[group] = lane.astype(jnp.float32).astype(jnp.bfloat16)
        sums = lax.dot_general(
            left[group], right[group], (((1,), (1,)), ((), ())), preferred_element_type=jnp.float32
        )
        for name in range(7):
            total = sums[name * half:(name + 1) * half]
            if name < 6:
                total = total + sums[(7 + name) * half:(8 + name) * half]
                total = total + sums[(13 + name) * half:(14 + name) * half]
            for index in range(layers):
                side, at = divmod((first + index) * layer, half)
                out[name, where + index] = total[at:at + layer, side * LANES:(side + 1) * LANES]


PITCH = 24


def clear(buffer, layers):
    for part in range(6):
        for layer in range(layers + 1):
            buffer[part, layer * PITCH:layer * PITCH + 8] = jnp.zeros((8, LANES), jnp.float32)


def coefficients(absorbs, pq, tile, tiles):
    depth = len(absorbs) - 4 * HALO
    for layer, absorb in enumerate(absorbs):
        place = tile * depth + layer - 2 * HALO
        scale = jnp.where((place >= 0) & (place < tiles * depth), DAMPING, 0.0)
        weight = scale / (36.0 + absorb * absorb)
        pq[0, layer] = 6.0 * weight
        pq[1, layer] = absorb * weight


def first_sweep(src, pq, dst, layers):
    def step(layer, carry):
        at = pl.ds(pl.multiple_of(layer * PITCH + 8, 8), 16)
        p, q = pq[0, layer], pq[1, layer]
        for part in range(3):
            re, im = src[part, layer], src[part + 3, layer]
            dst[part, at] = p * re + q * im
            dst[part + 3, at] = p * im - q * re
        return carry

    lax.fori_loop(0, layers, step, 0, unroll=2)


def sweep(src, pq, old, new, lo, hi, emit=None):
    lane = lax.broadcasted_iota(jnp.int32, (16, LANES), 1)
    not_first, not_last = lane > 0, lane < LANES - 1

    def neighbours(part, base):
        middle = old[part, pl.ds(base, 16)]
        beside = old[part, pl.ds(base - PITCH, 16)] + old[part, pl.ds(base + PITCH, 16)]
        beside = beside + (old[part, pl.ds(base - 1, 16)] + old[part, pl.ds(base + 1, 16)])
        beside = beside + jnp.where(not_first, pltpu.roll(middle, 1, 1), 0.0)
        beside = beside + jnp.where(not_last, pltpu.roll(middle, LANES - 1, 1), 0.0)
        return middle, beside

    def step(layer, carry):
        base = layer * PITCH + 8
        p, q = pq[0, layer], pq[1, layer]
        results = []
        for part in range(3):
            mid_re, sum_re = neighbours(part, base)
            mid_im, sum_im = neighbours(part + 3, base)
            sum_re = sum_re + src[part, layer]
            sum_im = sum_im + src[part + 3, layer]
            new_re = (1.0 - DAMPING) * mid_re + (p * sum_re + q * sum_im)
            new_im = (1.0 - DAMPING) * mid_im + (p * sum_im - q * sum_re)
            if emit is None:
                at = pl.ds(pl.multiple_of(base, 8), 16)
                new[part, at] = new_re
                new[part + 3, at] = new_im
            results.append((new_re, new_im))
        if emit is not None:
            emit(layer, results)
        return carry

    lax.fori_loop(lo, hi, step, 0, unroll=hi - lo)


def relax(src, pq, one, two, emit):
    layers = src.shape[1]
    clear(one, layers)
    clear(two, layers)
    first_sweep(src, pq, one, layers)
    old, new = one, two
    for index in range(1, SWEEPS):
        final = index == SWEEPS - 1
        sweep(src, pq, old, new, index, layers - index, emit if final else None)
        old, new = new, old


def choose_kernel(own, across, out):
    out[0] = own[...]
    out[1] = across[...]


def edge_kernel(factor, own, near_edge, absorb):
    core = lax.axis_index("tile") % 2
    near_edge[...] = own[:, pl.ds(2 * (1 - core), 2)]
    absorb[...] = factor[0] * own[6]


def forward_kernel(factor, absorb, own, across, edge, other, near, near_pq, src, pq, one, two):
    depth = own.shape[1]
    tile, tiles = lax.axis_index("tile"), lax.axis_size("tile")
    even = tile % 2 == 0
    mine, theirs = other.at[0], other.at[1]
    views = [(edge, i, across, depth - 2 + i) for i in range(2)]
    views += [(theirs, i, mine, i) for i in range(depth)]
    views += [(own, i, own, i) for i in range(depth)]
    views += [(mine, i, theirs, i) for i in range(depth)]
    views += [(across, i, edge, i) for i in range(2)]
    absorbs = []
    for layer, (first, at, second, there) in enumerate(views):
        if first is second:
            src[:, layer] = first[:6, at]
            absorbs.append(absorb[at])
        else:
            src[:, layer] = jnp.where(even, first[:6, at], second[:6, there])
            absorbs.append(factor[0] * jnp.where(even, first[6, at], second[6, there]))
    coefficients(absorbs, pq, tile, tiles)
    near_pq[...] = pq[:, HALO:-HALO]

    def emit(layer, results):
        for part, (re, im) in enumerate(results):
            near[part, layer - HALO] = re
            near[part + 3, layer - HALO] = im

    relax(src, pq, one, two, emit)


def adjoint_kernel(factor, sums, near, pq, terms, field, src, one, two, left):
    depth = near.shape[1] - 2 * HALO
    copy = pltpu.make_async_copy(near.at[:, pl.ds(HALO, depth)], field.at[0], left)
    copy.start()
    for part in range(6):
        src[part] = sums[6] * near[part] - sums[part]

    def emit(layer, results):
        total = 0.0
        for part, (re, im) in enumerate(results):
            total = total + (re * near[part + 3, layer] + im * near[part, layer])
        total = factor[0] * total
        rows = pl.ds(pl.multiple_of((layer - HALO) * 16, 16), 16)
        for index in range(terms.shape[0]):
            terms[index, rows] = total

    relax(src, pq, one, two, emit)
    copy.wait()


def working(layers):
    buffer = pltpu.VMEM((6, layers * PITCH + 8, LANES), jnp.float32)
    return [pltpu.VMEM((6, layers, 16, LANES), jnp.float32), buffer, buffer]


def shape(*dims):
    return jax.ShapeDtypeStruct(dims, jnp.float32)


LIMIT = pltpu.CompilerParams(vmem_limit_bytes=16 * 2**20)


def cost(flops, size):
    return pl.CostEstimate(flops=flops, bytes_accessed=size, transcendentals=0)


def pack(source, conductivity, observed, slot_cells, block_counts):
    depth, ny, nz = conductivity.shape
    slots, tiles = slot_cells.shape[0], block_counts.shape[0]
    return pl.pallas_call(
        pack_kernel,
        out_shape=(shape(7, depth, ny, nz), shape(tiles, 2, LANES)),
        in_specs=[HBM] * 5,
        out_specs=(VMEM, VMEM),
        scratch_shapes=[
            pltpu.VMEM((6, 1, slots), jnp.float32),
            pltpu.VMEM((1, slots), jnp.int32),
            pltpu.VMEM((1, tiles), jnp.int32),
            pltpu.VMEM((ROWS, slots), jnp.float32),
            pltpu.VMEM((slots + 2 * (slots // tiles), LANES), jnp.float32),
            pltpu.SemaphoreType.DMA((5,)),
        ],
        compiler_params=LIMIT,
        cost_estimate=cost(10**6, 10**6),
        name="pack",
    )(
        *(
            pltpu.with_memory_space_constraint(x, pltpu.HBM)
            for x in (
                source,
                conductivity,
                observed.transpose(1, 0, 2),
                slot_cells.reshape(1, -1),
                block_counts.reshape(1, -1),
            )
        )
    )


def choose(own, across):
    return pl.pallas_call(
        choose_kernel,
        out_shape=shape(2, *own.shape),
        in_specs=[VMEM] * 2,
        out_specs=VMEM,
        compiler_params=LIMIT,
        cost_estimate=cost(10**10, 10**9),
        name="choose",
    )(own, across)


def edges(factor, own):
    parts, depth, ny, nz = own.shape
    return pl.pallas_call(
        edge_kernel,
        out_shape=(shape(parts, 2, ny, nz), shape(depth, ny, nz)),
        in_specs=[SMEM, VMEM],
        out_specs=(VMEM, VMEM),
        compiler_params=LIMIT,
        cost_estimate=cost(10**10, 10**9),
        name="edges",
    )(factor, own)


def forward(factor, absorb, own, across, edge, other):
    depth, ny, nz = own.shape[1:]
    wide, layers = depth + 4 * HALO, depth + 2 * HALO
    return pl.pallas_call(
        forward_kernel,
        out_shape=(shape(6, layers, ny, nz), shape(2, layers, ny, nz)),
        in_specs=[SMEM] + [VMEM] * 5,
        out_specs=(VMEM, VMEM),
        scratch_shapes=[working(wide)[0], pltpu.VMEM((2, wide, ny, nz), jnp.float32)] + working(wide)[1:],
        compiler_params=LIMIT,
        cost_estimate=cost(10**6, 10**6),
        name="forward",
    )(factor, absorb, own, across, edge, other)


def spread(received, depth, ny, nz):
    slots = received.shape[0] * received.shape[2] // (2 * ROWS)
    return pl.pallas_call(
        spread_kernel,
        out_shape=shape(7, depth + 2 * HALO, ny, nz),
        in_specs=[VMEM],
        out_specs=VMEM,
        scratch_shapes=[
            pltpu.VMEM((3, 19 * depth * ny // 2, slots), jnp.bfloat16),
            pltpu.VMEM((3, 2 * LANES, slots), jnp.bfloat16),
        ],
        compiler_params=LIMIT,
        cost_estimate=cost(10**10, 10**9),
        name="spread",
    )(received)


def adjoint(factor, sums, near, near_pq, freqs):
    layers, ny, nz = near.shape[1:]
    depth = layers - 2 * HALO
    return pl.pallas_call(
        adjoint_kernel,
        out_shape=(shape(freqs, depth * ny, nz), shape(1, 6, depth, ny, nz)),
        in_specs=[SMEM] + [VMEM] * 3,
        out_specs=(VMEM, HBM),
        scratch_shapes=working(layers) + [pltpu.SemaphoreType.DMA],
        compiler_params=LIMIT,
        cost_estimate=cost(10**7, 10**6),
        name="adjoint",
    )(factor, sums, near, near_pq)


def body(source, conductivity, freq_factor, observed, slot_cells, block_counts):
    tiles, freqs = lax.axis_size("tile"), lax.axis_size("freq")
    depth, ny, nz = conductivity.shape
    own, payload = pack(source, conductivity, observed, slot_cells, block_counts)
    chips = tiles // 2
    up = [(2 * k, 2 * k + 2) for k in range(chips - 1)]
    down = [(2 * k + 2, 2 * k) for k in range(chips - 1)]
    across = lax.ppermute(own, "tile", down + [(i + 1, j + 1) for i, j in up])
    near_edge, absorb = edges(freq_factor, own)
    edge = lax.ppermute(near_edge, "tile", up + [(i + 1, j + 1) for i, j in down])
    received = lax.all_to_all(payload, "tile", split_axis=0, concat_axis=0, tiled=True)
    chosen = choose(own, across)
    other = lax.ppermute(chosen, "tile", [(i, i ^ 1) for i in range(tiles)])
    near, near_pq = forward(freq_factor, absorb, own, across, edge, other)
    sums = spread(received, depth, ny, nz)
    terms, field = adjoint(freq_factor, sums, near, near_pq, freqs)
    terms = lax.all_to_all(terms, "freq", split_axis=0, concat_axis=0, tiled=True)
    gradient = jnp.sum(terms, axis=0).reshape(depth, ny, nz)
    return (field, gradient)


def solution(mesh):
    in_specs = (
        P(None, "tile", None, None),
        P("tile", None, None),
        P("freq"),
        P("freq", None, "tile"),
        P("tile"),
        P("tile"),
    )
    out_specs = (P("freq", None, "tile", None, None), P("tile", None, None))
    return jax.shard_map(body, mesh=mesh, in_specs=in_specs, out_specs=out_specs, check_vma=False)
```

```python
import jax
import jax.numpy as jnp
from jax import lax
from jax.experimental import pallas as pl
from jax.experimental.pallas import tpu as pltpu
from jax.sharding import PartitionSpec as P

SWEEPS = 4
DAMPING = 0.8
HALO = SWEEPS - 1
ROWS = 8
LANES = 128

VMEM = pl.BlockSpec(memory_space=pltpu.VMEM)
SMEM = pl.BlockSpec(memory_space=pltpu.SMEM)
HBM = pl.BlockSpec(memory_space=pltpu.HBM)


def pack_kernel(
    source, cond, observed, cells, counts, own, near_edge, payload,
    observed_in, cells_in, counts_in, values, columns, arrived,
):
    core = lax.axis_index("tile") % 2
    edge = pl.ds(2 * (1 - core), 2)
    copies = [
        pltpu.make_async_copy(start, end, arrived.at[i])
        for i, (start, end) in enumerate(
            (
                (observed, observed_in),
                (cells, cells_in),
                (counts, counts_in),
                (cond, own.at[6]),
                (cond.at[edge], near_edge.at[6]),
                (source, own.at[pl.ds(0, 6)]),
                (source.at[:, edge], near_edge.at[pl.ds(0, 6)]),
            )
        )
    ]
    for copy in copies:
        copy.start()
    for copy in copies[:3]:
        copy.wait()
    tiles = counts.shape[1]
    slots = cells.shape[1]
    cap = slots // tiles
    for part in range(6):
        values[part:part + 1] = observed_in[part]
    values[6:7] = cells_in[...].astype(jnp.float32)
    owner = lax.broadcasted_iota(jnp.int32, (tiles, slots), 1) // cap
    spread = (owner == lax.broadcasted_iota(jnp.int32, (tiles, slots), 0)).astype(jnp.bfloat16)
    count = jnp.broadcast_to(counts_in[...].astype(jnp.float32), (8, tiles)).astype(jnp.bfloat16)
    repeated = lax.dot_general(count, spread, (((1,), (0,)), ((), ())), preferred_element_type=jnp.float32)
    within = lax.broadcasted_iota(jnp.int32, (8, slots), 1) % cap
    live = (within.astype(jnp.float32) < repeated).astype(jnp.float32)
    values[7:8] = live[7:8]
    columns[...] = jnp.zeros_like(columns)
    for part in range(slots // LANES):
        turned = values[:, part * LANES:(part + 1) * LANES].T
        columns[cap + part * LANES:cap + (part + 1) * LANES, 0:ROWS] = turned
    planes = [jnp.zeros((tiles, LANES), jnp.float32), jnp.zeros((tiles, LANES), jnp.float32)]
    for group in range(3):
        for slot in range(cap):
            piece = columns[pl.ds(group * cap + slot, tiles, stride=cap), :]
            shift = (group % 2) * 64 + slot * ROWS
            planes[group // 2] += pltpu.roll(piece, shift, 1) if shift else piece
    for plane in range(2):
        payload[:, plane, :] = planes[plane]
    for copy in copies[3:]:
        copy.wait()


def spread_kernel(received, near, out, left, right):
    tiles = received.shape[0]
    turned = []
    for plane in range(2):
        here = received[:, plane, :]
        turned.append(jnp.concatenate([here, pltpu.roll(here, LANES - ROWS, 1)], axis=0).T)
    layer = out.shape[2]
    depth = out.shape[1] - 2 * HALO
    half = depth * layer // 2
    plan = ((depth - HALO, HALO, 0), (0, depth, HALO), (0, HALO, HALO + depth))
    for group, (first, layers, where) in enumerate(plan):
        base = (group % 2) * 64
        record = jnp.concatenate(
            [turned[group // 2][base + 16 * j:base + 16 * j + ROWS] for j in range(4)], axis=1
        )
        slots = record.shape[1]
        alive = record[7:8]
        cell = record[6:7].astype(jnp.int32)
        value = jnp.where(alive > 0.0, record, 0.0)
        high = value.astype(jnp.bfloat16).astype(jnp.float32)
        rest = value - high
        middle = rest.astype(jnp.bfloat16).astype(jnp.float32)
        low = rest - middle
        row = cell // LANES
        hit = lax.broadcasted_iota(jnp.int32, (half, slots), 0) == row % half
        place = 0
        for terms, names in ((high, (0, 1, 2, 3, 4, 5, 7)), (middle, range(6)), (low, range(6))):
            for name in names:
                left[group, place:place + half] = jnp.where(hit, terms[name:name + 1], 0.0).astype(jnp.bfloat16)
                place += half
        column = cell % LANES + LANES * (row // half)
        lane = lax.broadcasted_iota(jnp.int32, (2 * LANES, slots), 0) == column
        right[group] = lane.astype(jnp.float32).astype(jnp.bfloat16)
        sums = lax.dot_general(
            left[group], right[group], (((1,), (1,)), ((), ())), preferred_element_type=jnp.float32
        )
        for index in range(layers):
            side, at = divmod((first + index) * layer, half)
            columns = slice(side * LANES, (side + 1) * LANES)
            count = sums[6 * half + at:6 * half + at + layer, columns]
            for name in range(6):
                total = 0.0
                for part in (0, 7, 13):
                    row = (part + name) * half + at
                    total = total + sums[row:row + layer, columns]
                out[name, where + index] = count * near[name, where + index] - total


PITCH = 24


def clear(buffer, layers):
    for part in range(6):
        for layer in range(layers + 1):
            buffer[part, layer * PITCH:layer * PITCH + 8] = jnp.zeros((8, LANES), jnp.float32)


def coefficients(absorbs, pq, tile, tiles):
    depth = len(absorbs) - 4 * HALO
    for layer, absorb in enumerate(absorbs):
        place = tile * depth + layer - 2 * HALO
        scale = jnp.where((place >= 0) & (place < tiles * depth), DAMPING, 0.0)
        weight = scale / (36.0 + absorb * absorb)
        pq[0, layer] = 6.0 * weight
        pq[1, layer] = absorb * weight


def first_sweep(src, pq, dst, layers):
    def step(layer, carry):
        at = pl.ds(pl.multiple_of(layer * PITCH + 8, 8), 16)
        p, q = pq[0, layer], pq[1, layer]
        for part in range(3):
            re, im = src[part, layer], src[part + 3, layer]
            dst[part, at] = p * re + q * im
            dst[part + 3, at] = p * im - q * re
        return carry

    lax.fori_loop(0, layers, step, 0, unroll=2)


def sweep(src, pq, old, new, lo, hi, emit=None):
    lane = lax.broadcasted_iota(jnp.int32, (16, LANES), 1)
    not_first, not_last = lane > 0, lane < LANES - 1

    def neighbours(part, base):
        middle = old[part, pl.ds(base, 16)]
        beside = old[part, pl.ds(base - PITCH, 16)] + old[part, pl.ds(base + PITCH, 16)]
        beside = beside + (old[part, pl.ds(base - 1, 16)] + old[part, pl.ds(base + 1, 16)])
        beside = beside + jnp.where(not_first, pltpu.roll(middle, 1, 1), 0.0)
        beside = beside + jnp.where(not_last, pltpu.roll(middle, LANES - 1, 1), 0.0)
        return middle, beside

    def step(layer, carry):
        base = layer * PITCH + 8
        p, q = pq[0, layer], pq[1, layer]
        results = []
        for part in range(3):
            mid_re, sum_re = neighbours(part, base)
            mid_im, sum_im = neighbours(part + 3, base)
            sum_re = sum_re + src[part, layer]
            sum_im = sum_im + src[part + 3, layer]
            new_re = (1.0 - DAMPING) * mid_re + (p * sum_re + q * sum_im)
            new_im = (1.0 - DAMPING) * mid_im + (p * sum_im - q * sum_re)
            if emit is None:
                at = pl.ds(pl.multiple_of(base, 8), 16)
                new[part, at] = new_re
                new[part + 3, at] = new_im
            results.append((new_re, new_im))
        if emit is not None:
            emit(layer, results)
        return carry

    lax.fori_loop(lo, hi, step, 0, unroll=hi - lo)


def relax(src, pq, one, two, emit):
    layers = src.shape[1]
    clear(one, layers)
    clear(two, layers)
    first_sweep(src, pq, one, layers)
    old, new = one, two
    for index in range(1, SWEEPS):
        final = index == SWEEPS - 1
        sweep(src, pq, old, new, index, layers - index, emit if final else None)
        old, new = new, old


def choose_kernel(own, across, out):
    out[0] = own[...]
    out[1] = across[...]


def absorb_kernel(factor, own, absorb):
    absorb[...] = factor[0] * own[6]


def forward_kernel(factor, absorb, own, across, edge, other, near, near_pq, src, pq, one, two):
    depth = own.shape[1]
    tile, tiles = lax.axis_index("tile"), lax.axis_size("tile")
    even = tile % 2 == 0
    mine, theirs = other.at[0], other.at[1]
    views = [(edge, i, across, depth - 2 + i) for i in range(2)]
    views += [(theirs, i, mine, i) for i in range(depth)]
    views += [(own, i, own, i) for i in range(depth)]
    views += [(mine, i, theirs, i) for i in range(depth)]
    views += [(across, i, edge, i) for i in range(2)]

    def absorption(view, at):
        if view is not own:
            return factor[0] * view[6, at]
        return absorb[at]

    absorbs = []
    for layer, (first, at, second, there) in enumerate(views):
        if first is second:
            src[:, layer] = first[:6, at]
            absorbs.append(absorption(first, at))
        else:
            src[:, layer] = jnp.where(even, first[:6, at], second[:6, there])
            absorbs.append(jnp.where(even, absorption(first, at), absorption(second, there)))
    coefficients(absorbs, pq, tile, tiles)
    near_pq[...] = pq[:, HALO:-HALO]

    def emit(layer, results):
        for part, (re, im) in enumerate(results):
            near[part, layer - HALO] = re
            near[part + 3, layer - HALO] = im

    relax(src, pq, one, two, emit)


def adjoint_kernel(factor, src, near, pq, terms, field, one, two, left):
    depth = near.shape[1] - 2 * HALO
    copy = pltpu.make_async_copy(near.at[:, pl.ds(HALO, depth)], field.at[0], left)
    copy.start()

    def emit(layer, results):
        total = 0.0
        for part, (re, im) in enumerate(results):
            total = total + (re * near[part + 3, layer] + im * near[part, layer])
        total = factor[0] * total
        rows = pl.ds(pl.multiple_of((layer - HALO) * 16, 16), 16)
        for index in range(terms.shape[0]):
            terms[index, rows] = total

    relax(src, pq, one, two, emit)
    copy.wait()


def working(layers):
    buffer = pltpu.VMEM((6, layers * PITCH + 8, LANES), jnp.float32)
    return [pltpu.VMEM((6, layers, 16, LANES), jnp.float32), buffer, buffer]


def shape(*dims):
    return jax.ShapeDtypeStruct(dims, jnp.float32)


LIMIT = pltpu.CompilerParams(vmem_limit_bytes=16 * 2**20)


def cost(flops, size):
    return pl.CostEstimate(flops=flops, bytes_accessed=size, transcendentals=0)


def pack(source, conductivity, observed, slot_cells, block_counts):
    depth, ny, nz = conductivity.shape
    slots, tiles = slot_cells.shape[0], block_counts.shape[0]
    return pl.pallas_call(
        pack_kernel,
        out_shape=(shape(7, depth, ny, nz), shape(7, 2, ny, nz), shape(tiles, 2, LANES)),
        in_specs=[HBM] * 5,
        out_specs=(VMEM, VMEM, VMEM),
        scratch_shapes=[
            pltpu.VMEM((6, 1, slots), jnp.float32),
            pltpu.VMEM((1, slots), jnp.int32),
            pltpu.VMEM((1, tiles), jnp.int32),
            pltpu.VMEM((ROWS, slots), jnp.float32),
            pltpu.VMEM((slots + 2 * (slots // tiles), LANES), jnp.float32),
            pltpu.SemaphoreType.DMA((7,)),
        ],
        compiler_params=LIMIT,
        cost_estimate=cost(10**6, 10**6),
        name="pack",
    )(
        *(
            pltpu.with_memory_space_constraint(x, pltpu.HBM)
            for x in (
                source,
                conductivity,
                observed.transpose(1, 0, 2),
                slot_cells.reshape(1, -1),
                block_counts.reshape(1, -1),
            )
        )
    )


def choose(own, across):
    return pl.pallas_call(
        choose_kernel,
        out_shape=shape(2, *own.shape),
        in_specs=[VMEM] * 2,
        out_specs=VMEM,
        compiler_params=LIMIT,
        cost_estimate=cost(10**10, 10**9),
        name="choose",
    )(own, across)


def absorption(factor, own):
    parts, depth, ny, nz = own.shape
    return pl.pallas_call(
        absorb_kernel,
        out_shape=shape(depth, ny, nz),
        in_specs=[SMEM, VMEM],
        out_specs=VMEM,
        compiler_params=LIMIT,
        cost_estimate=cost(10**10, 10**9),
        name="absorb",
    )(factor, own)


def forward(factor, absorb, own, across, edge, other):
    depth, ny, nz = own.shape[1:]
    wide, layers = depth + 4 * HALO, depth + 2 * HALO
    return pl.pallas_call(
        forward_kernel,
        out_shape=(shape(6, layers, ny, nz), shape(2, layers, ny, nz)),
        in_specs=[SMEM] + [VMEM] * 5,
        out_specs=(VMEM, VMEM),
        scratch_shapes=[working(wide)[0], pltpu.VMEM((2, wide, ny, nz), jnp.float32)] + working(wide)[1:],
        compiler_params=LIMIT,
        cost_estimate=cost(10**6, 10**6),
        name="forward",
    )(factor, absorb, own, across, edge, other)


def spread(received, near):
    layers, ny, nz = near.shape[1:]
    depth = layers - 2 * HALO
    slots = received.shape[0] * received.shape[2] // (2 * ROWS)
    return pl.pallas_call(
        spread_kernel,
        out_shape=shape(*near.shape),
        in_specs=[VMEM] * 2,
        out_specs=VMEM,
        scratch_shapes=[
            pltpu.VMEM((3, 19 * depth * ny // 2, slots), jnp.bfloat16),
            pltpu.VMEM((3, 2 * LANES, slots), jnp.bfloat16),
        ],
        compiler_params=LIMIT,
        cost_estimate=cost(10**10, 10**9),
        name="spread",
    )(received, near)


def adjoint(factor, adjoint_source, near, near_pq, freqs):
    layers, ny, nz = near.shape[1:]
    depth = layers - 2 * HALO
    return pl.pallas_call(
        adjoint_kernel,
        out_shape=(shape(freqs, depth * ny, nz), shape(1, 6, depth, ny, nz)),
        in_specs=[SMEM] + [VMEM] * 3,
        out_specs=(VMEM, HBM),
        scratch_shapes=working(layers)[1:] + [pltpu.SemaphoreType.DMA],
        compiler_params=LIMIT,
        cost_estimate=cost(10**7, 10**6),
        name="adjoint",
    )(factor, adjoint_source, near, near_pq)


def body(source, conductivity, freq_factor, observed, slot_cells, block_counts):
    tiles, freqs = lax.axis_size("tile"), lax.axis_size("freq")
    depth, ny, nz = conductivity.shape
    own, near_edge, payload = pack(source, conductivity, observed, slot_cells, block_counts)
    chips = tiles // 2
    up = [(2 * k, 2 * k + 2) for k in range(chips - 1)]
    down = [(2 * k + 2, 2 * k) for k in range(chips - 1)]
    across = lax.ppermute(own, "tile", down + [(i + 1, j + 1) for i, j in up])
    edge = lax.ppermute(near_edge, "tile", up + [(i + 1, j + 1) for i, j in down])
    received = lax.all_to_all(payload, "tile", split_axis=0, concat_axis=0, tiled=True)
    chosen = choose(own, across)
    other = lax.ppermute(chosen, "tile", [(i, i ^ 1) for i in range(tiles)])
    absorb = absorption(freq_factor, own)
    near, near_pq = forward(freq_factor, absorb, own, across, edge, other)
    adjoint_source = spread(received, near)
    terms, field = adjoint(freq_factor, adjoint_source, near, near_pq, freqs)
    terms = lax.all_to_all(terms, "freq", split_axis=0, concat_axis=0, tiled=True)
    gradient = jnp.sum(terms, axis=0).reshape(depth, ny, nz)
    return (field, gradient)


def solution(mesh):
    in_specs = (
        P(None, "tile", None, None),
        P("tile", None, None),
        P("freq"),
        P("freq", None, "tile"),
        P("tile"),
        P("tile"),
    )
    out_specs = (P("freq", None, "tile", None, None), P("tile", None, None))
    return jax.shard_map(body, mesh=mesh, in_specs=in_specs, out_specs=out_specs, check_vma=False)
```

```python
import jax
import jax.numpy as jnp
from jax import lax
from jax.experimental import pallas as pl
from jax.experimental.pallas import tpu as pltpu
from jax.sharding import PartitionSpec as P

SWEEPS = 4
DAMPING = 0.8
HALO = SWEEPS - 1
ROWS = 8
LANES = 128

VMEM = pl.BlockSpec(memory_space=pltpu.VMEM)
SMEM = pl.BlockSpec(memory_space=pltpu.SMEM)
HBM = pl.BlockSpec(memory_space=pltpu.HBM)


def pack_kernel(
    source, cond, observed, cells, counts, own, near_edge, payload,
    observed_in, cells_in, counts_in, values, columns, arrived,
):
    core = lax.axis_index("tile") % 2
    edge = pl.ds(2 * (1 - core), 2)
    copies = [
        pltpu.make_async_copy(start, end, arrived.at[i])
        for i, (start, end) in enumerate(
            (
                (observed, observed_in),
                (cells, cells_in),
                (counts, counts_in),
                (cond, own.at[6]),
                (cond.at[edge], near_edge.at[6]),
                (source, own.at[pl.ds(0, 6)]),
                (source.at[:, edge], near_edge.at[pl.ds(0, 6)]),
            )
        )
    ]
    for copy in copies:
        copy.start()
    for copy in copies[:3]:
        copy.wait()
    tiles = counts.shape[1]
    slots = cells.shape[1]
    cap = slots // tiles
    for part in range(6):
        values[part:part + 1] = observed_in[part]
    values[6:7] = cells_in[...].astype(jnp.float32)
    owner = lax.broadcasted_iota(jnp.int32, (tiles, slots), 1) // cap
    spread = (owner == lax.broadcasted_iota(jnp.int32, (tiles, slots), 0)).astype(jnp.bfloat16)
    count = jnp.broadcast_to(counts_in[...].astype(jnp.float32), (8, tiles)).astype(jnp.bfloat16)
    repeated = lax.dot_general(count, spread, (((1,), (0,)), ((), ())), preferred_element_type=jnp.float32)
    within = lax.broadcasted_iota(jnp.int32, (8, slots), 1) % cap
    live = (within.astype(jnp.float32) < repeated).astype(jnp.float32)
    values[7:8] = live[7:8]
    columns[...] = jnp.zeros_like(columns)
    for part in range(slots // LANES):
        turned = values[:, part * LANES:(part + 1) * LANES].T
        columns[cap + part * LANES:cap + (part + 1) * LANES, 0:ROWS] = turned
    planes = [jnp.zeros((tiles, LANES), jnp.float32), jnp.zeros((tiles, LANES), jnp.float32)]
    for group in range(3):
        for slot in range(cap):
            piece = columns[pl.ds(group * cap + slot, tiles, stride=cap), :]
            shift = (group % 2) * 64 + slot * ROWS
            planes[group // 2] += pltpu.roll(piece, shift, 1) if shift else piece
    for plane in range(2):
        payload[:, plane, :] = planes[plane]
    for copy in copies[3:]:
        copy.wait()


def adjoint_source(received, near, out, left, right):
    tiles = received.shape[0]
    turned = []
    for plane in range(2):
        here = received[:, plane, :]
        turned.append(jnp.concatenate([here, pltpu.roll(here, LANES - ROWS, 1)], axis=0).T)
    layer = out.shape[2]
    depth = out.shape[1] - 2 * HALO
    half = depth * layer // 2
    plan = ((depth - HALO, HALO, 0), (0, depth, HALO), (0, HALO, HALO + depth))
    for group, (first, layers, where) in enumerate(plan):
        base = (group % 2) * 64
        record = jnp.concatenate(
            [turned[group // 2][base + 16 * j:base + 16 * j + ROWS] for j in range(4)], axis=1
        )
        slots = record.shape[1]
        alive = record[7:8]
        cell = record[6:7].astype(jnp.int32)
        value = jnp.where(alive > 0.0, record, 0.0)
        high = value.astype(jnp.bfloat16).astype(jnp.float32)
        rest = value - high
        middle = rest.astype(jnp.bfloat16).astype(jnp.float32)
        low = rest - middle
        row = cell // LANES
        hit = lax.broadcasted_iota(jnp.int32, (half, slots), 0) == row % half
        place = 0
        for terms, names in ((high, (0, 1, 2, 3, 4, 5, 7)), (middle, range(6)), (low, range(6))):
            for name in names:
                left[group, place:place + half] = jnp.where(hit, terms[name:name + 1], 0.0).astype(jnp.bfloat16)
                place += half
        column = cell % LANES + LANES * (row // half)
        lane = lax.broadcasted_iota(jnp.int32, (2 * LANES, slots), 0) == column
        right[group] = lane.astype(jnp.float32).astype(jnp.bfloat16)
        sums = lax.dot_general(
            left[group], right[group], (((1,), (1,)), ((), ())), preferred_element_type=jnp.float32
        )
        for index in range(layers):
            side, at = divmod((first + index) * layer, half)
            columns = slice(side * LANES, (side + 1) * LANES)
            count = sums[6 * half + at:6 * half + at + layer, columns]
            for name in range(6):
                total = 0.0
                for part in (0, 7, 13):
                    row = (part + name) * half + at
                    total = total + sums[row:row + layer, columns]
                out[name, where + index] = count * near[name, where + index] - total


PITCH = 24


def clear(buffer, layers):
    for part in range(6):
        for layer in range(layers + 1):
            buffer[part, layer * PITCH:layer * PITCH + 8] = jnp.zeros((8, LANES), jnp.float32)


def coefficients(absorbs, pq, tile, tiles):
    depth = len(absorbs) - 4 * HALO
    for layer, absorb in enumerate(absorbs):
        place = tile * depth + layer - 2 * HALO
        scale = jnp.where((place >= 0) & (place < tiles * depth), DAMPING, 0.0)
        weight = scale / (36.0 + absorb * absorb)
        pq[0, layer] = 6.0 * weight
        pq[1, layer] = absorb * weight


def first_sweep(src, pq, dst, layers):
    def step(layer, carry):
        at = pl.ds(pl.multiple_of(layer * PITCH + 8, 8), 16)
        p, q = pq[0, layer], pq[1, layer]
        for part in range(3):
            re, im = src[part, layer], src[part + 3, layer]
            dst[part, at] = p * re + q * im
            dst[part + 3, at] = p * im - q * re
        return carry

    lax.fori_loop(0, layers, step, 0, unroll=2)


def sweep(src, pq, old, new, lo, hi, emit=None):
    lane = lax.broadcasted_iota(jnp.int32, (16, LANES), 1)
    not_first, not_last = lane > 0, lane < LANES - 1

    def neighbours(part, base):
        middle = old[part, pl.ds(base, 16)]
        beside = old[part, pl.ds(base - PITCH, 16)] + old[part, pl.ds(base + PITCH, 16)]
        beside = beside + (old[part, pl.ds(base - 1, 16)] + old[part, pl.ds(base + 1, 16)])
        beside = beside + jnp.where(not_first, pltpu.roll(middle, 1, 1), 0.0)
        beside = beside + jnp.where(not_last, pltpu.roll(middle, LANES - 1, 1), 0.0)
        return middle, beside

    def step(layer, carry):
        base = layer * PITCH + 8
        p, q = pq[0, layer], pq[1, layer]
        results = []
        for part in range(3):
            mid_re, sum_re = neighbours(part, base)
            mid_im, sum_im = neighbours(part + 3, base)
            sum_re = sum_re + src[part, layer]
            sum_im = sum_im + src[part + 3, layer]
            new_re = (1.0 - DAMPING) * mid_re + (p * sum_re + q * sum_im)
            new_im = (1.0 - DAMPING) * mid_im + (p * sum_im - q * sum_re)
            if emit is None:
                at = pl.ds(pl.multiple_of(base, 8), 16)
                new[part, at] = new_re
                new[part + 3, at] = new_im
            results.append((new_re, new_im))
        if emit is not None:
            emit(layer, results)
        return carry

    lax.fori_loop(lo, hi, step, 0, unroll=hi - lo)


def relax(src, pq, one, two, emit):
    layers = src.shape[1]
    clear(one, layers)
    clear(two, layers)
    first_sweep(src, pq, one, layers)
    old, new = one, two
    for index in range(1, SWEEPS):
        final = index == SWEEPS - 1
        sweep(src, pq, old, new, index, layers - index, emit if final else None)
        old, new = new, old


def choose_kernel(own, across, out):
    core = lax.axis_index("tile") % 2
    depth = own.shape[1]
    out[:, 0:depth] = own[...]
    out[:, depth:] = across[:, pl.ds(2 * (1 - core), 2)]


def absorb_kernel(factor, own, absorb):
    absorb[...] = factor[0] * own[6]


def forward_kernel(factor, absorb, own, across, edge, other, near, near_pq, src, pq, one, two):
    depth = own.shape[1]
    tile, tiles = lax.axis_index("tile"), lax.axis_size("tile")
    even = tile % 2 == 0
    views = [(edge, i, other, depth + i) for i in range(2)]
    views += [(across, i, other, i) for i in range(depth)]
    views += [(own, i, own, i) for i in range(depth)]
    views += [(other, i, across, i) for i in range(depth)]
    views += [(other, depth + i, edge, i) for i in range(2)]

    def absorption(view, at):
        if view is own:
            return absorb[at]
        return factor[0] * view[6, at]

    absorbs = []
    for layer, (first, at, second, there) in enumerate(views):
        if first is second:
            src[:, layer] = first[:6, at]
            absorbs.append(absorption(first, at))
        else:
            src[:, layer] = jnp.where(even, first[:6, at], second[:6, there])
            absorbs.append(jnp.where(even, absorption(first, at), absorption(second, there)))
    coefficients(absorbs, pq, tile, tiles)
    near_pq[...] = pq[:, HALO:-HALO]

    def emit(layer, results):
        for part, (re, im) in enumerate(results):
            near[part, layer - HALO] = re
            near[part + 3, layer - HALO] = im

    relax(src, pq, one, two, emit)


def finish_kernel(factor, received, near, pq, terms, field, src, one, two, left, right, written):
    depth = near.shape[1] - 2 * HALO
    copy = pltpu.make_async_copy(near.at[:, pl.ds(HALO, depth)], field.at[0], written)
    copy.start()
    adjoint_source(received, near, src, left, right)

    def emit(layer, results):
        total = 0.0
        for part, (re, im) in enumerate(results):
            total = total + (re * near[part + 3, layer] + im * near[part, layer])
        total = factor[0] * total
        rows = pl.ds(pl.multiple_of((layer - HALO) * 16, 16), 16)
        for index in range(terms.shape[0]):
            terms[index, rows] = total

    relax(src, pq, one, two, emit)
    copy.wait()


def working(layers):
    buffer = pltpu.VMEM((6, layers * PITCH + 8, LANES), jnp.float32)
    return [pltpu.VMEM((6, layers, 16, LANES), jnp.float32), buffer, buffer]


def shape(*dims):
    return jax.ShapeDtypeStruct(dims, jnp.float32)


LIMIT = pltpu.CompilerParams(vmem_limit_bytes=16 * 2**20)


def cost(flops, size):
    return pl.CostEstimate(flops=flops, bytes_accessed=size, transcendentals=0)


def pack(source, conductivity, observed, slot_cells, block_counts):
    depth, ny, nz = conductivity.shape
    slots, tiles = slot_cells.shape[0], block_counts.shape[0]
    return pl.pallas_call(
        pack_kernel,
        out_shape=(shape(7, depth, ny, nz), shape(7, 2, ny, nz), shape(tiles, 2, LANES)),
        in_specs=[HBM] * 5,
        out_specs=(VMEM, VMEM, VMEM),
        scratch_shapes=[
            pltpu.VMEM((6, 1, slots), jnp.float32),
            pltpu.VMEM((1, slots), jnp.int32),
            pltpu.VMEM((1, tiles), jnp.int32),
            pltpu.VMEM((ROWS, slots), jnp.float32),
            pltpu.VMEM((slots + 2 * (slots // tiles), LANES), jnp.float32),
            pltpu.SemaphoreType.DMA((7,)),
        ],
        compiler_params=LIMIT,
        cost_estimate=cost(10**6, 10**6),
        name="pack",
    )(
        *(
            pltpu.with_memory_space_constraint(x, pltpu.HBM)
            for x in (
                source,
                conductivity,
                observed.transpose(1, 0, 2),
                slot_cells.reshape(1, -1),
                block_counts.reshape(1, -1),
            )
        )
    )


def choose(own, across):
    return pl.pallas_call(
        choose_kernel,
        out_shape=shape(own.shape[0], own.shape[1] + 2, *own.shape[2:]),
        in_specs=[VMEM] * 2,
        out_specs=VMEM,
        compiler_params=LIMIT,
        cost_estimate=cost(10**10, 10**9),
        name="choose",
    )(own, across)


def absorption(factor, own):
    parts, depth, ny, nz = own.shape
    return pl.pallas_call(
        absorb_kernel,
        out_shape=shape(depth, ny, nz),
        in_specs=[SMEM, VMEM],
        out_specs=VMEM,
        compiler_params=LIMIT,
        cost_estimate=cost(10**10, 10**9),
        name="absorb",
    )(factor, own)


def forward(factor, absorb, own, across, edge, other):
    depth, ny, nz = own.shape[1:]
    wide, layers = depth + 4 * HALO, depth + 2 * HALO
    return pl.pallas_call(
        forward_kernel,
        out_shape=(shape(6, layers, ny, nz), shape(2, layers, ny, nz)),
        in_specs=[SMEM] + [VMEM] * 5,
        out_specs=(VMEM, VMEM),
        scratch_shapes=[working(wide)[0], pltpu.VMEM((2, wide, ny, nz), jnp.float32)] + working(wide)[1:],
        compiler_params=LIMIT,
        cost_estimate=cost(10**6, 10**6),
        name="forward",
    )(factor, absorb, own, across, edge, other)


def finish(factor, received, near, near_pq, freqs):
    layers, ny, nz = near.shape[1:]
    depth = layers - 2 * HALO
    slots = received.shape[0] * received.shape[2] // (2 * ROWS)
    return pl.pallas_call(
        finish_kernel,
        out_shape=(shape(freqs, depth * ny, nz), shape(1, 6, depth, ny, nz)),
        in_specs=[SMEM] + [VMEM] * 3,
        out_specs=(VMEM, HBM),
        scratch_shapes=working(layers) + [
            pltpu.VMEM((3, 19 * depth * ny // 2, slots), jnp.bfloat16),
            pltpu.VMEM((3, 2 * LANES, slots), jnp.bfloat16),
            pltpu.SemaphoreType.DMA,
        ],
        compiler_params=LIMIT,
        cost_estimate=cost(10**10, 10**9),
        name="finish",
    )(factor, received, near, near_pq)


def body(source, conductivity, freq_factor, observed, slot_cells, block_counts):
    tiles, freqs = lax.axis_size("tile"), lax.axis_size("freq")
    depth, ny, nz = conductivity.shape
    own, near_edge, payload = pack(source, conductivity, observed, slot_cells, block_counts)
    chips = tiles // 2
    up = [(2 * k, 2 * k + 2) for k in range(chips - 1)]
    down = [(2 * k + 2, 2 * k) for k in range(chips - 1)]
    meet = [(2 * k + 1, 2 * k + 2) for k in range(chips - 1)]
    across = lax.ppermute(own, "tile", meet + [(j, i) for i, j in meet])
    edge = lax.ppermute(near_edge, "tile", up + [(i + 1, j + 1) for i, j in down])
    received = lax.all_to_all(payload, "tile", split_axis=0, concat_axis=0, tiled=True)
    chosen = choose(own, across)
    other = lax.ppermute(chosen, "tile", [(i, i ^ 1) for i in range(tiles)])
    absorb = absorption(freq_factor, own)
    near, near_pq = forward(freq_factor, absorb, own, across, edge, other)
    terms, field = finish(freq_factor, received, near, near_pq, freqs)
    terms = lax.all_to_all(terms, "freq", split_axis=0, concat_axis=0, tiled=True)
    gradient = jnp.sum(terms, axis=0).reshape(depth, ny, nz)
    return (field, gradient)


def solution(mesh):
    in_specs = (
        P(None, "tile", None, None),
        P("tile", None, None),
        P("freq"),
        P("freq", None, "tile"),
        P("tile"),
        P("tile"),
    )
    out_specs = (P("freq", None, "tile", None, None), P("tile", None, None))
    return jax.shard_map(body, mesh=mesh, in_specs=in_specs, out_specs=out_specs, check_vma=False)
```

```python
import functools

import jax
import jax.numpy as jnp
from jax import lax
from jax.experimental import pallas as pl
from jax.experimental.pallas import tpu as pltpu
from jax.sharding import PartitionSpec as P

SWEEPS = 4
DAMPING = 0.8
HALO = SWEEPS - 1
ROWS = 8
LANES = 128

VMEM = pl.BlockSpec(memory_space=pltpu.VMEM)
SMEM = pl.BlockSpec(memory_space=pltpu.SMEM)
HBM = pl.BlockSpec(memory_space=pltpu.HBM)


def pack_kernel(
    source, cond, observed, cells, counts, own, payload,
    observed_in, cells_in, counts_in, values, columns, arrived,
):
    copies = [
        pltpu.make_async_copy(start, end, arrived.at[i])
        for i, (start, end) in enumerate(
            (
                (observed, observed_in),
                (cells, cells_in),
                (counts, counts_in),
                (cond, own.at[6]),
                (source, own.at[pl.ds(0, 6)]),
            )
        )
    ]
    for copy in copies:
        copy.start()
    for copy in copies[:3]:
        copy.wait()
    tiles = counts.shape[1]
    slots = cells.shape[1]
    cap = slots // tiles
    for part in range(6):
        values[part:part + 1] = observed_in[part]
    values[6:7] = cells_in[...].astype(jnp.float32)
    owner = lax.broadcasted_iota(jnp.int32, (tiles, slots), 1) // cap
    spread = (owner == lax.broadcasted_iota(jnp.int32, (tiles, slots), 0)).astype(jnp.bfloat16)
    count = jnp.broadcast_to(counts_in[...].astype(jnp.float32), (8, tiles)).astype(jnp.bfloat16)
    repeated = lax.dot_general(count, spread, (((1,), (0,)), ((), ())), preferred_element_type=jnp.float32)
    within = lax.broadcasted_iota(jnp.int32, (8, slots), 1) % cap
    live = (within.astype(jnp.float32) < repeated).astype(jnp.float32)
    values[7:8] = live[7:8]
    columns[...] = jnp.zeros_like(columns)
    for part in range(slots // LANES):
        turned = values[:, part * LANES:(part + 1) * LANES].T
        columns[cap + part * LANES:cap + (part + 1) * LANES, 0:ROWS] = turned
    planes = [jnp.zeros((tiles, LANES), jnp.float32), jnp.zeros((tiles, LANES), jnp.float32)]
    for group in range(3):
        for slot in range(cap):
            piece = columns[pl.ds(group * cap + slot, tiles, stride=cap), :]
            shift = (group % 2) * 64 + slot * ROWS
            planes[group // 2] += pltpu.roll(piece, shift, 1) if shift else piece
    for plane in range(2):
        payload[:, plane, :] = planes[plane]
    for copy in copies[3:]:
        copy.wait()


def adjoint_source(received, near, out, left, right):
    tiles = received.shape[0]
    turned = []
    for plane in range(2):
        here = received[:, plane, :]
        turned.append(jnp.concatenate([here, pltpu.roll(here, LANES - ROWS, 1)], axis=0).T)
    layer = out.shape[2]
    depth = out.shape[1] - 2 * HALO
    half = depth * layer // 2
    plan = ((depth - HALO, HALO, 0), (0, depth, HALO), (0, HALO, HALO + depth))
    for group, (first, layers, where) in enumerate(plan):
        base = (group % 2) * 64
        record = jnp.concatenate(
            [turned[group // 2][base + 16 * j:base + 16 * j + ROWS] for j in range(4)], axis=1
        )
        slots = record.shape[1]
        alive = record[7:8]
        cell = record[6:7].astype(jnp.int32)
        value = jnp.where(alive > 0.0, record, 0.0)
        high = value.astype(jnp.bfloat16).astype(jnp.float32)
        rest = value - high
        middle = rest.astype(jnp.bfloat16).astype(jnp.float32)
        low = rest - middle
        row = cell // LANES
        hit = lax.broadcasted_iota(jnp.int32, (half, slots), 0) == row % half
        place = 0
        for terms, names in ((high, (0, 1, 2, 3, 4, 5, 7)), (middle, range(6)), (low, range(6))):
            for name in names:
                left[group, place:place + half] = jnp.where(hit, terms[name:name + 1], 0.0).astype(jnp.bfloat16)
                place += half
        column = cell % LANES + LANES * (row // half)
        lane = lax.broadcasted_iota(jnp.int32, (2 * LANES, slots), 0) == column
        right[group] = lane.astype(jnp.float32).astype(jnp.bfloat16)
        sums = lax.dot_general(
            left[group], right[group], (((1,), (1,)), ((), ())), preferred_element_type=jnp.float32
        )
        for index in range(layers):
            side, at = divmod((first + index) * layer, half)
            columns = slice(side * LANES, (side + 1) * LANES)
            count = sums[6 * half + at:6 * half + at + layer, columns]
            for name in range(6):
                total = 0.0
                for part in (0, 7, 13):
                    row = (part + name) * half + at
                    total = total + sums[row:row + layer, columns]
                out[name, where + index] = count * near[name, where + index] - total


CUT = 3
PITCH = 24


def clear(buffer, layers):
    for part in range(6):
        for layer in range(layers + 1):
            buffer[part, layer * PITCH:layer * PITCH + 8] = jnp.zeros((8, LANES), jnp.float32)


def damping_kernel(out, depth, tiles):
    tile = lax.axis_index("tile")
    for layer in range(out.shape[0]):
        place = tile * depth + layer - 2 * HALO
        scale = jnp.where((place >= 0) & (place < tiles * depth), DAMPING, 0.0)
        out[layer] = jnp.full(out.shape[1:], scale, jnp.float32)


def coefficients(absorbs, damping, pq):
    for layer, absorb in enumerate(absorbs):
        weight = damping[layer] / (36.0 + absorb * absorb)
        pq[0, layer] = 6.0 * weight
        pq[1, layer] = absorb * weight


def first_sweep(src, pq, dst, layers):
    def step(layer, carry):
        at = pl.ds(pl.multiple_of(layer * PITCH + 8, 8), 16)
        p, q = pq[0, layer], pq[1, layer]
        for part in range(3):
            re, im = src[part, layer], src[part + 3, layer]
            dst[part, at] = p * re + q * im
            dst[part + 3, at] = p * im - q * re
        return carry

    lax.fori_loop(0, layers, step, 0, unroll=2)


def sweep(src, pq, old, new, lo, hi, emit=None):
    lane = lax.broadcasted_iota(jnp.int32, (16, LANES), 1)
    not_first, not_last = lane > 0, lane < LANES - 1

    def neighbours(part, base):
        middle = old[part, pl.ds(base, 16)]
        beside = old[part, pl.ds(base - PITCH, 16)] + old[part, pl.ds(base + PITCH, 16)]
        beside = beside + (old[part, pl.ds(base - 1, 16)] + old[part, pl.ds(base + 1, 16)])
        beside = beside + jnp.where(not_first, pltpu.roll(middle, 1, 1), 0.0)
        beside = beside + jnp.where(not_last, pltpu.roll(middle, LANES - 1, 1), 0.0)
        return middle, beside

    def step(layer, carry):
        base = layer * PITCH + 8
        p, q = pq[0, layer], pq[1, layer]
        results = []
        for part in range(3):
            mid_re, sum_re = neighbours(part, base)
            mid_im, sum_im = neighbours(part + 3, base)
            sum_re = sum_re + src[part, layer]
            sum_im = sum_im + src[part + 3, layer]
            new_re = (1.0 - DAMPING) * mid_re + (p * sum_re + q * sum_im)
            new_im = (1.0 - DAMPING) * mid_im + (p * sum_im - q * sum_re)
            if emit is None:
                at = pl.ds(pl.multiple_of(base, 8), 16)
                new[part, at] = new_re
                new[part + 3, at] = new_im
            results.append((new_re, new_im))
        if emit is not None:
            emit(layer, results)
        return carry

    lax.fori_loop(lo, hi, step, 0, unroll=hi - lo)


def relax(src, pq, one, two, emit):
    layers = src.shape[1]
    clear(one, layers)
    clear(two, layers)
    first_sweep(src, pq, one, layers)
    old, new = one, two
    for index in range(1, SWEEPS):
        final = index == SWEEPS - 1
        sweep(src, pq, old, new, index, layers - index, emit if final else None)
        old, new = new, old


def parity_kernel(out):
    out[...] = jnp.full(out.shape, (1 - lax.axis_index("tile") % 2).astype(jnp.float32))


def edge_kernel(own, parity, out):
    even = jnp.concatenate([parity[...], parity[...]], axis=0) > 0.0
    out[...] = jnp.where(even, own[:, 2:4], own[:, 0:2])


def choose_kernel(own, early, late, out, across):
    core = lax.axis_index("tile") % 2
    depth = own.shape[1]
    across[...] = early[...] + late[...]
    out[:, 0:depth] = own[...]
    out[:, depth:] = across[:, pl.ds(2 * (1 - core), 2)]


def forward_kernel(factor, damping, own, across, edge, other, near, near_pq, src, pq, one, two):
    depth = own.shape[1]
    even = lax.axis_index("tile") % 2 == 0
    views = [(edge, i, other, depth + i) for i in range(2)]
    views += [(across, i, other, i) for i in range(depth)]
    views += [(own, i, own, i) for i in range(depth)]
    views += [(other, i, across, i) for i in range(depth)]
    views += [(other, depth + i, edge, i) for i in range(2)]

    absorbs = []
    for layer, (first, at, second, there) in enumerate(views):
        if first is second:
            src[:, layer] = first[:6, at]
            absorbs.append(factor[0] * first[6, at])
        else:
            src[:, layer] = jnp.where(even, first[:6, at], second[:6, there])
            absorbs.append(factor[0] * jnp.where(even, first[6, at], second[6, there]))
    coefficients(absorbs, damping, pq)
    near_pq[...] = pq[:, HALO:-HALO]

    def emit(layer, results):
        for part, (re, im) in enumerate(results):
            near[part, layer - HALO] = re
            near[part + 3, layer - HALO] = im

    relax(src, pq, one, two, emit)


def finish_kernel(factor, received, near, pq, terms, field, src, one, two, left, right, written):
    depth = near.shape[1] - 2 * HALO
    copy = pltpu.make_async_copy(near.at[:, pl.ds(HALO, depth)], field.at[0], written)
    copy.start()
    adjoint_source(received, near, src, left, right)

    def emit(layer, results):
        total = 0.0
        for part, (re, im) in enumerate(results):
            total = total + (re * near[part + 3, layer] + im * near[part, layer])
        total = factor[0] * total
        rows = pl.ds(pl.multiple_of((layer - HALO) * 16, 16), 16)
        for index in range(terms.shape[0]):
            terms[index, rows] = total

    relax(src, pq, one, two, emit)
    copy.wait()


def working(layers):
    buffer = pltpu.VMEM((6, layers * PITCH + 8, LANES), jnp.float32)
    return [pltpu.VMEM((6, layers, 16, LANES), jnp.float32), buffer, buffer]


def shape(*dims):
    return jax.ShapeDtypeStruct(dims, jnp.float32)


LIMIT = pltpu.CompilerParams(vmem_limit_bytes=16 * 2**20)


def cost(flops, size):
    return pl.CostEstimate(flops=flops, bytes_accessed=size, transcendentals=0)


def pack(source, conductivity, observed, slot_cells, block_counts):
    depth, ny, nz = conductivity.shape
    slots, tiles = slot_cells.shape[0], block_counts.shape[0]
    return pl.pallas_call(
        pack_kernel,
        out_shape=(shape(7, depth, ny, nz), shape(tiles, 2, LANES)),
        in_specs=[HBM] * 5,
        out_specs=(VMEM, VMEM),
        scratch_shapes=[
            pltpu.VMEM((6, 1, slots), jnp.float32),
            pltpu.VMEM((1, slots), jnp.int32),
            pltpu.VMEM((1, tiles), jnp.int32),
            pltpu.VMEM((ROWS, slots), jnp.float32),
            pltpu.VMEM((slots + 2 * (slots // tiles), LANES), jnp.float32),
            pltpu.SemaphoreType.DMA((5,)),
        ],
        compiler_params=LIMIT,
        cost_estimate=cost(10**6, 10**6),
        name="pack",
    )(
        *(
            pltpu.with_memory_space_constraint(x, pltpu.HBM)
            for x in (
                source,
                conductivity,
                observed.transpose(1, 0, 2),
                slot_cells.reshape(1, -1),
                block_counts.reshape(1, -1),
            )
        )
    )


def edges(own):
    parts, depth, ny, nz = own.shape
    parity = pl.pallas_call(
        parity_kernel,
        out_shape=shape(8, LANES),
        out_specs=VMEM,
        compiler_params=LIMIT,
        cost_estimate=cost(10**3, 10**3),
        name="parity",
    )()
    return pl.pallas_call(
        edge_kernel,
        out_shape=shape(parts, 2, ny, nz),
        in_specs=[VMEM] * 2,
        out_specs=VMEM,
        compiler_params=LIMIT,
        cost_estimate=cost(10**10, 10**9),
        name="edges",
    )(own, parity)


def choose(own, early, late):
    parts, depth, ny, nz = own.shape
    return pl.pallas_call(
        choose_kernel,
        out_shape=(shape(parts, depth + 2, ny, nz), shape(*own.shape)),
        in_specs=[VMEM] * 3,
        out_specs=(VMEM, VMEM),
        compiler_params=LIMIT,
        cost_estimate=cost(10**10, 10**9),
        name="choose",
    )(own, early, late)


def layer_damping(depth, ny, nz, tiles):
    return pl.pallas_call(
        functools.partial(damping_kernel, depth=depth, tiles=tiles),
        out_shape=shape(depth + 4 * HALO, ny, nz),
        out_specs=VMEM,
        compiler_params=LIMIT,
        cost_estimate=cost(10**10, 10**9),
        name="damping",
    )()


def forward(factor, damping, own, across, edge, other):
    depth, ny, nz = own.shape[1:]
    wide, layers = depth + 4 * HALO, depth + 2 * HALO
    return pl.pallas_call(
        forward_kernel,
        out_shape=(shape(6, layers, ny, nz), shape(2, layers, ny, nz)),
        in_specs=[SMEM] + [VMEM] * 5,
        out_specs=(VMEM, VMEM),
        scratch_shapes=[working(wide)[0], pltpu.VMEM((2, wide, ny, nz), jnp.float32)] + working(wide)[1:],
        compiler_params=LIMIT,
        cost_estimate=cost(10**6, 10**6),
        name="forward",
    )(factor, damping, own, across, edge, other)


def finish(factor, received, near, near_pq, freqs):
    layers, ny, nz = near.shape[1:]
    depth = layers - 2 * HALO
    slots = received.shape[0] * received.shape[2] // (2 * ROWS)
    return pl.pallas_call(
        finish_kernel,
        out_shape=(shape(freqs, depth * ny, nz), shape(1, 6, depth, ny, nz)),
        in_specs=[SMEM] + [VMEM] * 3,
        out_specs=(VMEM, HBM),
        scratch_shapes=working(layers) + [
            pltpu.VMEM((3, 19 * depth * ny // 2, slots), jnp.bfloat16),
            pltpu.VMEM((3, 2 * LANES, slots), jnp.bfloat16),
            pltpu.SemaphoreType.DMA,
        ],
        compiler_params=LIMIT,
        cost_estimate=cost(10**10, 10**9),
        name="finish",
    )(factor, received, near, near_pq)


def body(source, conductivity, freq_factor, observed, slot_cells, block_counts):
    tiles, freqs = lax.axis_size("tile"), lax.axis_size("freq")
    depth, ny, nz = conductivity.shape
    own, payload = pack(source, conductivity, observed, slot_cells, block_counts)
    chips = tiles // 2
    up = [(2 * k, 2 * k + 2) for k in range(chips - 1)]
    down = [(2 * k + 2, 2 * k) for k in range(chips - 1)]
    meet = [(2 * k + 1, 2 * k + 2) for k in range(chips - 1)]
    cut = CUT * tiles // 8
    early = [(i, j) for i, j in meet if j < cut]
    late = [(i, j) for i, j in meet if j >= cut]
    across_early = lax.ppermute(own, "tile", early + [(j, i) for i, j in early])
    payload, across_early, own = lax.optimization_barrier((payload, across_early, own))
    received = lax.all_to_all(payload, "tile", split_axis=0, concat_axis=0, tiled=True)
    across_late = lax.ppermute(own, "tile", late + [(j, i) for i, j in late])
    edge = lax.ppermute(edges(own), "tile", up + [(i + 1, j + 1) for i, j in down])
    chosen, across = choose(own, across_early, across_late)
    other = lax.ppermute(chosen, "tile", [(i, i ^ 1) for i in range(tiles)])
    damping = layer_damping(depth, ny, nz, tiles)
    near, near_pq = forward(freq_factor, damping, own, across, edge, other)
    terms, field = finish(freq_factor, received, near, near_pq, freqs)
    terms = lax.all_to_all(terms, "freq", split_axis=0, concat_axis=0, tiled=True)
    gradient = jnp.sum(terms, axis=0).reshape(depth, ny, nz)
    return (field, gradient)


def solution(mesh):
    in_specs = (
        P(None, "tile", None, None),
        P("tile", None, None),
        P("freq"),
        P("freq", None, "tile"),
        P("tile"),
        P("tile"),
    )
    out_specs = (P("freq", None, "tile", None, None), P("tile", None, None))
    return jax.shard_map(body, mesh=mesh, in_specs=in_specs, out_specs=out_specs, check_vma=False)
```

```python
import functools

import jax
import jax.numpy as jnp
from jax import lax
from jax.experimental import pallas as pl
from jax.experimental.pallas import tpu as pltpu
from jax.sharding import PartitionSpec as P

SWEEPS = 4
DAMPING = 0.8
HALO = SWEEPS - 1
ROWS = 8
LANES = 128

VMEM = pl.BlockSpec(memory_space=pltpu.VMEM)
SMEM = pl.BlockSpec(memory_space=pltpu.SMEM)
HBM = pl.BlockSpec(memory_space=pltpu.HBM)


def pack_kernel(
    source, cond, observed, cells, counts, own, near_edge, payload,
    observed_in, cells_in, counts_in, values, columns, arrived,
):
    core = lax.axis_index("tile") % 2
    edge = pl.ds(2 * (1 - core), 2)
    copies = [
        pltpu.make_async_copy(start, end, arrived.at[i])
        for i, (start, end) in enumerate(
            (
                (observed, observed_in),
                (cells, cells_in),
                (counts, counts_in),
                (cond, own.at[6]),
                (cond.at[edge], near_edge.at[6]),
                (source, own.at[pl.ds(0, 6)]),
                (source.at[:, edge], near_edge.at[pl.ds(0, 6)]),
            )
        )
    ]
    for copy in copies:
        copy.start()
    for copy in copies[:3]:
        copy.wait()
    tiles = counts.shape[1]
    slots = cells.shape[1]
    cap = slots // tiles
    for part in range(6):
        values[part:part + 1] = observed_in[part]
    values[6:7] = cells_in[...].astype(jnp.float32)
    owner = lax.broadcasted_iota(jnp.int32, (tiles, slots), 1) // cap
    spread = (owner == lax.broadcasted_iota(jnp.int32, (tiles, slots), 0)).astype(jnp.bfloat16)
    count = jnp.broadcast_to(counts_in[...].astype(jnp.float32), (8, tiles)).astype(jnp.bfloat16)
    repeated = lax.dot_general(count, spread, (((1,), (0,)), ((), ())), preferred_element_type=jnp.float32)
    within = lax.broadcasted_iota(jnp.int32, (8, slots), 1) % cap
    live = (within.astype(jnp.float32) < repeated).astype(jnp.float32)
    values[7:8] = live[7:8]
    columns[...] = jnp.zeros_like(columns)
    for part in range(slots // LANES):
        turned = values[:, part * LANES:(part + 1) * LANES].T
        columns[cap + part * LANES:cap + (part + 1) * LANES, 0:ROWS] = turned
    planes = [jnp.zeros((tiles, LANES), jnp.float32), jnp.zeros((tiles, LANES), jnp.float32)]
    for group in range(3):
        for slot in range(cap):
            piece = columns[pl.ds(group * cap + slot, tiles, stride=cap), :]
            shift = (group % 2) * 64 + slot * ROWS
            planes[group // 2] += pltpu.roll(piece, shift, 1) if shift else piece
    for plane in range(2):
        payload[:, plane, :] = planes[plane]
    for copy in copies[3:]:
        copy.wait()


def adjoint_source(received, near, out, left, right):
    tiles = received.shape[0]
    turned = []
    for plane in range(2):
        here = received[:, plane, :]
        turned.append(jnp.concatenate([here, pltpu.roll(here, LANES - ROWS, 1)], axis=0).T)
    layer = out.shape[2]
    depth = out.shape[1] - 2 * HALO
    half = depth * layer // 2
    plan = ((depth - HALO, HALO, 0), (0, depth, HALO), (0, HALO, HALO + depth))
    for group, (first, layers, where) in enumerate(plan):
        base = (group % 2) * 64
        record = jnp.concatenate(
            [turned[group // 2][base + 16 * j:base + 16 * j + ROWS] for j in range(4)], axis=1
        )
        slots = record.shape[1]
        alive = record[7:8]
        cell = record[6:7].astype(jnp.int32)
        value = jnp.where(alive > 0.0, record, 0.0)
        high = value.astype(jnp.bfloat16).astype(jnp.float32)
        rest = value - high
        middle = rest.astype(jnp.bfloat16).astype(jnp.float32)
        low = rest - middle
        row = cell // LANES
        hit = lax.broadcasted_iota(jnp.int32, (half, slots), 0) == row % half
        place = 0
        for terms, names in ((high, (0, 1, 2, 3, 4, 5, 7)), (middle, range(6)), (low, range(6))):
            for name in names:
                left[group, place:place + half] = jnp.where(hit, terms[name:name + 1], 0.0).astype(jnp.bfloat16)
                place += half
        column = cell % LANES + LANES * (row // half)
        lane = lax.broadcasted_iota(jnp.int32, (2 * LANES, slots), 0) == column
        right[group] = lane.astype(jnp.float32).astype(jnp.bfloat16)
        sums = lax.dot_general(
            left[group], right[group], (((1,), (1,)), ((), ())), preferred_element_type=jnp.float32
        )
        for index in range(layers):
            side, at = divmod((first + index) * layer, half)
            columns = slice(side * LANES, (side + 1) * LANES)
            count = sums[6 * half + at:6 * half + at + layer, columns]
            for name in range(6):
                total = 0.0
                for part in (0, 7, 13):
                    row = (part + name) * half + at
                    total = total + sums[row:row + layer, columns]
                out[name, where + index] = count * near[name, where + index] - total


PITCH = 24


def clear(buffer, layers):
    for part in range(6):
        for layer in range(layers + 1):
            buffer[part, layer * PITCH:layer * PITCH + 8] = jnp.zeros((8, LANES), jnp.float32)


def damping_kernel(out, depth, tiles):
    tile = lax.axis_index("tile")
    for layer in range(out.shape[0]):
        place = tile * depth + layer - 2 * HALO
        scale = jnp.where((place >= 0) & (place < tiles * depth), DAMPING, 0.0)
        out[layer] = jnp.full(out.shape[1:], scale, jnp.float32)


def coefficients(absorbs, damping, pq):
    for layer, absorb in enumerate(absorbs):
        weight = damping[layer] / (36.0 + absorb * absorb)
        pq[0, layer] = 6.0 * weight
        pq[1, layer] = absorb * weight


def first_sweep(src, pq, dst, layers):
    def step(layer, carry):
        at = pl.ds(pl.multiple_of(layer * PITCH + 8, 8), 16)
        p, q = pq[0, layer], pq[1, layer]
        for part in range(3):
            re, im = src[part, layer], src[part + 3, layer]
            dst[part, at] = p * re + q * im
            dst[part + 3, at] = p * im - q * re
        return carry

    lax.fori_loop(0, layers, step, 0, unroll=2)


def sweep(src, pq, old, new, lo, hi, emit=None):
    lane = lax.broadcasted_iota(jnp.int32, (16, LANES), 1)
    not_first, not_last = lane > 0, lane < LANES - 1

    def neighbours(part, base):
        middle = old[part, pl.ds(base, 16)]
        beside = old[part, pl.ds(base - PITCH, 16)] + old[part, pl.ds(base + PITCH, 16)]
        beside = beside + (old[part, pl.ds(base - 1, 16)] + old[part, pl.ds(base + 1, 16)])
        beside = beside + jnp.where(not_first, pltpu.roll(middle, 1, 1), 0.0)
        beside = beside + jnp.where(not_last, pltpu.roll(middle, LANES - 1, 1), 0.0)
        return middle, beside

    def step(layer, carry):
        base = layer * PITCH + 8
        p, q = pq[0, layer], pq[1, layer]
        results = []
        for part in range(3):
            mid_re, sum_re = neighbours(part, base)
            mid_im, sum_im = neighbours(part + 3, base)
            sum_re = sum_re + src[part, layer]
            sum_im = sum_im + src[part + 3, layer]
            new_re = (1.0 - DAMPING) * mid_re + (p * sum_re + q * sum_im)
            new_im = (1.0 - DAMPING) * mid_im + (p * sum_im - q * sum_re)
            if emit is None:
                at = pl.ds(pl.multiple_of(base, 8), 16)
                new[part, at] = new_re
                new[part + 3, at] = new_im
            results.append((new_re, new_im))
        if emit is not None:
            emit(layer, results)
        return carry

    lax.fori_loop(lo, hi, step, 0, unroll=hi - lo)


def relax(src, pq, one, two, emit):
    layers = src.shape[1]
    clear(one, layers)
    clear(two, layers)
    first_sweep(src, pq, one, layers)
    old, new = one, two
    for index in range(1, SWEEPS):
        final = index == SWEEPS - 1
        sweep(src, pq, old, new, index, layers - index, emit if final else None)
        old, new = new, old


def choose_kernel(own, across, out):
    core = lax.axis_index("tile") % 2
    depth = own.shape[1]
    out[:, 0:depth] = own[...]
    out[:, depth:] = across[:, pl.ds(2 * (1 - core), 2)]


def forward_kernel(factor, damping, own, across, edge, other, near, near_pq, src, pq, one, two):
    depth = own.shape[1]
    even = lax.axis_index("tile") % 2 == 0
    views = [(edge, i, other, depth + i) for i in range(2)]
    views += [(across, i, other, i) for i in range(depth)]
    views += [(own, i, own, i) for i in range(depth)]
    views += [(other, i, across, i) for i in range(depth)]
    views += [(other, depth + i, edge, i) for i in range(2)]

    absorbs = []
    for layer, (first, at, second, there) in enumerate(views):
        if first is second:
            src[:, layer] = first[:6, at]
            absorbs.append(factor[0] * first[6, at])
        else:
            src[:, layer] = jnp.where(even, first[:6, at], second[:6, there])
            absorbs.append(factor[0] * jnp.where(even, first[6, at], second[6, there]))
    coefficients(absorbs, damping, pq)
    near_pq[...] = pq[:, HALO:-HALO]

    def emit(layer, results):
        for part, (re, im) in enumerate(results):
            near[part, layer - HALO] = re
            near[part + 3, layer - HALO] = im

    relax(src, pq, one, two, emit)


def finish_kernel(factor, received, near, pq, terms, field, src, one, two, left, right, written):
    depth = near.shape[1] - 2 * HALO
    copy = pltpu.make_async_copy(near.at[:, pl.ds(HALO, depth)], field.at[0], written)
    copy.start()
    adjoint_source(received, near, src, left, right)

    def emit(layer, results):
        total = 0.0
        for part, (re, im) in enumerate(results):
            total = total + (re * near[part + 3, layer] + im * near[part, layer])
        total = factor[0] * total
        rows = pl.ds(pl.multiple_of((layer - HALO) * 16, 16), 16)
        for index in range(terms.shape[0]):
            terms[index, rows] = total

    relax(src, pq, one, two, emit)
    copy.wait()


def working(layers):
    buffer = pltpu.VMEM((6, layers * PITCH + 8, LANES), jnp.float32)
    return [pltpu.VMEM((6, layers, 16, LANES), jnp.float32), buffer, buffer]


def shape(*dims):
    return jax.ShapeDtypeStruct(dims, jnp.float32)


LIMIT = pltpu.CompilerParams(vmem_limit_bytes=16 * 2**20)


def cost(flops, size):
    return pl.CostEstimate(flops=flops, bytes_accessed=size, transcendentals=0)


def pack(source, conductivity, observed, slot_cells, block_counts):
    depth, ny, nz = conductivity.shape
    slots, tiles = slot_cells.shape[0], block_counts.shape[0]
    return pl.pallas_call(
        pack_kernel,
        out_shape=(shape(7, depth, ny, nz), shape(7, 2, ny, nz), shape(tiles, 2, LANES)),
        in_specs=[HBM] * 5,
        out_specs=(VMEM, VMEM, VMEM),
        scratch_shapes=[
            pltpu.VMEM((6, 1, slots), jnp.float32),
            pltpu.VMEM((1, slots), jnp.int32),
            pltpu.VMEM((1, tiles), jnp.int32),
            pltpu.VMEM((ROWS, slots), jnp.float32),
            pltpu.VMEM((slots + 2 * (slots // tiles), LANES), jnp.float32),
            pltpu.SemaphoreType.DMA((7,)),
        ],
        compiler_params=LIMIT,
        cost_estimate=cost(10**6, 10**6),
        name="pack",
    )(
        *(
            pltpu.with_memory_space_constraint(x, pltpu.HBM)
            for x in (
                source,
                conductivity,
                observed.transpose(1, 0, 2),
                slot_cells.reshape(1, -1),
                block_counts.reshape(1, -1),
            )
        )
    )


def choose(own, across):
    return pl.pallas_call(
        choose_kernel,
        out_shape=shape(own.shape[0], own.shape[1] + 2, *own.shape[2:]),
        in_specs=[VMEM] * 2,
        out_specs=VMEM,
        compiler_params=LIMIT,
        cost_estimate=cost(10**10, 10**9),
        name="choose",
    )(own, across)


def layer_damping(depth, ny, nz, tiles):
    return pl.pallas_call(
        functools.partial(damping_kernel, depth=depth, tiles=tiles),
        out_shape=shape(depth + 4 * HALO, ny, nz),
        out_specs=VMEM,
        compiler_params=LIMIT,
        cost_estimate=cost(10**10, 10**9),
        name="damping",
    )()


def forward(factor, damping, own, across, edge, other):
    depth, ny, nz = own.shape[1:]
    wide, layers = depth + 4 * HALO, depth + 2 * HALO
    return pl.pallas_call(
        forward_kernel,
        out_shape=(shape(6, layers, ny, nz), shape(2, layers, ny, nz)),
        in_specs=[SMEM] + [VMEM] * 5,
        out_specs=(VMEM, VMEM),
        scratch_shapes=[working(wide)[0], pltpu.VMEM((2, wide, ny, nz), jnp.float32)] + working(wide)[1:],
        compiler_params=LIMIT,
        cost_estimate=cost(10**6, 10**6),
        name="forward",
    )(factor, damping, own, across, edge, other)


def finish(factor, received, near, near_pq, freqs):
    layers, ny, nz = near.shape[1:]
    depth = layers - 2 * HALO
    slots = received.shape[0] * received.shape[2] // (2 * ROWS)
    return pl.pallas_call(
        finish_kernel,
        out_shape=(shape(freqs, depth * ny, nz), shape(1, 6, depth, ny, nz)),
        in_specs=[SMEM] + [VMEM] * 3,
        out_specs=(VMEM, HBM),
        scratch_shapes=working(layers) + [
            pltpu.VMEM((3, 19 * depth * ny // 2, slots), jnp.bfloat16),
            pltpu.VMEM((3, 2 * LANES, slots), jnp.bfloat16),
            pltpu.SemaphoreType.DMA,
        ],
        compiler_params=LIMIT,
        cost_estimate=cost(10**10, 10**9),
        name="finish",
    )(factor, received, near, near_pq)


def body(source, conductivity, freq_factor, observed, slot_cells, block_counts):
    tiles, freqs = lax.axis_size("tile"), lax.axis_size("freq")
    depth, ny, nz = conductivity.shape
    own, near_edge, payload = pack(source, conductivity, observed, slot_cells, block_counts)
    chips = tiles // 2
    up = [(2 * k, 2 * k + 2) for k in range(chips - 1)]
    down = [(2 * k + 2, 2 * k) for k in range(chips - 1)]
    meet = [(2 * k + 1, 2 * k + 2) for k in range(chips - 1)]
    across = lax.ppermute(own, "tile", meet + [(j, i) for i, j in meet])
    edge = lax.ppermute(near_edge, "tile", up + [(i + 1, j + 1) for i, j in down])
    received = lax.all_to_all(payload, "tile", split_axis=0, concat_axis=0, tiled=True)
    chosen = choose(own, across)
    other = lax.ppermute(chosen, "tile", [(i, i ^ 1) for i in range(tiles)])
    damping = layer_damping(depth, ny, nz, tiles)
    near, near_pq = forward(freq_factor, damping, own, across, edge, other)
    terms, field = finish(freq_factor, received, near, near_pq, freqs)
    terms = lax.all_to_all(terms, "freq", split_axis=0, concat_axis=0, tiled=True)
    gradient = jnp.sum(terms, axis=0).reshape(depth, ny, nz)
    return (field, gradient)


def solution(mesh):
    in_specs = (
        P(None, "tile", None, None),
        P("tile", None, None),
        P("freq"),
        P("freq", None, "tile"),
        P("tile"),
        P("tile"),
    )
    out_specs = (P("freq", None, "tile", None, None), P("tile", None, None))
    return jax.shard_map(body, mesh=mesh, in_specs=in_specs, out_specs=out_specs, check_vma=False)
```

```python
import functools

import jax
import jax.numpy as jnp
from jax import lax
from jax.experimental import pallas as pl
from jax.experimental.pallas import tpu as pltpu
from jax.sharding import PartitionSpec as P

SWEEPS = 4
DAMPING = 0.8
HALO = SWEEPS - 1
ROWS = 8
LANES = 128

VMEM = pl.BlockSpec(memory_space=pltpu.VMEM)
SMEM = pl.BlockSpec(memory_space=pltpu.SMEM)
HBM = pl.BlockSpec(memory_space=pltpu.HBM)


def pack_kernel(
    source, cond, observed, cells, counts, own, near_edge, payload,
    observed_in, cells_in, counts_in, values, columns, arrived,
):
    core = lax.axis_index("tile") % 2
    edge = pl.ds(2 * (1 - core), 2)
    copies = [
        pltpu.make_async_copy(start, end, arrived.at[i])
        for i, (start, end) in enumerate(
            (
                (observed, observed_in),
                (cells, cells_in),
                (counts, counts_in),
                (cond, own.at[6]),
                (cond.at[edge], near_edge.at[6]),
                (source, own.at[pl.ds(0, 6)]),
                (source.at[:, edge], near_edge.at[pl.ds(0, 6)]),
            )
        )
    ]
    for copy in copies:
        copy.start()
    for copy in copies[:3]:
        copy.wait()
    tiles = counts.shape[1]
    slots = cells.shape[1]
    cap = slots // tiles
    for part in range(6):
        values[part:part + 1] = observed_in[part]
    values[6:7] = cells_in[...].astype(jnp.float32)
    owner = lax.broadcasted_iota(jnp.int32, (tiles, slots), 1) // cap
    spread = (owner == lax.broadcasted_iota(jnp.int32, (tiles, slots), 0)).astype(jnp.bfloat16)
    count = jnp.broadcast_to(counts_in[...].astype(jnp.float32), (8, tiles)).astype(jnp.bfloat16)
    repeated = lax.dot_general(count, spread, (((1,), (0,)), ((), ())), preferred_element_type=jnp.float32)
    within = lax.broadcasted_iota(jnp.int32, (8, slots), 1) % cap
    live = (within.astype(jnp.float32) < repeated).astype(jnp.float32)
    values[7:8] = live[7:8]
    columns[...] = jnp.zeros_like(columns)
    for part in range(slots // LANES):
        turned = values[:, part * LANES:(part + 1) * LANES].T
        columns[cap + part * LANES:cap + (part + 1) * LANES, 0:ROWS] = turned
    planes = [jnp.zeros((tiles, LANES), jnp.float32), jnp.zeros((tiles, LANES), jnp.float32)]
    for group in range(3):
        for slot in range(cap):
            piece = columns[pl.ds(group * cap + slot, tiles, stride=cap), :]
            shift = (group % 2) * 64 + slot * ROWS
            planes[group // 2] += pltpu.roll(piece, shift, 1) if shift else piece
    for plane in range(2):
        payload[:, plane, :] = planes[plane]
    for copy in copies[3:]:
        copy.wait()


def adjoint_source(received, near, out, left, right):
    tiles = received.shape[0]
    turned = []
    for plane in range(2):
        here = received[:, plane, :]
        turned.append(jnp.concatenate([here, pltpu.roll(here, LANES - ROWS, 1)], axis=0).T)
    layer = out.shape[2]
    depth = out.shape[1] - 2 * HALO
    half = depth * layer // 2
    plan = ((depth - HALO, HALO, 0), (0, depth, HALO), (0, HALO, HALO + depth))
    for group, (first, layers, where) in enumerate(plan):
        base = (group % 2) * 64
        record = jnp.concatenate(
            [turned[group // 2][base + 16 * j:base + 16 * j + ROWS] for j in range(4)], axis=1
        )
        slots = record.shape[1]
        alive = record[7:8]
        cell = record[6:7].astype(jnp.int32)
        value = jnp.where(alive > 0.0, record, 0.0)
        high = value.astype(jnp.bfloat16).astype(jnp.float32)
        rest = value - high
        middle = rest.astype(jnp.bfloat16).astype(jnp.float32)
        low = rest - middle
        row = cell // LANES
        hit = lax.broadcasted_iota(jnp.int32, (half, slots), 0) == row % half
        place = 0
        for terms, names in ((high, (0, 1, 2, 3, 4, 5, 7)), (middle, range(6)), (low, range(6))):
            for name in names:
                left[group, place:place + half] = jnp.where(hit, terms[name:name + 1], 0.0).astype(jnp.bfloat16)
                place += half
        column = cell % LANES + LANES * (row // half)
        lane = lax.broadcasted_iota(jnp.int32, (2 * LANES, slots), 0) == column
        right[group] = lane.astype(jnp.float32).astype(jnp.bfloat16)
        sums = lax.dot_general(
            left[group], right[group], (((1,), (1,)), ((), ())), preferred_element_type=jnp.float32
        )
        for index in range(layers):
            side, at = divmod((first + index) * layer, half)
            columns = slice(side * LANES, (side + 1) * LANES)
            count = sums[6 * half + at:6 * half + at + layer, columns]
            for name in range(6):
                total = 0.0
                for part in (0, 7, 13):
                    row = (part + name) * half + at
                    total = total + sums[row:row + layer, columns]
                out[name, where + index] = count * near[name, where + index] - total


PITCH = 24


def clear(buffer, layers):
    for part in range(6):
        for layer in range(layers + 1):
            buffer[part, layer * PITCH:layer * PITCH + 8] = jnp.zeros((8, LANES), jnp.float32)


def damping_kernel(out, depth, tiles):
    tile = lax.axis_index("tile")
    for layer in range(out.shape[0]):
        place = tile * depth + layer - 2 * HALO
        scale = jnp.where((place >= 0) & (place < tiles * depth), DAMPING, 0.0)
        out[layer] = jnp.full(out.shape[1:], scale, jnp.float32)


def coefficients(absorbs, damping, pq):
    for layer, absorb in enumerate(absorbs):
        weight = damping[layer] / (36.0 + absorb * absorb)
        pq[0, layer] = 6.0 * weight
        pq[1, layer] = absorb * weight


def first_sweep(src, pq, dst, layers):
    def step(layer, carry):
        at = pl.ds(pl.multiple_of(layer * PITCH + 8, 8), 16)
        p, q = pq[0, layer], pq[1, layer]
        for part in range(3):
            re, im = src[part, layer], src[part + 3, layer]
            dst[part, at] = p * re + q * im
            dst[part + 3, at] = p * im - q * re
        return carry

    lax.fori_loop(0, layers, step, 0, unroll=2)


def sweep(src, pq, old, new, lo, hi, emit=None):
    lane = lax.broadcasted_iota(jnp.int32, (16, LANES), 1)
    not_first, not_last = lane > 0, lane < LANES - 1

    def neighbours(part, base):
        middle = old[part, pl.ds(base, 16)]
        beside = old[part, pl.ds(base - PITCH, 16)] + old[part, pl.ds(base + PITCH, 16)]
        beside = beside + (old[part, pl.ds(base - 1, 16)] + old[part, pl.ds(base + 1, 16)])
        beside = beside + jnp.where(not_first, pltpu.roll(middle, 1, 1), 0.0)
        beside = beside + jnp.where(not_last, pltpu.roll(middle, LANES - 1, 1), 0.0)
        return middle, beside

    def step(layer, carry):
        base = layer * PITCH + 8
        p, q = pq[0, layer], pq[1, layer]
        results = []
        for part in range(3):
            mid_re, sum_re = neighbours(part, base)
            mid_im, sum_im = neighbours(part + 3, base)
            sum_re = sum_re + src[part, layer]
            sum_im = sum_im + src[part + 3, layer]
            new_re = (1.0 - DAMPING) * mid_re + (p * sum_re + q * sum_im)
            new_im = (1.0 - DAMPING) * mid_im + (p * sum_im - q * sum_re)
            if emit is None:
                at = pl.ds(pl.multiple_of(base, 8), 16)
                new[part, at] = new_re
                new[part + 3, at] = new_im
            results.append((new_re, new_im))
        if emit is not None:
            emit(layer, results)
        return carry

    lax.fori_loop(lo, hi, step, 0, unroll=hi - lo)


def relax(src, pq, one, two, emit):
    layers = src.shape[1]
    clear(one, layers)
    clear(two, layers)
    first_sweep(src, pq, one, layers)
    old, new = one, two
    for index in range(1, SWEEPS):
        final = index == SWEEPS - 1
        sweep(src, pq, old, new, index, layers - index, emit if final else None)
        old, new = new, old


def choose_kernel(own, across, out):
    out[0] = own[...]
    out[1] = across[...]


def forward_kernel(factor, damping, own, across, edge, other, near, near_pq, src, pq, one, two):
    depth = own.shape[1]
    even = lax.axis_index("tile") % 2 == 0
    mine, theirs = other.at[0], other.at[1]
    views = [(edge, i, across, depth - 2 + i) for i in range(2)]
    views += [(theirs, i, mine, i) for i in range(depth)]
    views += [(own, i, own, i) for i in range(depth)]
    views += [(mine, i, theirs, i) for i in range(depth)]
    views += [(across, i, edge, i) for i in range(2)]
    absorbs = []
    for layer, (first, at, second, there) in enumerate(views):
        if first is second:
            src[:, layer] = first[:6, at]
            absorbs.append(factor[0] * first[6, at])
        else:
            src[:, layer] = jnp.where(even, first[:6, at], second[:6, there])
            absorbs.append(factor[0] * jnp.where(even, first[6, at], second[6, there]))
    coefficients(absorbs, damping, pq)
    near_pq[...] = pq[:, HALO:-HALO]

    def emit(layer, results):
        for part, (re, im) in enumerate(results):
            near[part, layer - HALO] = re
            near[part + 3, layer - HALO] = im

    relax(src, pq, one, two, emit)


def finish_kernel(factor, received, near, pq, terms, field, src, one, two, left, right, written):
    depth = near.shape[1] - 2 * HALO
    copy = pltpu.make_async_copy(near.at[:, pl.ds(HALO, depth)], field.at[0], written)
    copy.start()
    adjoint_source(received, near, src, left, right)

    def emit(layer, results):
        total = 0.0
        for part, (re, im) in enumerate(results):
            total = total + (re * near[part + 3, layer] + im * near[part, layer])
        total = factor[0] * total
        rows = pl.ds(pl.multiple_of((layer - HALO) * 16, 16), 16)
        for index in range(terms.shape[0]):
            terms[index, rows] = total

    relax(src, pq, one, two, emit)
    copy.wait()


def working(layers):
    buffer = pltpu.VMEM((6, layers * PITCH + 8, LANES), jnp.float32)
    return [pltpu.VMEM((6, layers, 16, LANES), jnp.float32), buffer, buffer]


def shape(*dims):
    return jax.ShapeDtypeStruct(dims, jnp.float32)


LIMIT = pltpu.CompilerParams(vmem_limit_bytes=16 * 2**20)


def cost(flops, size):
    return pl.CostEstimate(flops=flops, bytes_accessed=size, transcendentals=0)


def pack(source, conductivity, observed, slot_cells, block_counts):
    depth, ny, nz = conductivity.shape
    slots, tiles = slot_cells.shape[0], block_counts.shape[0]
    return pl.pallas_call(
        pack_kernel,
        out_shape=(shape(7, depth, ny, nz), shape(7, 2, ny, nz), shape(tiles, 2, LANES)),
        in_specs=[HBM] * 5,
        out_specs=(VMEM, VMEM, VMEM),
        scratch_shapes=[
            pltpu.VMEM((6, 1, slots), jnp.float32),
            pltpu.VMEM((1, slots), jnp.int32),
            pltpu.VMEM((1, tiles), jnp.int32),
            pltpu.VMEM((ROWS, slots), jnp.float32),
            pltpu.VMEM((slots + 2 * (slots // tiles), LANES), jnp.float32),
            pltpu.SemaphoreType.DMA((7,)),
        ],
        compiler_params=LIMIT,
        cost_estimate=cost(10**6, 10**6),
        name="pack",
    )(
        *(
            pltpu.with_memory_space_constraint(x, pltpu.HBM)
            for x in (
                source,
                conductivity,
                observed.transpose(1, 0, 2),
                slot_cells.reshape(1, -1),
                block_counts.reshape(1, -1),
            )
        )
    )


def choose(own, across):
    return pl.pallas_call(
        choose_kernel,
        out_shape=shape(2, *own.shape),
        in_specs=[VMEM] * 2,
        out_specs=VMEM,
        compiler_params=LIMIT,
        cost_estimate=cost(10**10, 10**9),
        name="choose",
    )(own, across)


def layer_damping(depth, ny, nz, tiles):
    return pl.pallas_call(
        functools.partial(damping_kernel, depth=depth, tiles=tiles),
        out_shape=shape(depth + 4 * HALO, ny, nz),
        out_specs=VMEM,
        compiler_params=LIMIT,
        cost_estimate=cost(10**10, 10**9),
        name="damping",
    )()


def forward(factor, damping, own, across, edge, other):
    depth, ny, nz = own.shape[1:]
    wide, layers = depth + 4 * HALO, depth + 2 * HALO
    return pl.pallas_call(
        forward_kernel,
        out_shape=(shape(6, layers, ny, nz), shape(2, layers, ny, nz)),
        in_specs=[SMEM] + [VMEM] * 5,
        out_specs=(VMEM, VMEM),
        scratch_shapes=[working(wide)[0], pltpu.VMEM((2, wide, ny, nz), jnp.float32)] + working(wide)[1:],
        compiler_params=LIMIT,
        cost_estimate=cost(10**6, 10**6),
        name="forward",
    )(factor, damping, own, across, edge, other)


def finish(factor, received, near, near_pq, freqs):
    layers, ny, nz = near.shape[1:]
    depth = layers - 2 * HALO
    slots = received.shape[0] * received.shape[2] // (2 * ROWS)
    return pl.pallas_call(
        finish_kernel,
        out_shape=(shape(freqs, depth * ny, nz), shape(1, 6, depth, ny, nz)),
        in_specs=[SMEM] + [VMEM] * 3,
        out_specs=(VMEM, HBM),
        scratch_shapes=working(layers) + [
            pltpu.VMEM((3, 19 * depth * ny // 2, slots), jnp.bfloat16),
            pltpu.VMEM((3, 2 * LANES, slots), jnp.bfloat16),
            pltpu.SemaphoreType.DMA,
        ],
        compiler_params=LIMIT,
        cost_estimate=cost(10**10, 10**9),
        name="finish",
    )(factor, received, near, near_pq)


def body(source, conductivity, freq_factor, observed, slot_cells, block_counts):
    tiles, freqs = lax.axis_size("tile"), lax.axis_size("freq")
    depth, ny, nz = conductivity.shape
    own, near_edge, payload = pack(source, conductivity, observed, slot_cells, block_counts)
    chips = tiles // 2
    up = [(2 * k, 2 * k + 2) for k in range(chips - 1)]
    down = [(2 * k + 2, 2 * k) for k in range(chips - 1)]
    across = lax.ppermute(own, "tile", down + [(i + 1, j + 1) for i, j in up])
    edge = lax.ppermute(near_edge, "tile", up + [(i + 1, j + 1) for i, j in down])
    received = lax.all_to_all(payload, "tile", split_axis=0, concat_axis=0, tiled=True)
    chosen = choose(own, across)
    other = lax.ppermute(chosen, "tile", [(i, i ^ 1) for i in range(tiles)])
    damping = layer_damping(depth, ny, nz, tiles)
    near, near_pq = forward(freq_factor, damping, own, across, edge, other)
    terms, field = finish(freq_factor, received, near, near_pq, freqs)
    terms = lax.all_to_all(terms, "freq", split_axis=0, concat_axis=0, tiled=True)
    gradient = jnp.sum(terms, axis=0).reshape(depth, ny, nz)
    return (field, gradient)


def solution(mesh):
    in_specs = (
        P(None, "tile", None, None),
        P("tile", None, None),
        P("freq"),
        P("freq", None, "tile"),
        P("tile"),
        P("tile"),
    )
    out_specs = (P("freq", None, "tile", None, None), P("tile", None, None))
    return jax.shard_map(body, mesh=mesh, in_specs=in_specs, out_specs=out_specs, check_vma=False)
```

```python
import functools

import jax
import jax.numpy as jnp
from jax import lax
from jax.experimental import pallas as pl
from jax.experimental.pallas import tpu as pltpu
from jax.sharding import PartitionSpec as P

SWEEPS = 4
DAMPING = 0.8
HALO = SWEEPS - 1
ROWS = 8
LANES = 128

VMEM = pl.BlockSpec(memory_space=pltpu.VMEM)
SMEM = pl.BlockSpec(memory_space=pltpu.SMEM)
HBM = pl.BlockSpec(memory_space=pltpu.HBM)


def pack_kernel(
    source, cond, observed, cells, counts, own, near_edge, payload,
    observed_in, cells_in, counts_in, values, columns, arrived,
):
    core = lax.axis_index("tile") % 2
    edge = pl.ds(2 * (1 - core), 2)
    copies = [
        pltpu.make_async_copy(start, end, arrived.at[i])
        for i, (start, end) in enumerate(
            (
                (observed, observed_in),
                (cells, cells_in),
                (counts, counts_in),
                (cond, own.at[6]),
                (cond.at[edge], near_edge.at[6]),
                (source, own.at[pl.ds(0, 6)]),
                (source.at[:, edge], near_edge.at[pl.ds(0, 6)]),
            )
        )
    ]
    for copy in copies:
        copy.start()
    for copy in copies[:3]:
        copy.wait()
    tiles = counts.shape[1]
    slots = cells.shape[1]
    cap = slots // tiles
    for part in range(6):
        values[part:part + 1] = observed_in[part]
    values[6:7] = cells_in[...].astype(jnp.float32)
    owner = lax.broadcasted_iota(jnp.int32, (tiles, slots), 1) // cap
    spread = (owner == lax.broadcasted_iota(jnp.int32, (tiles, slots), 0)).astype(jnp.bfloat16)
    count = jnp.broadcast_to(counts_in[...].astype(jnp.float32), (8, tiles)).astype(jnp.bfloat16)
    repeated = lax.dot_general(count, spread, (((1,), (0,)), ((), ())), preferred_element_type=jnp.float32)
    within = lax.broadcasted_iota(jnp.int32, (8, slots), 1) % cap
    live = (within.astype(jnp.float32) < repeated).astype(jnp.float32)
    values[7:8] = live[7:8]
    columns[...] = jnp.zeros_like(columns)
    for part in range(slots // LANES):
        turned = values[:, part * LANES:(part + 1) * LANES].T
        columns[cap + part * LANES:cap + (part + 1) * LANES, 0:ROWS] = turned
    planes = [jnp.zeros((tiles, LANES), jnp.float32), jnp.zeros((tiles, LANES), jnp.float32)]
    for group in range(3):
        for slot in range(cap):
            piece = columns[pl.ds(group * cap + slot, tiles, stride=cap), :]
            shift = (group % 2) * 64 + slot * ROWS
            planes[group // 2] += pltpu.roll(piece, shift, 1) if shift else piece
    for plane in range(2):
        payload[:, plane, :] = planes[plane]
    for copy in copies[3:]:
        copy.wait()


def adjoint_source(received, near, out, left, right):
    tiles = received.shape[0]
    turned = []
    for plane in range(2):
        here = received[:, plane, :]
        turned.append(jnp.concatenate([here, pltpu.roll(here, LANES - ROWS, 1)], axis=0).T)
    layer = out.shape[2]
    depth = out.shape[1] - 2 * HALO
    plan = ((depth - HALO, HALO, 0), (0, depth, HALO), (0, HALO, HALO + depth))
    for group, (first, layers, where) in enumerate(plan):
        base = (group % 2) * 64
        record = jnp.concatenate(
            [turned[group // 2][base + 16 * j:base + 16 * j + ROWS] for j in range(4)], axis=1
        )
        slots = record.shape[1]
        alive = record[7:8]
        cell = record[6:7].astype(jnp.int32)
        value = jnp.where(alive > 0.0, record, 0.0)
        high = value.astype(jnp.bfloat16).astype(jnp.float32)
        rest = value - high
        middle = rest.astype(jnp.bfloat16).astype(jnp.float32)
        low = rest - middle
        half = layers * layer // 2
        row = (cell >> 7) - first * layer
        upper = (row >= half).astype(jnp.int32)
        hit = lax.broadcasted_iota(jnp.int32, (half, slots), 0) == row - half * upper
        blocks = [
            jnp.where(hit, terms[name:name + 1], 0.0)
            for terms, names in ((high, (0, 1, 2, 3, 4, 5, 7)), (middle, range(6)), (low, range(6)))
            for name in names
        ]
        if len(blocks) * half % 16:
            blocks.append(jnp.zeros((half, slots), jnp.float32))
        stacked = jnp.concatenate(blocks, axis=0).astype(jnp.bfloat16)
        left[group, :stacked.shape[0]] = stacked
        column = (cell & (LANES - 1)) + LANES * upper
        lane = lax.broadcasted_iota(jnp.int32, (2 * LANES, slots), 0) == column
        right[group] = lane.astype(jnp.float32).astype(jnp.bfloat16)
        sums = lax.dot_general(
            left[group, :stacked.shape[0]], right[group], (((1,), (1,)), ((), ())),
            preferred_element_type=jnp.float32,
        )

        def part(block, at, size):
            side, at = divmod(at, half)
            return sums[block * half + at:block * half + at + size, side * LANES:(side + 1) * LANES]

        for index in range(layers):
            for piece in range(0, layer, 8):
                at = index * layer + piece
                rows = slice(piece, piece + 8)
                count = part(6, at, 8)
                for name in range(6):
                    total = part(name, at, 8) + part(7 + name, at, 8) + part(13 + name, at, 8)
                    out[name, where + index, rows] = count * near[name, where + index, rows] - total


PITCH = 24


def clear(buffer, layers):
    for part in range(6):
        for layer in range(layers + 1):
            buffer[part, layer * PITCH:layer * PITCH + 8] = jnp.zeros((8, LANES), jnp.float32)


def damping_kernel(out, depth, tiles):
    tile = lax.axis_index("tile")
    for layer in range(out.shape[0]):
        place = tile * depth + layer - 2 * HALO
        scale = jnp.where((place >= 0) & (place < tiles * depth), DAMPING, 0.0)
        out[layer] = jnp.full(out.shape[1:], scale, jnp.float32)


def coefficients(absorbs, damping, pq):
    for layer, absorb in enumerate(absorbs):
        weight = damping[layer] / (36.0 + absorb * absorb)
        pq[0, layer] = 6.0 * weight
        pq[1, layer] = absorb * weight


def first_sweep(src, pq, dst, layers):
    def step(layer, carry):
        at = pl.ds(pl.multiple_of(layer * PITCH + 8, 8), 16)
        p, q = pq[0, layer], pq[1, layer]
        for part in range(3):
            re, im = src[part, layer], src[part + 3, layer]
            dst[part, at] = p * re + q * im
            dst[part + 3, at] = p * im - q * re
        return carry

    lax.fori_loop(0, layers, step, 0, unroll=16 if layers == 16 else 2)


def sweep(src, pq, old, new, lo, hi, emit=None):
    lane = lax.broadcasted_iota(jnp.int32, (16, LANES), 1)
    not_first, not_last = lane > 0, lane < LANES - 1

    def neighbours(part, base):
        middle = old[part, pl.ds(base, 16)]
        beside = old[part, pl.ds(base - PITCH, 16)] + old[part, pl.ds(base + PITCH, 16)]
        beside = beside + (old[part, pl.ds(base - 1, 16)] + old[part, pl.ds(base + 1, 16)])
        beside = beside + jnp.where(not_first, pltpu.roll(middle, 1, 1), 0.0)
        beside = beside + jnp.where(not_last, pltpu.roll(middle, LANES - 1, 1), 0.0)
        return middle, beside

    def step(layer, carry):
        base = layer * PITCH + 8
        p, q = pq[0, layer], pq[1, layer]
        results = []
        for part in range(3):
            mid_re, sum_re = neighbours(part, base)
            mid_im, sum_im = neighbours(part + 3, base)
            sum_re = sum_re + src[part, layer]
            sum_im = sum_im + src[part + 3, layer]
            new_re = (1.0 - DAMPING) * mid_re + (p * sum_re + q * sum_im)
            new_im = (1.0 - DAMPING) * mid_im + (p * sum_im - q * sum_re)
            if emit is None:
                at = pl.ds(pl.multiple_of(base, 8), 16)
                new[part, at] = new_re
                new[part + 3, at] = new_im
            results.append((new_re, new_im))
        if emit is not None:
            emit(layer, results)
        return carry

    lax.fori_loop(lo, hi, step, 0, unroll=hi - lo)


def relax(src, pq, one, two, emit):
    layers = src.shape[1]
    clear(one, layers)
    clear(two, layers)
    first_sweep(src, pq, one, layers)
    old, new = one, two
    for index in range(1, SWEEPS):
        final = index == SWEEPS - 1
        sweep(src, pq, old, new, index, layers - index, emit if final else None)
        old, new = new, old


def choose_kernel(own, across, out):
    out[0] = own[...]
    out[1] = across[...]


def forward_kernel(factor, damping, own, across, edge, other, near, near_pq, src, pq, one, two):
    depth = own.shape[1]
    even = lax.axis_index("tile") % 2 == 0
    mine, theirs = other.at[0], other.at[1]
    views = [(edge, i, across, depth - 2 + i) for i in range(2)]
    views += [(theirs, i, mine, i) for i in range(depth)]
    views += [(own, i, own, i) for i in range(depth)]
    views += [(mine, i, theirs, i) for i in range(depth)]
    views += [(across, i, edge, i) for i in range(2)]
    absorbs = []
    for layer, (first, at, second, there) in enumerate(views):
        if first is second:
            src[:, layer] = first[:6, at]
            absorbs.append(factor[0] * first[6, at])
        else:
            src[:, layer] = jnp.where(even, first[:6, at], second[:6, there])
            absorbs.append(factor[0] * jnp.where(even, first[6, at], second[6, there]))
    coefficients(absorbs, damping, pq)
    near_pq[...] = pq[:, HALO:-HALO]

    def emit(layer, results):
        for part, (re, im) in enumerate(results):
            near[part, layer - HALO] = re
            near[part + 3, layer - HALO] = im

    relax(src, pq, one, two, emit)


def finish_kernel(factor, received, near, pq, terms, field, src, one, two, left, right, written):
    depth = near.shape[1] - 2 * HALO
    copy = pltpu.make_async_copy(near.at[:, pl.ds(HALO, depth)], field.at[0], written)
    copy.start()
    adjoint_source(received, near, src, left, right)

    def emit(layer, results):
        total = 0.0
        for part, (re, im) in enumerate(results):
            total = total + (re * near[part + 3, layer] + im * near[part, layer])
        total = factor[0] * total
        rows = pl.ds(pl.multiple_of((layer - HALO) * 16, 16), 16)
        for index in range(terms.shape[0]):
            terms[index, rows] = total

    relax(src, pq, one, two, emit)
    copy.wait()


def working(layers):
    buffer = pltpu.VMEM((6, layers * PITCH + 8, LANES), jnp.float32)
    return [pltpu.VMEM((6, layers, 16, LANES), jnp.float32), buffer, buffer]


def shape(*dims):
    return jax.ShapeDtypeStruct(dims, jnp.float32)


LIMIT = pltpu.CompilerParams(vmem_limit_bytes=16 * 2**20)


def cost(flops, size):
    return pl.CostEstimate(flops=flops, bytes_accessed=size, transcendentals=0)


def pack(source, conductivity, observed, slot_cells, block_counts):
    depth, ny, nz = conductivity.shape
    slots, tiles = slot_cells.shape[0], block_counts.shape[0]
    return pl.pallas_call(
        pack_kernel,
        out_shape=(shape(7, depth, ny, nz), shape(7, 2, ny, nz), shape(tiles, 2, LANES)),
        in_specs=[HBM] * 5,
        out_specs=(VMEM, VMEM, VMEM),
        scratch_shapes=[
            pltpu.VMEM((6, 1, slots), jnp.float32),
            pltpu.VMEM((1, slots), jnp.int32),
            pltpu.VMEM((1, tiles), jnp.int32),
            pltpu.VMEM((ROWS, slots), jnp.float32),
            pltpu.VMEM((slots + 2 * (slots // tiles), LANES), jnp.float32),
            pltpu.SemaphoreType.DMA((7,)),
        ],
        compiler_params=LIMIT,
        cost_estimate=cost(10**6, 10**6),
        name="pack",
    )(
        *(
            pltpu.with_memory_space_constraint(x, pltpu.HBM)
            for x in (
                source,
                conductivity,
                observed.transpose(1, 0, 2),
                slot_cells.reshape(1, -1),
                block_counts.reshape(1, -1),
            )
        )
    )


def choose(own, across):
    return pl.pallas_call(
        choose_kernel,
        out_shape=shape(2, *own.shape),
        in_specs=[VMEM] * 2,
        out_specs=VMEM,
        compiler_params=LIMIT,
        cost_estimate=cost(10**10, 10**9),
        name="choose",
    )(own, across)


def layer_damping(depth, ny, nz, tiles):
    return pl.pallas_call(
        functools.partial(damping_kernel, depth=depth, tiles=tiles),
        out_shape=shape(depth + 4 * HALO, ny, nz),
        out_specs=VMEM,
        compiler_params=LIMIT,
        cost_estimate=cost(10**10, 10**9),
        name="damping",
    )()


def forward(factor, damping, own, across, edge, other):
    depth, ny, nz = own.shape[1:]
    wide, layers = depth + 4 * HALO, depth + 2 * HALO
    return pl.pallas_call(
        forward_kernel,
        out_shape=(shape(6, layers, ny, nz), shape(2, layers, ny, nz)),
        in_specs=[SMEM] + [VMEM] * 5,
        out_specs=(VMEM, VMEM),
        scratch_shapes=[working(wide)[0], pltpu.VMEM((2, wide, ny, nz), jnp.float32)] + working(wide)[1:],
        compiler_params=LIMIT,
        cost_estimate=cost(10**6, 10**6),
        name="forward",
    )(factor, damping, own, across, edge, other)


def finish(factor, received, near, near_pq, freqs):
    layers, ny, nz = near.shape[1:]
    depth = layers - 2 * HALO
    slots = received.shape[0] * received.shape[2] // (2 * ROWS)
    return pl.pallas_call(
        finish_kernel,
        out_shape=(shape(freqs, depth * ny, nz), shape(1, 6, depth, ny, nz)),
        in_specs=[SMEM] + [VMEM] * 3,
        out_specs=(VMEM, HBM),
        scratch_shapes=working(layers) + [
            pltpu.VMEM((3, 19 * depth * ny // 2, slots), jnp.bfloat16),
            pltpu.VMEM((3, 2 * LANES, slots), jnp.bfloat16),
            pltpu.SemaphoreType.DMA,
        ],
        compiler_params=LIMIT,
        cost_estimate=cost(10**10, 10**9),
        name="finish",
    )(factor, received, near, near_pq)


def body(source, conductivity, freq_factor, observed, slot_cells, block_counts):
    tiles, freqs = lax.axis_size("tile"), lax.axis_size("freq")
    depth, ny, nz = conductivity.shape
    own, near_edge, payload = pack(source, conductivity, observed, slot_cells, block_counts)
    chips = tiles // 2
    up = [(2 * k, 2 * k + 2) for k in range(chips - 1)]
    down = [(2 * k + 2, 2 * k) for k in range(chips - 1)]
    across = lax.ppermute(own, "tile", down + [(i + 1, j + 1) for i, j in up])
    edge = lax.ppermute(near_edge, "tile", up + [(i + 1, j + 1) for i, j in down])
    received = lax.all_to_all(payload, "tile", split_axis=0, concat_axis=0, tiled=True)
    chosen = choose(own, across)
    other = lax.ppermute(chosen, "tile", [(i, i ^ 1) for i in range(tiles)])
    damping = layer_damping(depth, ny, nz, tiles)
    near, near_pq = forward(freq_factor, damping, own, across, edge, other)
    terms, field = finish(freq_factor, received, near, near_pq, freqs)
    terms = lax.all_to_all(terms, "freq", split_axis=0, concat_axis=0, tiled=True)
    gradient = jnp.sum(terms, axis=0).reshape(depth, ny, nz)
    return (field, gradient)


def solution(mesh):
    in_specs = (
        P(None, "tile", None, None),
        P("tile", None, None),
        P("freq"),
        P("freq", None, "tile"),
        P("tile"),
        P("tile"),
    )
    out_specs = (P("freq", None, "tile", None, None), P("tile", None, None))
    return jax.shard_map(body, mesh=mesh, in_specs=in_specs, out_specs=out_specs, check_vma=False)
```

```python
import functools

import jax
import jax.numpy as jnp
from jax import lax
from jax.experimental import pallas as pl
from jax.experimental.pallas import tpu as pltpu
from jax.sharding import PartitionSpec as P

SWEEPS = 4
DAMPING = 0.8
HALO = SWEEPS - 1
ROWS = 8
LANES = 128

VMEM = pl.BlockSpec(memory_space=pltpu.VMEM)
SMEM = pl.BlockSpec(memory_space=pltpu.SMEM)
HBM = pl.BlockSpec(memory_space=pltpu.HBM)


def pack_kernel(
    source, cond, observed, cells, counts, own, near_edge, payload,
    observed_in, cells_in, counts_in, values, columns, staged, arrived, left,
):
    core = lax.axis_index("tile") % 2
    edge = pl.ds(2 * (1 - core), 2)
    copies = [
        pltpu.make_async_copy(start, end, arrived.at[i])
        for i, (start, end) in enumerate(
            (
                (observed, observed_in),
                (cells, cells_in),
                (counts, counts_in),
                (cond, own.at[6]),
                (cond.at[edge], near_edge.at[6]),
                (source, own.at[pl.ds(0, 6)]),
                (source.at[:, edge], near_edge.at[pl.ds(0, 6)]),
            )
        )
    ]
    for copy in copies:
        copy.start()
    for copy in copies[:3]:
        copy.wait()
    tiles = counts.shape[1]
    slots = cells.shape[1]
    cap = slots // tiles
    for part in range(6):
        values[part:part + 1] = observed_in[part]
    values[6:7] = cells_in[...].astype(jnp.float32)
    owner = lax.broadcasted_iota(jnp.int32, (tiles, slots), 1) // cap
    spread = (owner == lax.broadcasted_iota(jnp.int32, (tiles, slots), 0)).astype(jnp.bfloat16)
    count = jnp.broadcast_to(counts_in[...].astype(jnp.float32), (8, tiles)).astype(jnp.bfloat16)
    repeated = lax.dot_general(count, spread, (((1,), (0,)), ((), ())), preferred_element_type=jnp.float32)
    within = lax.broadcasted_iota(jnp.int32, (8, slots), 1) % cap
    live = (within.astype(jnp.float32) < repeated).astype(jnp.float32)
    values[7:8] = live[7:8]
    columns[...] = jnp.zeros_like(columns)
    for part in range(slots // LANES):
        turned = values[:, part * LANES:(part + 1) * LANES].T
        columns[cap + part * LANES:cap + (part + 1) * LANES, 0:ROWS] = turned
    planes = [jnp.zeros((tiles, LANES), jnp.float32), jnp.zeros((tiles, LANES), jnp.float32)]
    for group in range(3):
        for slot in range(cap):
            piece = columns[pl.ds(group * cap + slot, tiles, stride=cap), :]
            shift = (group % 2) * 64 + slot * ROWS
            planes[group // 2] += pltpu.roll(piece, shift, 1) if shift else piece
    for plane in range(2):
        staged[:, plane, :] = planes[plane]
    sent = pltpu.make_async_copy(staged, payload, left)
    sent.start()
    for copy in copies[3:]:
        copy.wait()
    sent.wait()


def adjoint_source(received, near, out, left, right):
    tiles = received.shape[0]
    turned = []
    for plane in range(2):
        here = received[:, plane, :]
        turned.append(jnp.concatenate([here, pltpu.roll(here, LANES - ROWS, 1)], axis=0).T)
    layer = out.shape[2]
    depth = out.shape[1] - 2 * HALO
    plan = ((depth - HALO, HALO, 0), (0, depth, HALO), (0, HALO, HALO + depth))
    for group, (first, layers, where) in enumerate(plan):
        base = (group % 2) * 64
        record = jnp.concatenate(
            [turned[group // 2][base + 16 * j:base + 16 * j + ROWS] for j in range(4)], axis=1
        )
        slots = record.shape[1]
        alive = record[7:8]
        cell = record[6:7].astype(jnp.int32)
        value = jnp.where(alive > 0.0, record, 0.0)
        high = value.astype(jnp.bfloat16).astype(jnp.float32)
        rest = value - high
        middle = rest.astype(jnp.bfloat16).astype(jnp.float32)
        low = rest - middle
        half = layers * layer // 2
        row = (cell >> 7) - first * layer
        upper = (row >= half).astype(jnp.int32)
        hit = lax.broadcasted_iota(jnp.int32, (half, slots), 0) == row - half * upper
        blocks = [
            jnp.where(hit, terms[name:name + 1], 0.0)
            for terms, names in ((high, (0, 1, 2, 3, 4, 5, 7)), (middle, range(6)), (low, range(6)))
            for name in names
        ]
        if len(blocks) * half % 16:
            blocks.append(jnp.zeros((half, slots), jnp.float32))
        stacked = jnp.concatenate(blocks, axis=0).astype(jnp.bfloat16)
        left[group, :stacked.shape[0]] = stacked
        column = (cell & (LANES - 1)) + LANES * upper
        lane = lax.broadcasted_iota(jnp.int32, (2 * LANES, slots), 0) == column
        right[group] = lane.astype(jnp.float32).astype(jnp.bfloat16)
        sums = lax.dot_general(
            left[group, :stacked.shape[0]], right[group], (((1,), (1,)), ((), ())),
            preferred_element_type=jnp.float32,
        )

        def part(block, at, size):
            side, at = divmod(at, half)
            return sums[block * half + at:block * half + at + size, side * LANES:(side + 1) * LANES]

        for index in range(layers):
            for piece in range(0, layer, 8):
                at = index * layer + piece
                rows = slice(piece, piece + 8)
                count = part(6, at, 8)
                for name in range(6):
                    total = part(name, at, 8) + part(7 + name, at, 8) + part(13 + name, at, 8)
                    out[name, where + index, rows] = count * near[name, where + index, rows] - total


PITCH = 24


def clear(buffer, layers):
    for part in range(6):
        for layer in range(layers + 1):
            buffer[part, layer * PITCH:layer * PITCH + 8] = jnp.zeros((8, LANES), jnp.float32)


def damping_kernel(out, depth, tiles):
    tile = lax.axis_index("tile")
    for layer in range(out.shape[0]):
        place = tile * depth + layer - 2 * HALO
        scale = jnp.where((place >= 0) & (place < tiles * depth), DAMPING, 0.0)
        out[layer] = jnp.full(out.shape[1:], scale, jnp.float32)


def coefficients(absorbs, damping, pq):
    for layer, absorb in enumerate(absorbs):
        weight = damping[layer] / (36.0 + absorb * absorb)
        pq[0, layer] = 6.0 * weight
        pq[1, layer] = absorb * weight


def first_sweep(src, pq, dst, layers):
    def step(layer, carry):
        at = pl.ds(pl.multiple_of(layer * PITCH + 8, 8), 16)
        p, q = pq[0, layer], pq[1, layer]
        for part in range(3):
            re, im = src[part, layer], src[part + 3, layer]
            dst[part, at] = p * re + q * im
            dst[part + 3, at] = p * im - q * re
        return carry

    lax.fori_loop(0, layers, step, 0, unroll=16 if layers == 16 else 2)


def sweep(src, pq, old, new, lo, hi, emit=None):
    lane = lax.broadcasted_iota(jnp.int32, (16, LANES), 1)
    not_first, not_last = lane > 0, lane < LANES - 1

    def neighbours(part, base):
        middle = old[part, pl.ds(base, 16)]
        beside = old[part, pl.ds(base - PITCH, 16)] + old[part, pl.ds(base + PITCH, 16)]
        beside = beside + (old[part, pl.ds(base - 1, 16)] + old[part, pl.ds(base + 1, 16)])
        beside = beside + jnp.where(not_first, pltpu.roll(middle, 1, 1), 0.0)
        beside = beside + jnp.where(not_last, pltpu.roll(middle, LANES - 1, 1), 0.0)
        return middle, beside

    def step(layer, carry):
        base = layer * PITCH + 8
        p, q = pq[0, layer], pq[1, layer]
        results = []
        for part in range(3):
            mid_re, sum_re = neighbours(part, base)
            mid_im, sum_im = neighbours(part + 3, base)
            sum_re = sum_re + src[part, layer]
            sum_im = sum_im + src[part + 3, layer]
            new_re = (1.0 - DAMPING) * mid_re + (p * sum_re + q * sum_im)
            new_im = (1.0 - DAMPING) * mid_im + (p * sum_im - q * sum_re)
            if emit is None:
                at = pl.ds(pl.multiple_of(base, 8), 16)
                new[part, at] = new_re
                new[part + 3, at] = new_im
            results.append((new_re, new_im))
        if emit is not None:
            emit(layer, results)
        return carry

    lax.fori_loop(lo, hi, step, 0, unroll=hi - lo)


def relax(src, pq, one, two, emit):
    layers = src.shape[1]
    clear(one, layers)
    clear(two, layers)
    first_sweep(src, pq, one, layers)
    old, new = one, two
    for index in range(1, SWEEPS):
        final = index == SWEEPS - 1
        sweep(src, pq, old, new, index, layers - index, emit if final else None)
        old, new = new, old


def choose_kernel(own, across, out):
    out[0] = own[...]
    out[1] = across[...]


def forward_kernel(factor, damping, own, across, edge, other, near, near_pq, src, pq, one, two):
    depth = own.shape[1]
    even = lax.axis_index("tile") % 2 == 0
    mine, theirs = other.at[0], other.at[1]
    views = [(edge, i, across, depth - 2 + i) for i in range(2)]
    views += [(theirs, i, mine, i) for i in range(depth)]
    views += [(own, i, own, i) for i in range(depth)]
    views += [(mine, i, theirs, i) for i in range(depth)]
    views += [(across, i, edge, i) for i in range(2)]
    absorbs = []
    for layer, (first, at, second, there) in enumerate(views):
        if first is second:
            src[:, layer] = first[:6, at]
            absorbs.append(factor[0] * first[6, at])
        else:
            src[:, layer] = jnp.where(even, first[:6, at], second[:6, there])
            absorbs.append(factor[0] * jnp.where(even, first[6, at], second[6, there]))
    coefficients(absorbs, damping, pq)
    near_pq[...] = pq[:, HALO:-HALO]

    def emit(layer, results):
        for part, (re, im) in enumerate(results):
            near[part, layer - HALO] = re
            near[part + 3, layer - HALO] = im

    relax(src, pq, one, two, emit)


def finish_kernel(factor, received, near, pq, terms, field, src, one, two, left, right, written):
    depth = near.shape[1] - 2 * HALO
    copy = pltpu.make_async_copy(near.at[:, pl.ds(HALO, depth)], field.at[0], written)
    copy.start()
    adjoint_source(received, near, src, left, right)

    def emit(layer, results):
        total = 0.0
        for part, (re, im) in enumerate(results):
            total = total + (re * near[part + 3, layer] + im * near[part, layer])
        total = factor[0] * total
        rows = pl.ds(pl.multiple_of((layer - HALO) * 16, 16), 16)
        for index in range(terms.shape[0]):
            terms[index, rows] = total

    relax(src, pq, one, two, emit)
    copy.wait()


def working(layers):
    buffer = pltpu.VMEM((6, layers * PITCH + 8, LANES), jnp.float32)
    return [pltpu.VMEM((6, layers, 16, LANES), jnp.float32), buffer, buffer]


def shape(*dims):
    return jax.ShapeDtypeStruct(dims, jnp.float32)


LIMIT = pltpu.CompilerParams(vmem_limit_bytes=16 * 2**20)


def cost(flops, size):
    return pl.CostEstimate(flops=flops, bytes_accessed=size, transcendentals=0)


def pack(source, conductivity, observed, slot_cells, block_counts):
    depth, ny, nz = conductivity.shape
    slots, tiles = slot_cells.shape[0], block_counts.shape[0]
    return pl.pallas_call(
        pack_kernel,
        out_shape=(shape(7, depth, ny, nz), shape(7, 2, ny, nz), shape(tiles, 2, LANES)),
        in_specs=[HBM] * 5,
        out_specs=(VMEM, VMEM, HBM),
        scratch_shapes=[
            pltpu.VMEM((6, 1, slots), jnp.float32),
            pltpu.VMEM((1, slots), jnp.int32),
            pltpu.VMEM((1, tiles), jnp.int32),
            pltpu.VMEM((ROWS, slots), jnp.float32),
            pltpu.VMEM((slots + 2 * (slots // tiles), LANES), jnp.float32),
            pltpu.VMEM((tiles, 2, LANES), jnp.float32),
            pltpu.SemaphoreType.DMA((7,)),
            pltpu.SemaphoreType.DMA,
        ],
        compiler_params=LIMIT,
        cost_estimate=cost(10**6, 10**6),
        name="pack",
    )(
        *(
            pltpu.with_memory_space_constraint(x, pltpu.HBM)
            for x in (
                source,
                conductivity,
                observed.transpose(1, 0, 2),
                slot_cells.reshape(1, -1),
                block_counts.reshape(1, -1),
            )
        )
    )


def choose(own, across):
    return pl.pallas_call(
        choose_kernel,
        out_shape=shape(2, *own.shape),
        in_specs=[VMEM] * 2,
        out_specs=VMEM,
        compiler_params=LIMIT,
        cost_estimate=cost(10**10, 10**9),
        name="choose",
    )(own, across)


def layer_damping(depth, ny, nz, tiles):
    return pl.pallas_call(
        functools.partial(damping_kernel, depth=depth, tiles=tiles),
        out_shape=shape(depth + 4 * HALO, ny, nz),
        out_specs=VMEM,
        compiler_params=LIMIT,
        cost_estimate=cost(10**10, 10**9),
        name="damping",
    )()


def forward(factor, damping, own, across, edge, other):
    depth, ny, nz = own.shape[1:]
    wide, layers = depth + 4 * HALO, depth + 2 * HALO
    return pl.pallas_call(
        forward_kernel,
        out_shape=(shape(6, layers, ny, nz), shape(2, layers, ny, nz)),
        in_specs=[SMEM] + [VMEM] * 5,
        out_specs=(VMEM, VMEM),
        scratch_shapes=[working(wide)[0], pltpu.VMEM((2, wide, ny, nz), jnp.float32)] + working(wide)[1:],
        compiler_params=LIMIT,
        cost_estimate=cost(10**6, 10**6),
        name="forward",
    )(factor, damping, own, across, edge, other)


def finish(factor, received, near, near_pq, freqs):
    layers, ny, nz = near.shape[1:]
    depth = layers - 2 * HALO
    slots = received.shape[0] * received.shape[2] // (2 * ROWS)
    return pl.pallas_call(
        finish_kernel,
        out_shape=(shape(freqs, depth * ny, nz), shape(1, 6, depth, ny, nz)),
        in_specs=[SMEM] + [VMEM] * 3,
        out_specs=(VMEM, HBM),
        scratch_shapes=working(layers) + [
            pltpu.VMEM((3, 19 * depth * ny // 2, slots), jnp.bfloat16),
            pltpu.VMEM((3, 2 * LANES, slots), jnp.bfloat16),
            pltpu.SemaphoreType.DMA,
        ],
        compiler_params=LIMIT,
        cost_estimate=cost(10**10, 10**9),
        name="finish",
    )(factor, received, near, near_pq)


def body(source, conductivity, freq_factor, observed, slot_cells, block_counts):
    tiles, freqs = lax.axis_size("tile"), lax.axis_size("freq")
    depth, ny, nz = conductivity.shape
    own, near_edge, payload = pack(source, conductivity, observed, slot_cells, block_counts)
    chips = tiles // 2
    up = [(2 * k, 2 * k + 2) for k in range(chips - 1)]
    down = [(2 * k + 2, 2 * k) for k in range(chips - 1)]
    across = lax.ppermute(own, "tile", down + [(i + 1, j + 1) for i, j in up])
    edge = lax.ppermute(near_edge, "tile", up + [(i + 1, j + 1) for i, j in down])
    received = lax.all_to_all(payload, "tile", split_axis=0, concat_axis=0, tiled=True)
    chosen = choose(own, across)
    other = lax.ppermute(chosen, "tile", [(i, i ^ 1) for i in range(tiles)])
    damping = layer_damping(depth, ny, nz, tiles)
    near, near_pq = forward(freq_factor, damping, own, across, edge, other)
    terms, field = finish(freq_factor, received, near, near_pq, freqs)
    terms = lax.all_to_all(terms, "freq", split_axis=0, concat_axis=0, tiled=True)
    gradient = jnp.sum(terms, axis=0).reshape(depth, ny, nz)
    return (field, gradient)


def solution(mesh):
    in_specs = (
        P(None, "tile", None, None),
        P("tile", None, None),
        P("freq"),
        P("freq", None, "tile"),
        P("tile"),
        P("tile"),
    )
    out_specs = (P("freq", None, "tile", None, None), P("tile", None, None))
    return jax.shard_map(body, mesh=mesh, in_specs=in_specs, out_specs=out_specs, check_vma=False)
```

```python
import functools

import jax
import jax.numpy as jnp
from jax import lax
from jax.experimental import pallas as pl
from jax.experimental.pallas import tpu as pltpu
from jax.sharding import PartitionSpec as P

SWEEPS = 4
DAMPING = 0.8
HALO = SWEEPS - 1
ROWS = 8
LANES = 128

VMEM = pl.BlockSpec(memory_space=pltpu.VMEM)
SMEM = pl.BlockSpec(memory_space=pltpu.SMEM)
HBM = pl.BlockSpec(memory_space=pltpu.HBM)


def pack_kernel(
    source, cond, observed, cells, counts, own, near_edge, payload,
    observed_in, cells_in, counts_in, values, columns, counted, staged, arrived, left,
):
    core = lax.axis_index("tile") % 2
    edge = pl.ds(2 * (1 - core), 2)
    copies = [
        pltpu.make_async_copy(start, end, arrived.at[i])
        for i, (start, end) in enumerate(
            (
                (observed, observed_in),
                (cells, cells_in),
                (counts, counts_in),
                (cond, own.at[6]),
                (cond.at[edge], near_edge.at[6]),
                (source, own.at[pl.ds(0, 6)]),
                (source.at[:, edge], near_edge.at[pl.ds(0, 6)]),
            )
        )
    ]
    for copy in copies:
        copy.start()
    for copy in copies[:3]:
        copy.wait()
    tiles = counts.shape[1]
    slots = cells.shape[1]
    cap = slots // tiles
    for part in range(6):
        values[part:part + 1] = observed_in[part]
    values[6:7] = cells_in[...].astype(jnp.float32)
    values[7:8] = jnp.zeros((1, slots), jnp.float32)
    counted[...] = jnp.zeros_like(counted)
    row = jnp.concatenate([counts_in[...].astype(jnp.float32), jnp.zeros((1, LANES - tiles), jnp.float32)], axis=1)
    counted[8:8 + tiles, 0:8] = jnp.broadcast_to(row, (8, LANES)).T[:tiles]
    columns[...] = jnp.zeros_like(columns)
    for part in range(slots // LANES):
        turned = values[:, part * LANES:(part + 1) * LANES].T
        columns[cap + part * LANES:cap + (part + 1) * LANES, 0:ROWS] = turned
    planes = [jnp.zeros((tiles, LANES), jnp.float32), jnp.zeros((tiles, LANES), jnp.float32)]
    for group in range(3):
        for slot in range(cap):
            piece = columns[pl.ds(group * cap + slot, tiles, stride=cap), :]
            shift = (group % 2) * 64 + slot * ROWS
            planes[group // 2] += pltpu.roll(piece, shift, 1) if shift else piece
    lane = lax.broadcasted_iota(jnp.int32, (tiles, LANES), 1)
    within = ((lane & 63) >> 3).astype(jnp.float32)
    own_count, left_count, right_count = (counted[8 + i:8 + i + tiles, 0:1] for i in (0, -1, 1))
    for plane, limit in enumerate(
        (jnp.where(lane < 64, left_count, own_count), jnp.where(lane < 64, right_count, 0.0))
    ):
        live = ((lane & 7) == 7) & (within < limit)
        staged[:, plane, :] = jnp.where(live, 1.0, planes[plane])
    sent = pltpu.make_async_copy(staged, payload, left)
    sent.start()
    for copy in copies[3:]:
        copy.wait()
    sent.wait()


def adjoint_source(received, near, out, left, right):
    tiles = received.shape[0]
    turned = []
    for plane in range(2):
        here = received[:, plane, :]
        turned.append(jnp.concatenate([here, pltpu.roll(here, LANES - ROWS, 1)], axis=0).T)
    layer = out.shape[2]
    depth = out.shape[1] - 2 * HALO
    plan = ((depth - HALO, HALO, 0), (0, depth, HALO), (0, HALO, HALO + depth))
    for group, (first, layers, where) in enumerate(plan):
        base = (group % 2) * 64
        record = jnp.concatenate(
            [turned[group // 2][base + 16 * j:base + 16 * j + ROWS] for j in range(4)], axis=1
        )
        slots = record.shape[1]
        alive = record[7:8]
        cell = record[6:7].astype(jnp.int32)
        value = jnp.where(alive > 0.0, record, 0.0)
        high = value.astype(jnp.bfloat16).astype(jnp.float32)
        rest = value - high
        middle = rest.astype(jnp.bfloat16).astype(jnp.float32)
        low = rest - middle
        half = layers * layer // 2
        row = (cell >> 7) - first * layer
        upper = (row >= half).astype(jnp.int32)
        hit = lax.broadcasted_iota(jnp.int32, (half, slots), 0) == row - half * upper
        blocks = [
            jnp.where(hit, terms[name:name + 1], 0.0)
            for terms, names in ((high, (0, 1, 2, 3, 4, 5, 7)), (middle, range(6)), (low, range(6)))
            for name in names
        ]
        if len(blocks) * half % 16:
            blocks.append(jnp.zeros((half, slots), jnp.float32))
        stacked = jnp.concatenate(blocks, axis=0).astype(jnp.bfloat16)
        left[group, :stacked.shape[0]] = stacked
        column = (cell & (LANES - 1)) + LANES * upper
        lane = lax.broadcasted_iota(jnp.int32, (2 * LANES, slots), 0) == column
        right[group] = lane.astype(jnp.float32).astype(jnp.bfloat16)
        sums = lax.dot_general(
            left[group, :stacked.shape[0]], right[group], (((1,), (1,)), ((), ())),
            preferred_element_type=jnp.float32,
        )

        def part(block, at, size):
            side, at = divmod(at, half)
            return sums[block * half + at:block * half + at + size, side * LANES:(side + 1) * LANES]

        for index in range(layers):
            for piece in range(0, layer, 8):
                at = index * layer + piece
                rows = slice(piece, piece + 8)
                count = part(6, at, 8)
                for name in range(6):
                    total = part(name, at, 8) + part(7 + name, at, 8) + part(13 + name, at, 8)
                    out[name, where + index, rows] = count * near[name, where + index, rows] - total


PITCH = 24


def clear(buffer, layers):
    for part in range(6):
        for layer in range(layers + 1):
            buffer[part, layer * PITCH:layer * PITCH + 8] = jnp.zeros((8, LANES), jnp.float32)


def damping_kernel(out, depth, tiles):
    tile = lax.axis_index("tile")
    for layer in range(out.shape[0]):
        place = tile * depth + layer - 2 * HALO
        scale = jnp.where((place >= 0) & (place < tiles * depth), DAMPING, 0.0)
        out[layer] = jnp.full(out.shape[1:], scale, jnp.float32)


def coefficients(absorbs, damping, pq):
    for layer, absorb in enumerate(absorbs):
        weight = damping[layer] / (36.0 + absorb * absorb)
        pq[0, layer] = 6.0 * weight
        pq[1, layer] = absorb * weight


def first_sweep(src, pq, dst, layers):
    def step(layer, carry):
        at = pl.ds(pl.multiple_of(layer * PITCH + 8, 8), 16)
        p, q = pq[0, layer], pq[1, layer]
        for part in range(3):
            re, im = src[part, layer], src[part + 3, layer]
            dst[part, at] = p * re + q * im
            dst[part + 3, at] = p * im - q * re
        return carry

    lax.fori_loop(0, layers, step, 0, unroll=16 if layers == 16 else 2)


def sweep(src, pq, old, new, lo, hi, emit=None):
    lane = lax.broadcasted_iota(jnp.int32, (16, LANES), 1)
    not_first, not_last = lane > 0, lane < LANES - 1

    def neighbours(part, base):
        middle = old[part, pl.ds(base, 16)]
        beside = old[part, pl.ds(base - PITCH, 16)] + old[part, pl.ds(base + PITCH, 16)]
        beside = beside + (old[part, pl.ds(base - 1, 16)] + old[part, pl.ds(base + 1, 16)])
        beside = beside + jnp.where(not_first, pltpu.roll(middle, 1, 1), 0.0)
        beside = beside + jnp.where(not_last, pltpu.roll(middle, LANES - 1, 1), 0.0)
        return middle, beside

    def step(layer, carry):
        base = layer * PITCH + 8
        p, q = pq[0, layer], pq[1, layer]
        results = []
        for part in range(3):
            mid_re, sum_re = neighbours(part, base)
            mid_im, sum_im = neighbours(part + 3, base)
            sum_re = sum_re + src[part, layer]
            sum_im = sum_im + src[part + 3, layer]
            new_re = (1.0 - DAMPING) * mid_re + (p * sum_re + q * sum_im)
            new_im = (1.0 - DAMPING) * mid_im + (p * sum_im - q * sum_re)
            if emit is None:
                at = pl.ds(pl.multiple_of(base, 8), 16)
                new[part, at] = new_re
                new[part + 3, at] = new_im
            results.append((new_re, new_im))
        if emit is not None:
            emit(layer, results)
        return carry

    lax.fori_loop(lo, hi, step, 0, unroll=hi - lo)


def relax(src, pq, one, two, emit):
    layers = src.shape[1]
    clear(one, layers)
    clear(two, layers)
    first_sweep(src, pq, one, layers)
    old, new = one, two
    for index in range(1, SWEEPS):
        final = index == SWEEPS - 1
        sweep(src, pq, old, new, index, layers - index, emit if final else None)
        old, new = new, old


def choose_kernel(own, across, out):
    out[0] = own[...]
    out[1] = across[...]


def forward_kernel(factor, damping, own, across, edge, other, near, near_pq, src, pq, one, two):
    depth = own.shape[1]
    even = lax.axis_index("tile") % 2 == 0
    mine, theirs = other.at[0], other.at[1]
    views = [(edge, i, across, depth - 2 + i) for i in range(2)]
    views += [(theirs, i, mine, i) for i in range(depth)]
    views += [(own, i, own, i) for i in range(depth)]
    views += [(mine, i, theirs, i) for i in range(depth)]
    views += [(across, i, edge, i) for i in range(2)]
    absorbs = []
    for layer, (first, at, second, there) in enumerate(views):
        if first is second:
            src[:, layer] = first[:6, at]
            absorbs.append(factor[0] * first[6, at])
        else:
            src[:, layer] = jnp.where(even, first[:6, at], second[:6, there])
            absorbs.append(factor[0] * jnp.where(even, first[6, at], second[6, there]))
    coefficients(absorbs, damping, pq)
    near_pq[...] = pq[:, HALO:-HALO]

    def emit(layer, results):
        for part, (re, im) in enumerate(results):
            near[part, layer - HALO] = re
            near[part + 3, layer - HALO] = im

    relax(src, pq, one, two, emit)


def finish_kernel(factor, received, near, pq, terms, field, src, one, two, left, right, written):
    depth = near.shape[1] - 2 * HALO
    copy = pltpu.make_async_copy(near.at[:, pl.ds(HALO, depth)], field.at[0], written)
    copy.start()
    adjoint_source(received, near, src, left, right)

    def emit(layer, results):
        total = 0.0
        for part, (re, im) in enumerate(results):
            total = total + (re * near[part + 3, layer] + im * near[part, layer])
        total = factor[0] * total
        rows = pl.ds(pl.multiple_of((layer - HALO) * 16, 16), 16)
        for index in range(terms.shape[0]):
            terms[index, rows] = total

    relax(src, pq, one, two, emit)
    copy.wait()


def working(layers):
    buffer = pltpu.VMEM((6, layers * PITCH + 8, LANES), jnp.float32)
    return [pltpu.VMEM((6, layers, 16, LANES), jnp.float32), buffer, buffer]


def shape(*dims):
    return jax.ShapeDtypeStruct(dims, jnp.float32)


LIMIT = pltpu.CompilerParams(vmem_limit_bytes=16 * 2**20)


def cost(flops, size):
    return pl.CostEstimate(flops=flops, bytes_accessed=size, transcendentals=0)


def pack(source, conductivity, observed, slot_cells, block_counts):
    depth, ny, nz = conductivity.shape
    slots, tiles = slot_cells.shape[0], block_counts.shape[0]
    return pl.pallas_call(
        pack_kernel,
        out_shape=(shape(7, depth, ny, nz), shape(7, 2, ny, nz), shape(tiles, 2, LANES)),
        in_specs=[HBM] * 5,
        out_specs=(VMEM, VMEM, HBM),
        scratch_shapes=[
            pltpu.VMEM((6, 1, slots), jnp.float32),
            pltpu.VMEM((1, slots), jnp.int32),
            pltpu.VMEM((1, tiles), jnp.int32),
            pltpu.VMEM((ROWS, slots), jnp.float32),
            pltpu.VMEM((slots + 2 * (slots // tiles), LANES), jnp.float32),
            pltpu.VMEM((tiles + 16, LANES), jnp.float32),
            pltpu.VMEM((tiles, 2, LANES), jnp.float32),
            pltpu.SemaphoreType.DMA((7,)),
            pltpu.SemaphoreType.DMA,
        ],
        compiler_params=LIMIT,
        cost_estimate=cost(10**6, 10**6),
        name="pack",
    )(
        *(
            pltpu.with_memory_space_constraint(x, pltpu.HBM)
            for x in (
                source,
                conductivity,
                observed.transpose(1, 0, 2),
                slot_cells.reshape(1, -1),
                block_counts.reshape(1, -1),
            )
        )
    )


def choose(own, across):
    return pl.pallas_call(
        choose_kernel,
        out_shape=shape(2, *own.shape),
        in_specs=[VMEM] * 2,
        out_specs=VMEM,
        compiler_params=LIMIT,
        cost_estimate=cost(10**10, 10**9),
        name="choose",
    )(own, across)


def layer_damping(depth, ny, nz, tiles):
    return pl.pallas_call(
        functools.partial(damping_kernel, depth=depth, tiles=tiles),
        out_shape=shape(depth + 4 * HALO, ny, nz),
        out_specs=VMEM,
        compiler_params=LIMIT,
        cost_estimate=cost(10**10, 10**9),
        name="damping",
    )()


def forward(factor, damping, own, across, edge, other):
    depth, ny, nz = own.shape[1:]
    wide, layers = depth + 4 * HALO, depth + 2 * HALO
    return pl.pallas_call(
        forward_kernel,
        out_shape=(shape(6, layers, ny, nz), shape(2, layers, ny, nz)),
        in_specs=[SMEM] + [VMEM] * 5,
        out_specs=(VMEM, VMEM),
        scratch_shapes=[working(wide)[0], pltpu.VMEM((2, wide, ny, nz), jnp.float32)] + working(wide)[1:],
        compiler_params=LIMIT,
        cost_estimate=cost(10**6, 10**6),
        name="forward",
    )(factor, damping, own, across, edge, other)


def finish(factor, received, near, near_pq, freqs):
    layers, ny, nz = near.shape[1:]
    depth = layers - 2 * HALO
    slots = received.shape[0] * received.shape[2] // (2 * ROWS)
    return pl.pallas_call(
        finish_kernel,
        out_shape=(shape(freqs, depth * ny, nz), shape(1, 6, depth, ny, nz)),
        in_specs=[SMEM] + [VMEM] * 3,
        out_specs=(VMEM, HBM),
        scratch_shapes=working(layers) + [
            pltpu.VMEM((3, 19 * depth * ny // 2, slots), jnp.bfloat16),
            pltpu.VMEM((3, 2 * LANES, slots), jnp.bfloat16),
            pltpu.SemaphoreType.DMA,
        ],
        compiler_params=LIMIT,
        cost_estimate=cost(10**10, 10**9),
        name="finish",
    )(factor, received, near, near_pq)


def body(source, conductivity, freq_factor, observed, slot_cells, block_counts):
    tiles, freqs = lax.axis_size("tile"), lax.axis_size("freq")
    depth, ny, nz = conductivity.shape
    own, near_edge, payload = pack(source, conductivity, observed, slot_cells, block_counts)
    chips = tiles // 2
    up = [(2 * k, 2 * k + 2) for k in range(chips - 1)]
    down = [(2 * k + 2, 2 * k) for k in range(chips - 1)]
    across = lax.ppermute(own, "tile", down + [(i + 1, j + 1) for i, j in up])
    edge = lax.ppermute(near_edge, "tile", up + [(i + 1, j + 1) for i, j in down])
    received = lax.all_to_all(payload, "tile", split_axis=0, concat_axis=0, tiled=True)
    chosen = choose(own, across)
    other = lax.ppermute(chosen, "tile", [(i, i ^ 1) for i in range(tiles)])
    damping = layer_damping(depth, ny, nz, tiles)
    near, near_pq = forward(freq_factor, damping, own, across, edge, other)
    terms, field = finish(freq_factor, received, near, near_pq, freqs)
    terms = lax.all_to_all(terms, "freq", split_axis=0, concat_axis=0, tiled=True)
    gradient = jnp.sum(terms, axis=0).reshape(depth, ny, nz)
    return (field, gradient)


def solution(mesh):
    in_specs = (
        P(None, "tile", None, None),
        P("tile", None, None),
        P("freq"),
        P("freq", None, "tile"),
        P("tile"),
        P("tile"),
    )
    out_specs = (P("freq", None, "tile", None, None), P("tile", None, None))
    return jax.shard_map(body, mesh=mesh, in_specs=in_specs, out_specs=out_specs, check_vma=False)
```

```python
import functools

import jax
import jax.numpy as jnp
from jax import lax
from jax.experimental import pallas as pl
from jax.experimental.pallas import tpu as pltpu
from jax.sharding import PartitionSpec as P

SWEEPS = 4
DAMPING = 0.8
HALO = SWEEPS - 1
ROWS = 8
LANES = 128

VMEM = pl.BlockSpec(memory_space=pltpu.VMEM)
SMEM = pl.BlockSpec(memory_space=pltpu.SMEM)
HBM = pl.BlockSpec(memory_space=pltpu.HBM)


def pack_kernel(
    source, cond, observed, cells, counts, own, near_edge, payload,
    observed_in, cells_in, counts_in, values, columns, counted, staged, arrived, left,
):
    core = lax.axis_index("tile") % 2
    edge = pl.ds(2 * (1 - core), 2)
    copies = [
        pltpu.make_async_copy(start, end, arrived.at[i])
        for i, (start, end) in enumerate(
            (
                (observed, observed_in),
                (cells, cells_in),
                (counts, counts_in),
                (cond, own.at[6]),
                (cond.at[edge], near_edge.at[6]),
                (source, own.at[pl.ds(0, 6)]),
                (source.at[:, edge], near_edge.at[pl.ds(0, 6)]),
            )
        )
    ]
    for copy in copies:
        copy.start()
    tiles = counts.shape[1]
    slots = cells.shape[1]
    cap = slots // tiles
    values[7:8] = jnp.zeros((1, slots), jnp.float32)
    columns[...] = jnp.zeros_like(columns)
    counted[...] = jnp.zeros_like(counted)
    for copy in copies[:3]:
        copy.wait()
    for part in range(6):
        values[part:part + 1] = observed_in[part]
    values[6:7] = cells_in[...].astype(jnp.float32)
    row = jnp.concatenate([counts_in[...].astype(jnp.float32), jnp.zeros((1, LANES - tiles), jnp.float32)], axis=1)
    counted[8:8 + tiles, 0:8] = jnp.broadcast_to(row, (8, LANES)).T[:tiles]
    for part in range(slots // LANES):
        turned = values[:, part * LANES:(part + 1) * LANES].T
        columns[cap + part * LANES:cap + (part + 1) * LANES, 0:ROWS] = turned
    planes = [jnp.zeros((tiles, LANES), jnp.float32), jnp.zeros((tiles, LANES), jnp.float32)]
    for group in range(3):
        for slot in range(cap):
            piece = columns[pl.ds(group * cap + slot, tiles, stride=cap), :]
            shift = (group % 2) * 64 + slot * ROWS
            planes[group // 2] += pltpu.roll(piece, shift, 1) if shift else piece
    lane = lax.broadcasted_iota(jnp.int32, (tiles, LANES), 1)
    within = ((lane & 63) >> 3).astype(jnp.float32)
    own_count, left_count, right_count = (counted[8 + i:8 + i + tiles, 0:1] for i in (0, -1, 1))
    for plane, limit in enumerate(
        (jnp.where(lane < 64, left_count, own_count), jnp.where(lane < 64, right_count, 0.0))
    ):
        live = ((lane & 7) == 7) & (within < limit)
        staged[:, plane, :] = jnp.where(live, 1.0, planes[plane])
    sent = pltpu.make_async_copy(staged, payload, left)
    sent.start()
    for copy in copies[3:]:
        copy.wait()
    sent.wait()


def adjoint_source(received, near, out, left, right):
    tiles = received.shape[0]
    turned = []
    for plane in range(2):
        here = received[:, plane, :]
        turned.append(jnp.concatenate([here, pltpu.roll(here, LANES - ROWS, 1)], axis=0).T)
    layer = out.shape[2]
    depth = out.shape[1] - 2 * HALO
    plan = ((depth - HALO, HALO, 0), (0, depth, HALO), (0, HALO, HALO + depth))
    for group, (first, layers, where) in enumerate(plan):
        base = (group % 2) * 64
        record = jnp.concatenate(
            [turned[group // 2][base + 16 * j:base + 16 * j + ROWS] for j in range(4)], axis=1
        )
        slots = record.shape[1]
        alive = record[7:8]
        cell = record[6:7].astype(jnp.int32)
        value = jnp.where(alive > 0.0, record, 0.0)
        high = value.astype(jnp.bfloat16).astype(jnp.float32)
        rest = value - high
        middle = rest.astype(jnp.bfloat16).astype(jnp.float32)
        low = rest - middle
        half = layers * layer // 2
        row = (cell >> 7) - first * layer
        upper = (row >= half).astype(jnp.int32)
        hit = lax.broadcasted_iota(jnp.int32, (half, slots), 0) == row - half * upper
        blocks = [
            jnp.where(hit, terms[name:name + 1], 0.0)
            for terms, names in ((high, (0, 1, 2, 3, 4, 5, 7)), (middle, range(6)), (low, range(6)))
            for name in names
        ]
        if len(blocks) * half % 16:
            blocks.append(jnp.zeros((half, slots), jnp.float32))
        stacked = jnp.concatenate(blocks, axis=0).astype(jnp.bfloat16)
        left[group, :stacked.shape[0]] = stacked
        column = (cell & (LANES - 1)) + LANES * upper
        lane = lax.broadcasted_iota(jnp.int32, (2 * LANES, slots), 0) == column
        right[group] = lane.astype(jnp.float32).astype(jnp.bfloat16)
        sums = lax.dot_general(
            left[group, :stacked.shape[0]], right[group], (((1,), (1,)), ((), ())),
            preferred_element_type=jnp.float32,
        )

        def part(block, at, size):
            side, at = divmod(at, half)
            return sums[block * half + at:block * half + at + size, side * LANES:(side + 1) * LANES]

        for index in range(layers):
            for piece in range(0, layer, 8):
                at = index * layer + piece
                rows = slice(piece, piece + 8)
                count = part(6, at, 8)
                for name in range(6):
                    total = part(name, at, 8) + part(7 + name, at, 8) + part(13 + name, at, 8)
                    out[name, where + index, rows] = count * near[name, where + index, rows] - total


PITCH = 24


def clear(buffer, layers):
    for part in range(6):
        for layer in range(layers + 1):
            buffer[part, layer * PITCH:layer * PITCH + 8] = jnp.zeros((8, LANES), jnp.float32)


def damping_kernel(out, depth, tiles):
    tile = lax.axis_index("tile")
    for layer in range(out.shape[0]):
        place = tile * depth + layer - 2 * HALO
        scale = jnp.where((place >= 0) & (place < tiles * depth), DAMPING, 0.0)
        out[layer] = jnp.full(out.shape[1:], scale, jnp.float32)


def coefficients(absorbs, damping, pq):
    for layer, absorb in enumerate(absorbs):
        weight = damping[layer] / (36.0 + absorb * absorb)
        pq[0, layer] = 6.0 * weight
        pq[1, layer] = absorb * weight


def first_sweep(src, pq, dst, layers):
    def step(layer, carry):
        at = pl.ds(pl.multiple_of(layer * PITCH + 8, 8), 16)
        p, q = pq[0, layer], pq[1, layer]
        for part in range(3):
            re, im = src[part, layer], src[part + 3, layer]
            dst[part, at] = p * re + q * im
            dst[part + 3, at] = p * im - q * re
        return carry

    lax.fori_loop(0, layers, step, 0, unroll=16 if layers == 16 else 2)


def sweep(src, pq, old, new, lo, hi, emit=None):
    lane = lax.broadcasted_iota(jnp.int32, (16, LANES), 1)
    not_first, not_last = lane > 0, lane < LANES - 1

    def neighbours(part, base):
        middle = old[part, pl.ds(base, 16)]
        beside = old[part, pl.ds(base - PITCH, 16)] + old[part, pl.ds(base + PITCH, 16)]
        beside = beside + (old[part, pl.ds(base - 1, 16)] + old[part, pl.ds(base + 1, 16)])
        beside = beside + jnp.where(not_first, pltpu.roll(middle, 1, 1), 0.0)
        beside = beside + jnp.where(not_last, pltpu.roll(middle, LANES - 1, 1), 0.0)
        return middle, beside

    def step(layer, carry):
        base = layer * PITCH + 8
        p, q = pq[0, layer], pq[1, layer]
        results = []
        for part in range(3):
            mid_re, sum_re = neighbours(part, base)
            mid_im, sum_im = neighbours(part + 3, base)
            sum_re = sum_re + src[part, layer]
            sum_im = sum_im + src[part + 3, layer]
            new_re = (1.0 - DAMPING) * mid_re + (p * sum_re + q * sum_im)
            new_im = (1.0 - DAMPING) * mid_im + (p * sum_im - q * sum_re)
            if emit is None:
                at = pl.ds(pl.multiple_of(base, 8), 16)
                new[part, at] = new_re
                new[part + 3, at] = new_im
            results.append((new_re, new_im))
        if emit is not None:
            emit(layer, results)
        return carry

    lax.fori_loop(lo, hi, step, 0, unroll=hi - lo)


def relax(src, pq, one, two, emit):
    layers = src.shape[1]
    clear(one, layers)
    clear(two, layers)
    first_sweep(src, pq, one, layers)
    old, new = one, two
    for index in range(1, SWEEPS):
        final = index == SWEEPS - 1
        sweep(src, pq, old, new, index, layers - index, emit if final else None)
        old, new = new, old


def choose_kernel(own, across, out):
    out[0] = own[...]
    out[1] = across[...]


def forward_kernel(factor, damping, own, across, edge, other, near, near_pq, src, pq, one, two):
    depth = own.shape[1]
    even = lax.axis_index("tile") % 2 == 0
    mine, theirs = other.at[0], other.at[1]
    views = [(edge, i, across, depth - 2 + i) for i in range(2)]
    views += [(theirs, i, mine, i) for i in range(depth)]
    views += [(own, i, own, i) for i in range(depth)]
    views += [(mine, i, theirs, i) for i in range(depth)]
    views += [(across, i, edge, i) for i in range(2)]
    absorbs = []
    for layer, (first, at, second, there) in enumerate(views):
        if first is second:
            src[:, layer] = first[:6, at]
            absorbs.append(factor[0] * first[6, at])
        else:
            src[:, layer] = jnp.where(even, first[:6, at], second[:6, there])
            absorbs.append(factor[0] * jnp.where(even, first[6, at], second[6, there]))
    coefficients(absorbs, damping, pq)
    near_pq[...] = pq[:, HALO:-HALO]

    def emit(layer, results):
        for part, (re, im) in enumerate(results):
            near[part, layer - HALO] = re
            near[part + 3, layer - HALO] = im

    relax(src, pq, one, two, emit)


def finish_kernel(factor, received, near, pq, terms, field, src, one, two, left, right, written):
    depth = near.shape[1] - 2 * HALO
    copy = pltpu.make_async_copy(near.at[:, pl.ds(HALO, depth)], field.at[0], written)
    copy.start()
    adjoint_source(received, near, src, left, right)

    def emit(layer, results):
        total = 0.0
        for part, (re, im) in enumerate(results):
            total = total + (re * near[part + 3, layer] + im * near[part, layer])
        total = factor[0] * total
        rows = pl.ds(pl.multiple_of((layer - HALO) * 16, 16), 16)
        for index in range(terms.shape[0]):
            terms[index, rows] = total

    relax(src, pq, one, two, emit)
    copy.wait()


def working(layers):
    buffer = pltpu.VMEM((6, layers * PITCH + 8, LANES), jnp.float32)
    return [pltpu.VMEM((6, layers, 16, LANES), jnp.float32), buffer, buffer]


def shape(*dims):
    return jax.ShapeDtypeStruct(dims, jnp.float32)


LIMIT = pltpu.CompilerParams(vmem_limit_bytes=16 * 2**20)


def cost(flops, size):
    return pl.CostEstimate(flops=flops, bytes_accessed=size, transcendentals=0)


def pack(source, conductivity, observed, slot_cells, block_counts):
    depth, ny, nz = conductivity.shape
    slots, tiles = slot_cells.shape[0], block_counts.shape[0]
    return pl.pallas_call(
        pack_kernel,
        out_shape=(shape(7, depth, ny, nz), shape(7, 2, ny, nz), shape(tiles, 2, LANES)),
        in_specs=[HBM] * 5,
        out_specs=(VMEM, VMEM, HBM),
        scratch_shapes=[
            pltpu.VMEM((6, 1, slots), jnp.float32),
            pltpu.VMEM((1, slots), jnp.int32),
            pltpu.VMEM((1, tiles), jnp.int32),
            pltpu.VMEM((ROWS, slots), jnp.float32),
            pltpu.VMEM((slots + 2 * (slots // tiles), LANES), jnp.float32),
            pltpu.VMEM((tiles + 16, LANES), jnp.float32),
            pltpu.VMEM((tiles, 2, LANES), jnp.float32),
            pltpu.SemaphoreType.DMA((7,)),
            pltpu.SemaphoreType.DMA,
        ],
        compiler_params=LIMIT,
        cost_estimate=cost(10**6, 10**6),
        name="pack",
    )(
        *(
            pltpu.with_memory_space_constraint(x, pltpu.HBM)
            for x in (
                source,
                conductivity,
                observed.transpose(1, 0, 2),
                slot_cells.reshape(1, -1),
                block_counts.reshape(1, -1),
            )
        )
    )


def choose(own, across):
    return pl.pallas_call(
        choose_kernel,
        out_shape=shape(2, *own.shape),
        in_specs=[VMEM] * 2,
        out_specs=VMEM,
        compiler_params=LIMIT,
        cost_estimate=cost(10**10, 10**9),
        name="choose",
    )(own, across)


def layer_damping(depth, ny, nz, tiles):
    return pl.pallas_call(
        functools.partial(damping_kernel, depth=depth, tiles=tiles),
        out_shape=shape(depth + 4 * HALO, ny, nz),
        out_specs=VMEM,
        compiler_params=LIMIT,
        cost_estimate=cost(10**10, 10**9),
        name="damping",
    )()


def forward(factor, damping, own, across, edge, other):
    depth, ny, nz = own.shape[1:]
    wide, layers = depth + 4 * HALO, depth + 2 * HALO
    return pl.pallas_call(
        forward_kernel,
        out_shape=(shape(6, layers, ny, nz), shape(2, layers, ny, nz)),
        in_specs=[SMEM] + [VMEM] * 5,
        out_specs=(VMEM, VMEM),
        scratch_shapes=[working(wide)[0], pltpu.VMEM((2, wide, ny, nz), jnp.float32)] + working(wide)[1:],
        compiler_params=LIMIT,
        cost_estimate=cost(10**6, 10**6),
        name="forward",
    )(factor, damping, own, across, edge, other)


def finish(factor, received, near, near_pq, freqs):
    layers, ny, nz = near.shape[1:]
    depth = layers - 2 * HALO
    slots = received.shape[0] * received.shape[2] // (2 * ROWS)
    return pl.pallas_call(
        finish_kernel,
        out_shape=(shape(freqs, depth * ny, nz), shape(1, 6, depth, ny, nz)),
        in_specs=[SMEM] + [VMEM] * 3,
        out_specs=(VMEM, HBM),
        scratch_shapes=working(layers) + [
            pltpu.VMEM((3, 19 * depth * ny // 2, slots), jnp.bfloat16),
            pltpu.VMEM((3, 2 * LANES, slots), jnp.bfloat16),
            pltpu.SemaphoreType.DMA,
        ],
        compiler_params=LIMIT,
        cost_estimate=cost(10**10, 10**9),
        name="finish",
    )(factor, received, near, near_pq)


def body(source, conductivity, freq_factor, observed, slot_cells, block_counts):
    tiles, freqs = lax.axis_size("tile"), lax.axis_size("freq")
    depth, ny, nz = conductivity.shape
    own, near_edge, payload = pack(source, conductivity, observed, slot_cells, block_counts)
    chips = tiles // 2
    up = [(2 * k, 2 * k + 2) for k in range(chips - 1)]
    down = [(2 * k + 2, 2 * k) for k in range(chips - 1)]
    across = lax.ppermute(own, "tile", down + [(i + 1, j + 1) for i, j in up])
    edge = lax.ppermute(near_edge, "tile", up + [(i + 1, j + 1) for i, j in down])
    received = lax.all_to_all(payload, "tile", split_axis=0, concat_axis=0, tiled=True)
    chosen = choose(own, across)
    other = lax.ppermute(chosen, "tile", [(i, i ^ 1) for i in range(tiles)])
    damping = layer_damping(depth, ny, nz, tiles)
    near, near_pq = forward(freq_factor, damping, own, across, edge, other)
    terms, field = finish(freq_factor, received, near, near_pq, freqs)
    terms = lax.all_to_all(terms, "freq", split_axis=0, concat_axis=0, tiled=True)
    gradient = jnp.sum(terms, axis=0).reshape(depth, ny, nz)
    return (field, gradient)


def solution(mesh):
    in_specs = (
        P(None, "tile", None, None),
        P("tile", None, None),
        P("freq"),
        P("freq", None, "tile"),
        P("tile"),
        P("tile"),
    )
    out_specs = (P("freq", None, "tile", None, None), P("tile", None, None))
    return jax.shard_map(body, mesh=mesh, in_specs=in_specs, out_specs=out_specs, check_vma=False)
```
